32 devices in a mesh: batch: 8 (over z, y), band: 4 (over x, core).
Axes of the slice: x: 2, y: 2, z: 4, core: 2. Of those that a mesh axis runs over, the one named last changes fastest.
Arguments:
- tokens: bfloat16 [24, 1024, 768], P('batch', 'band'), may hold values from -6 to 6
- w_qkv: bfloat16 [768, 2304], replicated, may hold values from -0.21875 to 0.21875
- w_proj: bfloat16 [768, 768], replicated, may hold values from -5 to 5
- w_fc1: bfloat16 [768, 3072], replicated, may hold values from -0.21875 to 0.21875
- w_fc2: bfloat16 [3072, 768], replicated, may hold values from -0.109375 to 0.109375
- gain_one: float32 [768], replicated, may hold values from 0.5 to 1.5
- gain_two: float32 [768], replicated, may hold values from 0.5 to 1.5
- cotangent: bfloat16 [24, 1024, 768], P('batch', 'band'), may hold values from -6 to 6
- band_counts: int32 [24, 4], P('batch'), may hold values from 64 to 256
- slot_live: int32 [24], P('batch'), may hold values 0 or 1
Outputs:
- output: bfloat16 [24, 1024, 768], P('batch', 'band')
- grad_input: bfloat16 [24, 1024, 768], P('batch', 'band')
- grad_qkv: float32 [768, 2304], replicated
- grad_proj: float32 [768, 768], replicated
- grad_fc1: float32 [768, 3072], replicated
- grad_fc2: float32 [3072, 768], replicated
- grad_norm1: float32 [768], replicated
- grad_norm2: float32 [768], replicated
The draws below stay inside these ranges and needn't reach their ends.
All inputs are finite; a program needn't handle non-finite values. No bound on the sum of `slot_live` on one device may be relied on, other than what follows from the above.
Results may differ from the reference program's by a relative error of at most 0.014.
Values may be sent and summed in bfloat16 or wider, within the bound.
No kernel may reach another device: no remote copies, remote signals or barrier semaphores. Data moves between devices by JAX's collectives and lax.ppermute only.
A program may use at most 192 MiB of HBM per device.

```python
import jax
import jax.numpy as jnp
from jax import lax

D = 768
HEADS = 12
HEAD_DIM = 64
FF = 3072
ROWS = 256
SAMPLES = 24
N_BAND = 4


def touch_ends(values, key, smallest, high):
    spot = [jax.random.randint(jax.random.fold_in(key, axis), (), 0, length) for axis, length in enumerate(values.shape)]
    widest = values.shape.index(max(values.shape))
    neighbour = spot[:widest] + [(spot[widest] + 1) % values.shape[widest]] + spot[widest + 1:]
    return values.at[tuple(spot)].set(smallest).at[tuple(neighbour)].set(high)


def block_scale(own_key, dims, cuts, low, high):
    def one(dim, blocks):
        draws = jax.random.uniform(jax.random.fold_in(jax.random.fold_in(own_key, 6), dim), (blocks,), jnp.float32, low / len(cuts), high / len(cuts))
        return jnp.repeat(jnp.exp(draws), dims[dim] // blocks).reshape((-1,) + (1,) * (len(dims) - dim - 1))

    loudness = one(*cuts[0])
    for cut in cuts[1:]:
        loudness = loudness * one(*cut)
    return loudness


def bell_draw(rng, shape, scale, bound, pieces=(), held_as=jnp.bfloat16):
    drawn = scale * jax.random.normal(rng, shape, jnp.float32)
    if pieces:
        drawn = drawn * block_scale(rng, shape, pieces, -0.22, 0.18)
    return jnp.clip(drawn, -bound, bound).astype(held_as)


def setup_inputs(seed: int = 0) -> dict:
    seeds = jax.random.split(jax.random.key(seed), 11)
    return {
        "tokens": bell_draw(seeds[0], (SAMPLES, N_BAND * ROWS, D), 1.0, 6.0, ((0, 8), (1, 4))),
        "w_qkv": bell_draw(seeds[1], (D, 3 * D), D ** -0.5, 0.21875),
        "w_proj": bell_draw(seeds[2], (D, D), 1.5 ** -0.5, 5.0),
        "w_fc1": bell_draw(seeds[3], (D, FF), D ** -0.5, 0.21875),
        "w_fc2": bell_draw(seeds[4], (FF, D), FF ** -0.5, 0.109375),
        "gain_one": jnp.clip(1.0 + 0.1 * jax.random.normal(seeds[5], (D,), jnp.float32), 0.5, 1.5),
        "gain_two": jnp.clip(1.0 + 0.1 * jax.random.normal(seeds[6], (D,), jnp.float32), 0.5, 1.5),
        "cotangent": bell_draw(seeds[7], (SAMPLES, N_BAND * ROWS, D), 1.0, 6.0, ((0, 8), (1, 4))),
        "band_counts": touch_ends(jax.random.randint(seeds[8], (SAMPLES, N_BAND), ROWS // 4, ROWS + 1), jax.random.fold_in(seeds[8], 1), ROWS // 4, ROWS).astype(jnp.int32),
        "slot_live": touch_ends((jax.random.randint(seeds[9], (SAMPLES,), 0, 8) < 7).astype(jnp.int32), jax.random.fold_in(seeds[9], 1), 0, 1),
    }


EPSILON = 1e-06

@jax.custom_vjp
def low(v):
    return lax.optimization_barrier(v.astype(jnp.bfloat16)).astype(jnp.float32)

@jax.custom_vjp
def low_back(v):
    return v

def low_keep(v):
    return (low(v), None)

def low_pass(kept, grad):
    return (grad,)

def back_keep(v):
    return (v, None)

def back_low(kept, grad):
    return (low(grad),)
low.defvjp(low_keep, low_pass)
low_back.defvjp(back_keep, back_low)

def normalize(values, gain_vector):
    centered = values - lax.optimization_barrier(jnp.mean(values, axis=-1, keepdims=True))
    spread = lax.optimization_barrier(jnp.mean(centered * centered, axis=-1, keepdims=True))
    return centered * lax.rsqrt(spread + EPSILON) * gain_vector

def matmul(left, right):
    return jnp.dot(left, right, precision=lax.Precision.HIGHEST)

def layer_one(sample, valid_rows, weights):
    w_qkv, w_proj, w_fc1, w_fc2, gain_one, gain_two = weights
    seq_length = sample.shape[0]
    first_in = low(normalize(sample, gain_one))
    projected = matmul(first_in, w_qkv)
    query_rows = low(low_back(projected[:, :D])).reshape(seq_length, HEADS, HEAD_DIM)
    key_rows = low(low_back(projected[:, D:2 * D])).reshape(seq_length, HEADS, HEAD_DIM)
    value_rows = low(low_back(projected[:, 2 * D:])).reshape(seq_length, HEADS, HEAD_DIM)
    scores = jnp.einsum('qhd,khd->hqk', query_rows, key_rows, precision=lax.Precision.HIGHEST) * HEAD_DIM ** (-0.5)
    scores = low_back(jnp.where(valid_rows[None, None, :] > 0, scores, -10000.0))
    soft_probs = jax.nn.softmax(scores, axis=-1)
    attended = jnp.einsum('hqk,khd->qhd', low(soft_probs), value_rows, precision=lax.Precision.HIGHEST)
    attended = low(low_back(attended.reshape(seq_length, D)))
    hidden = sample + low_back(matmul(attended, w_proj))
    second_in = low(normalize(hidden, gain_two))
    pre_act = low_back(matmul(second_in, w_fc1))
    act_low = low(jax.nn.gelu(pre_act, approximate=False))
    return (hidden + matmul(act_low, w_fc2)) * valid_rows[:, None]

def reference(tokens, w_qkv, w_proj, w_fc1, w_fc2, gain_one, gain_two, cotangent, band_counts, slot_live):
    positions = jnp.arange(N_BAND * ROWS, dtype=jnp.int32)
    limits = jnp.repeat(band_counts, ROWS, axis=1)
    valid_rows = (((positions % ROWS)[None, :] < limits) & (slot_live[:, None] > 0)).astype(jnp.float32)
    weights = (w_qkv.astype(jnp.float32), w_proj.astype(jnp.float32), w_fc1.astype(jnp.float32), w_fc2.astype(jnp.float32), gain_one.astype(jnp.float32), gain_two.astype(jnp.float32))

    def forward(inputs, params):

        def one_sample(pair):
            return layer_one(pair[0], pair[1], params)
        return lax.map(jax.checkpoint(one_sample), (inputs, valid_rows))
    result, pullback = jax.vjp(forward, tokens.astype(jnp.float32), weights)
    grad_inputs, grad_weights = pullback(cotangent.astype(jnp.float32))
    return (result.astype(jnp.bfloat16), grad_inputs.astype(jnp.bfloat16), grad_weights[0], grad_weights[1], grad_weights[2], grad_weights[3], grad_weights[4], grad_weights[5])
```

```python
import functools
import jax
import jax.numpy as jnp
from jax import lax
from jax.experimental import pallas as pl
from jax.experimental.pallas import tpu as pltpu
from jax.sharding import PartitionSpec as P

BF = jnp.bfloat16
F32 = jnp.float32
EPSILON = 1e-06
HEAD_DIM = 64
GROUP = 256
NN = (((1,), (0,)), ((), ()))
NT = (((1,), (1,)), ((), ()))
TN = (((0,), (0,)), ((), ()))


def dot(left, right, dims=NN):
    return lax.dot_general(left, right, dims, preferred_element_type=F32)


def params(mib=60):
    return pltpu.CompilerParams(vmem_limit_bytes=mib * 1024 * 1024)


def cost(flops, moved, exps=0):
    return pl.CostEstimate(flops=1, bytes_accessed=1, transcendentals=0)


HBM = pl.BlockSpec(memory_space=pltpu.HBM)


def normalized(values):
    centered = values - jnp.mean(values, axis=-1, keepdims=True)
    spread = jnp.mean(centered * centered, axis=-1, keepdims=True)
    scale = lax.rsqrt(spread + EPSILON)
    return centered * scale, scale


def project_kernel(tokens, weight, gain, first_in, query, both):
    normed, _ = normalized(tokens[0].astype(F32))
    first = (normed * gain[...]).astype(BF)
    first_in[0] = first
    width = first.shape[1]
    query[0] = (dot(first, weight[:, :width]) * HEAD_DIM ** -0.5).astype(BF)
    both[0, 0] = dot(first, weight[:, width:2 * width]).astype(BF)
    both[0, 1] = dot(first, weight[:, 2 * width:]).astype(BF)


def project(tokens, w_qkv, gain):
    slots, rows, width = tokens.shape
    row_spec = pl.BlockSpec((1, rows, width), lambda s: (s, 0, 0))
    return pl.pallas_call(
        project_kernel,
        out_shape=[
            jax.ShapeDtypeStruct(tokens.shape, BF),
            jax.ShapeDtypeStruct(tokens.shape, BF),
            jax.ShapeDtypeStruct((slots, 2, rows, width), BF),
        ],
        grid=(slots,),
        in_specs=[
            row_spec,
            pl.BlockSpec((width, 3 * width), lambda s: (0, 0)),
            pl.BlockSpec((1, width), lambda s: (0, 0)),
        ],
        out_specs=[row_spec, row_spec, pl.BlockSpec((1, 2, rows, width), lambda s: (s, 0, 0, 0))],
        compiler_params=params(),
        cost_estimate=cost(2 * slots * rows * width * width * 3, 8e6),
        name="project",
    )(tokens, w_qkv, gain)


def project_other_kernel(tokens, own, weight, gain, *refs):
    first_in, both = refs[-2:]
    normed, _ = normalized(tokens[0].astype(F32))
    first = (normed * gain[...]).astype(BF)
    first_in[0] = first
    width = first.shape[1]
    both[0] = own[0]
    both[1, 0] = dot(first, weight[:, :width]).astype(BF)
    both[1, 1] = dot(first, weight[:, width:]).astype(BF)


def project_other(slot, tokens, kv_own, w_qkv, gain, before):
    slots, _, rows, width = kv_own.shape
    return pl.pallas_call(
        project_other_kernel,
        out_shape=[
            jax.ShapeDtypeStruct((slots, rows, width), BF),
            jax.ShapeDtypeStruct((2, 2, rows, width), BF),
        ],
        grid=(1,),
        in_specs=[
            pl.BlockSpec((1, rows, width), lambda i: (0, 0, 0)),
            pl.BlockSpec((1, 2, rows, width), lambda i: (slot, 0, 0, 0)),
            pl.BlockSpec((pl.Element(width), pl.Element(2 * width)), lambda i: (0, width)),
            pl.BlockSpec((1, width), lambda i: (0, 0)),
        ] + [HBM] * len(before),
        out_specs=[
            pl.BlockSpec((1, rows, width), lambda i: (slot, 0, 0)),
            pl.BlockSpec((2, 2, rows, width), lambda i: (0, 0, 0, 0)),
        ],
        input_output_aliases={4 + i: i for i in range(len(before))},
        compiler_params=params(),
        cost_estimate=cost(2 * rows * width * width * 2, 5e6),
        name="project_other",
    )(tokens, kv_own, w_qkv, gain, *before)


def key_masks(counts, live, meta, slot, rows, flips, axis):
    shape = (rows, 1) if axis == 0 else (1, rows)
    place = lax.broadcasted_iota(jnp.int32, shape, axis)
    alive = live[slot] > 0
    return [place < jnp.where(alive, counts[slot, meta[0] ^ flip], 0) for flip in flips]


FLIPS = (0, 2, 1, 3)


def attend_kernel(slot, counts, live, meta, query, pair, pair_p, tokens, w_proj, gain, *refs):
    attended, lse, hidden, second, held, own_tokens, weight, sems = refs[-8:]
    group = pl.program_id(0)
    rows = query.shape[1]
    copies = (
        pltpu.make_async_copy(tokens.at[slot], own_tokens, sems.at[0]),
        pltpu.make_async_copy(w_proj, weight, sems.at[1]),
    )

    @pl.when(group == 0)
    def _():
        for copy in copies:
            copy.start()

    masks = key_masks(counts, live, meta, slot, rows, FLIPS, 1)
    q = query[0]
    lane = lax.broadcasted_iota(jnp.int32, (1, GROUP), 1)
    result = jnp.zeros((rows, GROUP), F32)
    sums = jnp.zeros((rows, 128), F32)
    lane128 = lax.broadcasted_iota(jnp.int32, (1, 128), 1)
    blocks = (pair.at[0], pair.at[1], pair_p.at[0], pair_p.at[1])
    for h in range(GROUP // HEAD_DIM):
        here = (lane // HEAD_DIM) == h
        qm = jnp.where(here, q, jnp.zeros_like(q))
        scores = [
            jnp.where(mask, dot(qm, block[0], NT), -10000.0) for mask, block in zip(masks, blocks)
        ]
        top = scores[0]
        for s in scores[1:]:
            top = jnp.maximum(top, s)
        top = jnp.max(top, axis=-1, keepdims=True)
        out = jnp.zeros((rows, GROUP), F32)
        exps = [jnp.exp(s - top) for s in scores]
        total = exps[0]
        for e in exps[1:]:
            total = total + e
        total = jnp.sum(total, axis=-1, keepdims=True)
        for e, block in zip(exps, blocks):
            out = out + dot(e.astype(BF), block[1])
        result = jnp.where(here, out * (1.0 / total), result)
        sums = jnp.where(lane128 == h, top + jnp.log(total), sums)
    low = result.astype(BF)
    attended[0] = low
    held[group] = low
    lse[0, 0] = sums.T[:8]

    @pl.when(group == pl.num_programs(0) - 1)
    def _():
        for copy in copies:
            copy.wait()
        value = own_tokens[...].astype(F32)
        for g in range(held.shape[0]):
            value = value + dot(held[g], weight[g * GROUP:(g + 1) * GROUP, :])
        hidden[0] = value
        normed, _ = normalized(value)
        second[...] = (normed * gain[...]).astype(BF)


def attend(slot, counts, live, meta, query, pair, pair_p, tokens, w_proj, gain, before):
    slots, rows, width = query.shape
    groups = width // GROUP
    at = slot
    kv_spec = pl.BlockSpec((2, 2, rows, GROUP), lambda g, *_: (0, 0, 0, g))
    piece = pl.BlockSpec((1, rows, GROUP), lambda g, *_: (at, 0, g))
    row_spec = pl.BlockSpec((1, rows, width), lambda g, *_: (at, 0, 0))
    operands = (counts, live, meta, query, pair, pair_p, tokens, w_proj, gain)
    return pl.pallas_call(
        functools.partial(attend_kernel, slot),
        out_shape=[
            jax.ShapeDtypeStruct(query.shape, BF),
            jax.ShapeDtypeStruct((slots, groups, 8, rows), F32),
            jax.ShapeDtypeStruct(query.shape, F32),
            jax.ShapeDtypeStruct((rows, width), BF),
        ],
        grid_spec=pltpu.PrefetchScalarGridSpec(
            num_scalar_prefetch=3,
            grid=(groups,),
            in_specs=[piece, kv_spec, kv_spec, HBM, HBM, pl.BlockSpec((1, width), lambda g, *_: (0, 0))]
            + [HBM] * len(before),
            out_specs=[
                piece,
                pl.BlockSpec((1, 1, 8, rows), lambda g, *_: (at, g, 0, 0)),
                row_spec,
                pl.BlockSpec((rows, width), lambda g, *_: (0, 0)),
            ],
            scratch_shapes=[
                pltpu.VMEM((groups, rows, GROUP), BF),
                pltpu.VMEM((rows, width), BF),
                pltpu.VMEM((width, width), BF),
                pltpu.SemaphoreType.DMA((2,)),
            ],
        ),
        input_output_aliases={len(operands) + i: i for i in range(len(before))},
        compiler_params=params(),
        cost_estimate=cost(2 * 2 * rows * 4 * rows * 4 * width, 1e7, 12 * rows * 4 * rows),
        name="attend",
    )(*operands, *before)


def attend_back_kernel(
    slot, counts, live, meta, query, pair, pair_p, grad, lse, delta, *refs
):
    grad_query, grad_keep, grad_send, probs, slopes, qms, gms, keys, values, keys_t = refs[-10:]
    rows = query.shape[1]
    heads = GROUP // HEAD_DIM
    masks = key_masks(counts, live, meta, slot, rows, FLIPS, 0)
    q = query[0]
    ga = grad[0]
    lane = lax.broadcasted_iota(jnp.int32, (1, GROUP), 1)
    zero = jnp.zeros_like(q)
    for h in range(heads):
        here = (lane // HEAD_DIM) == h
        qms[h * rows:(h + 1) * rows, :] = jnp.where(here, q, zero)
        gms[h * rows:(h + 1) * rows, :] = jnp.where(here, ga, zero)
    for i, mask in enumerate(masks):
        block = (pair, pair_p)[i // 2]
        keys[i * rows:(i + 1) * rows, :] = jnp.where(mask, block[i % 2, 0], zero)
        values[i * rows:(i + 1) * rows, :] = block[i % 2, 1]
    keys_t[...] = keys[...].T
    gq = []
    for h in range(heads):
        mine = slice(h * rows, (h + 1) * rows)
        for i, mask in enumerate(masks):
            at = slice(i * rows, (i + 1) * rows)
            scores = jnp.where(mask, dot(keys[at, :], qms[mine, :], NT), -10000.0)
            gp = dot(values[at, :], gms[mine, :], NT)
            p = jnp.exp(scores - lse[0, 0, h:h + 1, :])
            probs[at, mine] = p.astype(BF)
            slopes[at, mine] = (p * (gp - delta[0, 0, h:h + 1, :])).astype(BF)
        gq.append(dot(keys_t[h * HEAD_DIM:(h + 1) * HEAD_DIM, :], slopes[:, mine]))
    gk = dot(slopes[...], qms[...])
    gv = dot(probs[...], gms[...])
    outs = ((grad_keep, 0), (grad_keep, 1), (grad_send, 0), (grad_send, 1))
    for i, ((out, place), mask) in enumerate(zip(outs, masks)):
        at = slice(i * rows, (i + 1) * rows)
        out[0, place, 0] = jnp.where(mask, gk[at], 0.0).astype(BF)
        out[0, place, 1] = gv[at].astype(BF)
    grad_query[0] = (jnp.concatenate(gq, axis=0).T * HEAD_DIM ** -0.5).astype(BF)


def attend_back(slot, counts, live, meta, query, pair, pair_p, grad, lse, delta, before):
    slots, rows, width = query.shape
    groups = width // GROUP
    heads = GROUP // HEAD_DIM
    at = slot
    kv_spec = pl.BlockSpec((2, 2, rows, GROUP), lambda g, *_: (0, 0, 0, g))
    row_spec = pl.BlockSpec((1, rows, GROUP), lambda g, *_: (at, 0, g))
    stat_spec = pl.BlockSpec((1, 1, 8, rows), lambda g, *_: (at, g, 0, 0))
    out_spec = pl.BlockSpec((1, 2, 2, rows, GROUP), lambda g, *_: (0, 0, 0, 0, g))
    operands = (counts, live, meta, query, pair, pair_p, grad, lse, delta)
    return pl.pallas_call(
        functools.partial(attend_back_kernel, slot),
        out_shape=[
            jax.ShapeDtypeStruct(query.shape, BF),
            jax.ShapeDtypeStruct((1, 2, 2, rows, width), BF),
            jax.ShapeDtypeStruct((1, 2, 2, rows, width), BF),
        ],
        grid_spec=pltpu.PrefetchScalarGridSpec(
            num_scalar_prefetch=3,
            grid=(groups,),
            in_specs=[row_spec, kv_spec, kv_spec, row_spec, stat_spec, stat_spec]
            + [pl.BlockSpec(memory_space=pl.ANY)] * len(before),
            out_specs=[row_spec, out_spec, out_spec],
            scratch_shapes=[
                pltpu.VMEM((4 * rows, heads * rows), BF),
                pltpu.VMEM((4 * rows, heads * rows), BF),
                pltpu.VMEM((heads * rows, GROUP), BF),
                pltpu.VMEM((heads * rows, GROUP), BF),
                pltpu.VMEM((4 * rows, GROUP), BF),
                pltpu.VMEM((4 * rows, GROUP), BF),
                pltpu.VMEM((GROUP, 4 * rows), BF),
            ],
        ),
        input_output_aliases={len(operands) + i: i for i in range(len(before))},
        compiler_params=params(),
        cost_estimate=cost(5 * 2 * rows * 4 * rows * 4 * width, 2e7, 12 * rows * 4 * rows),
        name="attend_back",
    )(*operands, *before)


CHUNKS = 16


def row_mask(counts, live, meta, slot, rows):
    return key_masks(counts, live, meta, slot, rows, (0,), 0)[0]


def gelu_parts(v):
    size = jnp.abs(v)
    decay = jnp.exp2(v * v * (-0.5 * 1.4426950408889634))
    scale = 1.0 + (0.3275911 * 0.7071067811865476) * size
    t = pl.reciprocal(scale, approx=True)
    t = t * (2.0 - scale * t)
    poly = t * (0.127414796 + t * (-0.142248368 + t * (0.7107068705 + t * (-0.7265760135 + t * 0.5307027145))))
    tail = poly * decay
    phi = jnp.where(v >= 0, 1.0 - tail, tail)
    return phi, decay * 0.3989422804014327


def mlp_kernel(slots, half, counts, live, meta, *refs):
    seconds, rest = refs[:2 * slots], refs[2 * slots:]
    cot, cot_p, w_in, w_out, act_out, pre_out, *grads_out = rest[:8]
    sec, go, win, wout, act, pre, grads, sems, out_sems = rest[8:]
    rows = seconds[0].shape[0]
    count = slots * rows
    width = sec.shape[1]
    me = meta[2]
    part = pl.multiple_of((2 * meta[1] + half) * width, width)

    def copies_for(side):
        whole = pl.ds(side * count, count)
        out = [
            pltpu.make_async_copy(
                seconds[side * slots + s], sec.at[pl.ds(side * count + s * rows, rows)], sems.at[side * (slots + 1) + s]
            )
            for s in range(slots)
        ]
        source = (cot, cot_p)[side]
        return out, pltpu.make_async_copy(source, go.at[whole], sems.at[side * (slots + 1) + slots])

    last = 2 * (slots + 1)
    load_in = pltpu.make_async_copy(w_in.at[:, pl.ds(part, width)], win, sems.at[last])
    load_out = pltpu.make_async_copy(w_out.at[pl.ds(part, width), :], wout, sems.at[last + 1])
    sides = [copies_for(side) for side in range(2)]
    for c in sides[0][0]:
        c.start()
    load_in.start()
    sides[0][1].start()
    load_out.start()
    for c in sides[1][0]:
        c.start()
    sides[1][1].start()
    stores = []

    def store(source, target):
        copy = pltpu.make_async_copy(source, target, out_sems.at[len(stores)])
        copy.start()
        stores.append(copy)

    for side in range(2):
        at = slice(side * count, (side + 1) * count)
        for c in sides[side][0]:
            c.wait()
        if side == 0:
            load_in.wait()
        before = dot(sec[at, :], win[...])
        sides[side][1].wait()
        if side == 0:
            load_out.wait()
        for s in range(slots):
            mask = key_masks(counts, live, meta, s, rows, (side,), 0)[0]
            here = slice(side * count + s * rows, side * count + (s + 1) * rows)
            go[here, :] = jnp.where(mask, go[here, :], jnp.zeros((rows, width), BF))
        grad_act = dot(go[at, :], wout[...], NT)
        phi, density = gelu_parts(before)
        act[at, :] = (before * phi).astype(BF)
        pre[at, :] = (grad_act * (phi + before * density)).astype(BF)
        window = pl.ds(side * count, count)
        store(act.at[window], act_out.at[window])
        store(pre.at[window], pre_out.at[window])
    size = width // CHUNKS
    for kind, (left, right) in ((1, (act, go)), (0, (sec, pre))):
        value = dot(left[...], right[...], TN)
        for a in range(CHUNKS):
            grads[kind, a ^ me] = value[a * size:(a + 1) * size].astype(BF)
        for i, out in enumerate(grads_out):
            store(grads.at[kind, pl.ds(i * CHUNKS // 2, CHUNKS // 2)], out.at[:, kind])
    for copy in stores:
        copy.wait()


def mlp(counts, live, meta, seconds, cotangent, cotangent_p, w_fc1, w_fc2, half):
    rows, width = seconds[0].shape
    slots = len(seconds) // 2
    both = 2 * slots * rows
    operands = (*seconds, cotangent.reshape(slots * rows, width), cotangent_p.reshape(slots * rows, width), w_fc1, w_fc2)
    return pl.pallas_call(
        functools.partial(mlp_kernel, slots, half),
        out_shape=[
            jax.ShapeDtypeStruct((both, width), BF),
            jax.ShapeDtypeStruct((both, width), BF),
        ]
        + [jax.ShapeDtypeStruct((CHUNKS // 2, 2, width // CHUNKS, width), BF)] * 2,
        grid_spec=pltpu.PrefetchScalarGridSpec(
            num_scalar_prefetch=3,
            grid=(1,),
            in_specs=[HBM] * len(operands),
            out_specs=[HBM] * 4,
            scratch_shapes=[pltpu.VMEM((both, width), BF)] * 2
            + [pltpu.VMEM((width, width), BF)] * 2
            + [pltpu.VMEM((both, width), BF)] * 2
            + [
                pltpu.VMEM((2, CHUNKS, width // CHUNKS, width), BF),
                pltpu.SemaphoreType.DMA((2 * (slots + 1) + 2,)),
                pltpu.SemaphoreType.DMA((8,)),
            ],
        ),
        compiler_params=params(),
        cost_estimate=cost(2 * 4 * 2 * slots * rows * width * width, 2e7),
        name="mlp",
    )(counts, live, meta, *operands)


def lend_kernel(nt, meta, first, second, weight, out, left, held, sems):
    count, width = out.shape
    core = meta[1]
    loads = []
    for i, source in enumerate((first, second)):
        place = pl.ds(pl.multiple_of((2 * core + i) * width, width), width)
        loads.append(pltpu.make_async_copy(source.at[pl.ds(count, count)], left.at[i], sems.at[2 * i]))
        part = weight.at[:, place] if nt else weight.at[place, :]
        loads.append(pltpu.make_async_copy(part, held.at[i], sems.at[2 * i + 1]))
    for load in loads:
        load.start()
    dims = NT if nt else NN
    loads[0].wait()
    loads[1].wait()
    total = dot(left[0], held[0], dims)
    loads[2].wait()
    loads[3].wait()
    out[...] = (total + dot(left[1], held[1], dims)).astype(BF)


def lend(nt, meta, first, second, weight):
    both, width = first.shape
    return pl.pallas_call(
        functools.partial(lend_kernel, nt),
        out_shape=jax.ShapeDtypeStruct((both // 2, width), BF),
        grid_spec=pltpu.PrefetchScalarGridSpec(
            num_scalar_prefetch=1,
            grid=(1,),
            in_specs=[HBM] * 3,
            out_specs=pl.BlockSpec((both // 2, width), lambda i, *_: (0, 0)),
            scratch_shapes=[
                pltpu.VMEM((2, both // 2, width), BF),
                pltpu.VMEM((2, width, width), BF),
                pltpu.SemaphoreType.DMA((4,)),
            ],
        ),
        compiler_params=params(),
        cost_estimate=cost(2 * both * width * width, 6e6),
        name="lend",
    )(meta, first, second, weight)


def layer_norm_back(values, gain, grad):
    normed, scale = normalized(values)
    t = grad * gain
    return scale * (t - jnp.mean(t, axis=-1, keepdims=True) - normed * jnp.mean(t * normed, axis=-1, keepdims=True))


def turn_kernel(
    counts, live, meta, first, second, weight, got, hidden, cotangent, attended, gain, w_proj,
    grad_branch, grad_attended, delta, left, held, got_v, hidden_v, cot_v, att_v, proj_v, sems,
):
    slots, rows, width = grad_branch.shape
    count = slots * rows
    core = meta[1]
    loads = []
    for i, source in enumerate((first, second)):
        place = pl.ds(pl.multiple_of((2 * core + i) * width, width), width)
        loads.append(pltpu.make_async_copy(source.at[pl.ds(0, count)], left.at[i], sems.at[2 * i]))
        loads.append(pltpu.make_async_copy(weight.at[:, place], held.at[i], sems.at[2 * i + 1]))
    for i, (source, target) in enumerate(
        ((got, got_v), (hidden, hidden_v), (cotangent, cot_v), (w_proj, proj_v), (attended, att_v))
    ):
        loads.append(pltpu.make_async_copy(source, target, sems.at[4 + i]))
    for load in loads:
        load.start()
    loads[0].wait()
    loads[1].wait()
    total = dot(left[0], held[0], NT)
    loads[2].wait()
    loads[3].wait()
    total = total + dot(left[1], held[1], NT)
    for load in loads[4:]:
        load.wait()
    head = lax.broadcasted_iota(jnp.int32, (32, width), 0)
    column = lax.broadcasted_iota(jnp.int32, (32, width), 1) // HEAD_DIM
    per = GROUP // HEAD_DIM
    pick = (head == (column // per) * 8 + column % per).astype(BF)
    for s in range(slots):
        here = slice(s * rows, (s + 1) * rows)
        mask = row_mask(counts, live, meta, s, rows)
        grad_out = jnp.where(mask, cot_v[s].astype(F32), 0.0)
        given = total[here] + got_v[here, :].astype(F32)
        branch = (grad_out + layer_norm_back(hidden_v[s], gain[...], given)).astype(BF)
        grad_branch[s] = branch
        back = dot(branch, proj_v[...], NT).astype(BF)
        grad_attended[s] = back
        product = back.astype(F32) * att_v[s].astype(F32)
        high = product.astype(BF)
        low = (product - high.astype(F32)).astype(BF)
        sums = dot(pick, high, NT) + dot(pick, low, NT)
        for g in range(width // GROUP):
            delta[s, g] = sums[8 * g:8 * g + 8]


def turn(counts, live, meta, first, second, weight, got, hidden, cotangent, attended, gain, w_proj):
    slots, rows, width = hidden.shape
    count = slots * rows
    groups = width // GROUP
    whole = pl.BlockSpec(hidden.shape, lambda i, *_: (0, 0, 0))
    return pl.pallas_call(
        turn_kernel,
        out_shape=[
            jax.ShapeDtypeStruct(hidden.shape, BF),
            jax.ShapeDtypeStruct(hidden.shape, BF),
            jax.ShapeDtypeStruct((slots, groups, 8, rows), F32),
        ],
        grid_spec=pltpu.PrefetchScalarGridSpec(
            num_scalar_prefetch=3,
            grid=(1,),
            in_specs=[HBM] * 7 + [pl.BlockSpec((1, width), lambda i, *_: (0, 0)), HBM],
            out_specs=[whole, whole, pl.BlockSpec((slots, groups, 8, rows), lambda i, *_: (0, 0, 0, 0))],
            scratch_shapes=[
                pltpu.VMEM((2, count, width), BF),
                pltpu.VMEM((2, width, width), BF),
                pltpu.VMEM((count, width), BF),
                pltpu.VMEM(hidden.shape, F32),
                pltpu.VMEM(hidden.shape, BF),
                pltpu.VMEM(hidden.shape, BF),
                pltpu.VMEM((width, width), BF),
                pltpu.SemaphoreType.DMA((9,)),
            ],
        ),
        compiler_params=params(),
        cost_estimate=cost(3 * 2 * slots * rows * width * width, 1.5e7),
        name="turn",
    )(counts, live, meta, first, second, weight, got, hidden, cotangent, attended, gain, w_proj)


def finish_kernel(counts, live, meta, first, second, weight, got, hidden, output, left, held, got_v, hidden_v, sems):
    slots, rows, width = output.shape
    count = slots * rows
    core = meta[1]
    loads = []
    for i, source in enumerate((first, second)):
        place = pl.ds(pl.multiple_of((2 * core + i) * width, width), width)
        loads.append(pltpu.make_async_copy(source.at[pl.ds(0, count)], left.at[i], sems.at[2 * i]))
        loads.append(pltpu.make_async_copy(weight.at[place, :], held.at[i], sems.at[2 * i + 1]))
    loads.append(pltpu.make_async_copy(got, got_v, sems.at[4]))
    loads.append(pltpu.make_async_copy(hidden, hidden_v, sems.at[5]))
    for load in loads:
        load.start()
    loads[0].wait()
    loads[1].wait()
    total = dot(left[0], held[0])
    loads[2].wait()
    loads[3].wait()
    total = total + dot(left[1], held[1])
    loads[4].wait()
    loads[5].wait()
    for s in range(slots):
        here = slice(s * rows, (s + 1) * rows)
        mask = row_mask(counts, live, meta, s, rows)
        output[s] = jnp.where(mask, total[here] + got_v[here, :].astype(F32) + hidden_v[s], 0.0).astype(BF)


def finish(counts, live, meta, first, second, weight, got, hidden):
    slots, rows, width = hidden.shape
    count = slots * rows
    return pl.pallas_call(
        finish_kernel,
        out_shape=jax.ShapeDtypeStruct(hidden.shape, BF),
        grid_spec=pltpu.PrefetchScalarGridSpec(
            num_scalar_prefetch=3,
            grid=(1,),
            in_specs=[HBM] * 5,
            out_specs=pl.BlockSpec(hidden.shape, lambda i, *_: (0, 0, 0)),
            scratch_shapes=[
                pltpu.VMEM((2, count, width), BF),
                pltpu.VMEM((2, width, width), BF),
                pltpu.VMEM((count, width), BF),
                pltpu.VMEM(hidden.shape, F32),
                pltpu.SemaphoreType.DMA((6,)),
            ],
        ),
        compiler_params=params(),
        cost_estimate=cost(2 * 2 * slots * rows * width * width, 9e6),
        name="finish",
    )(counts, live, meta, first, second, weight, got, hidden)


def gather_kernel(mine, got, w_kv, *refs):
    key_own, value_own, key_other, value_other, partial = refs[-5:]
    width = partial.shape[-1]
    parts = []
    for place, out in ((0, (key_own, value_own)), (1, (key_other, value_other))):
        for i in range(2):
            total = (mine[0, place, i].astype(F32) + got[0, place, i].astype(F32)).astype(BF)
            out[i][0] = total
            parts.append(total)
    partial[0] = (dot(parts[2], w_kv[:, :width], NT) + dot(parts[3], w_kv[:, width:], NT)).astype(BF)


def gather(slot, slots, mine, got, w_qkv, before):
    _, _, _, rows, width = mine.shape
    row_spec = pl.BlockSpec((1, rows, width), lambda i: (slot, 0, 0))
    kv_spec = pl.BlockSpec((1, 2, 2, rows, width), lambda i: (0, 0, 0, 0, 0))
    return pl.pallas_call(
        gather_kernel,
        out_shape=[jax.ShapeDtypeStruct((slots, rows, width), BF)] * 4 + [jax.ShapeDtypeStruct((1, rows, width), BF)],
        grid=(1,),
        in_specs=[kv_spec, kv_spec, pl.BlockSpec((pl.Element(width), pl.Element(2 * width)), lambda s: (0, width))]
        + [pl.BlockSpec(memory_space=pl.ANY)] * len(before),
        out_specs=[row_spec] * 4 + [pl.BlockSpec((1, rows, width), lambda i: (0, 0, 0))],
        input_output_aliases={3 + i: i for i in range(len(before))},
        compiler_params=params(),
        cost_estimate=cost(2 * 2 * rows * width * width, 6e6),
        name="gather",
    )(mine, got, w_qkv, *before)


VALUE_UNITS = ((0, 4, 1, 0, 0), (1, 6, 0, 1, 0), (7, 8, 1, 1, 1))
QUERY_UNITS = ((0, 2, 1, 1, 0), (0, 3, 1, 0, 1), (1, 5, 0, 1, 1))


def weigh_steps(units):
    seen = set()
    steps = []
    for step in units:
        steps.append(step + (int(step[0] not in seen),))
        seen.add(step[0])
    return jnp.array(steps, jnp.int32)


def weigh_kernel(meta, steps, *refs):
    sources, (grads, held, total, sems) = refs[:9], refs[9:]
    step = pl.program_id(0)
    size = held.shape[1] // CHUNKS
    values = steps[0, 1] == VALUE_UNITS[0][1]

    def start(units):
        seen = []
        for unit in units:
            for i in unit[:2]:
                if i not in seen:
                    seen.append(i)
                    pltpu.make_async_copy(sources[i], held.at[i], sems.at[i]).start()

    @pl.when(jnp.logical_and(step == 0, values))
    def _():
        start(VALUE_UNITS)

    @pl.when(jnp.logical_and(step == 0, jnp.logical_not(values)))
    def _():
        start(QUERY_UNITS)

    left = steps[step, 0]
    right = steps[step, 1]

    @pl.when(steps[step, 5] == 1)
    def _():
        pltpu.make_async_copy(sources[0], held.at[left], sems.at[left]).wait()

    pltpu.make_async_copy(sources[0], held.at[right], sems.at[right]).wait()

    @pl.when(steps[step, 2] == 1)
    def _():
        total[...] = dot(held[left], held[right], TN)

    @pl.when(steps[step, 2] != 1)
    def _():
        total[...] += dot(held[left], held[right], TN)

    @pl.when(steps[step, 3] == 1)
    def _():
        unit = steps[step, 4]
        me = meta[4 + unit]
        for a in range(CHUNKS):
            grads[unit, a ^ me] = total[a * size:(a + 1) * size, :].astype(BF)


def weigh(meta, low, arrays):
    arrays = [a.reshape(-1, a.shape[-1]) for a in arrays]
    rows, width = arrays[0].shape
    shape = (2, CHUNKS, width // CHUNKS, width)
    steps = jnp.where(low, weigh_steps(QUERY_UNITS), weigh_steps(VALUE_UNITS))
    return pl.pallas_call(
        weigh_kernel,
        out_shape=jax.ShapeDtypeStruct(shape, BF),
        grid_spec=pltpu.PrefetchScalarGridSpec(
            num_scalar_prefetch=2,
            grid=(3,),
            in_specs=[HBM] * 9,
            out_specs=pl.BlockSpec(shape, lambda i, *_: (0, 0, 0, 0)),
            scratch_shapes=[
                pltpu.VMEM((9, rows, width), BF),
                pltpu.VMEM((rows, width), F32),
                pltpu.SemaphoreType.DMA((9,)),
            ],
        ),
        compiler_params=params(),
        cost_estimate=cost(3 * 2 * rows * width * width, 1e7),
        name="weigh",
    )(meta, steps, *arrays)


def close_kernel(gq, gk, gv, w_qkv, partial, tokens, grad_hidden, gain, out, total):
    step = pl.program_id(0)
    slots, rows, width = gq.shape
    flat = (slots * rows, width)

    @pl.when(step == 0)
    def _():
        total[...] = dot(gq[...].reshape(flat), w_qkv[...], NT)

    @pl.when(step == 1)
    def _():
        total[...] += dot(gk[...].reshape(flat), w_qkv[...], NT)

    @pl.when(step == 2)
    def _():
        total[...] += dot(gv[...].reshape(flat), w_qkv[...], NT)

    @pl.when(step > 2)
    def _():
        first = total[pl.ds(pl.multiple_of((step - 3) * rows, rows), rows), :] + partial[0].astype(F32)
        out[0] = (grad_hidden[0].astype(F32) + layer_norm_back(tokens[0].astype(F32), gain[...], first)).astype(BF)


def close(gq, gk, gv, partials, tokens, grad_hidden, gain, w_qkv):
    slots, rows, width = tokens.shape
    row_spec = pl.BlockSpec((1, rows, width), lambda i: (jnp.maximum(i - 3, 0), 0, 0))
    whole = pl.BlockSpec((slots, rows, width), lambda i: (0, 0, 0))
    (partial,) = pack([partials])
    return pl.pallas_call(
        close_kernel,
        out_shape=jax.ShapeDtypeStruct(tokens.shape, BF),
        grid=(3 + slots,),
        in_specs=[whole] * 3 + [pl.BlockSpec((width, width), lambda i: (0, jnp.minimum(i, 2)))] + [row_spec] * 3 + [
            pl.BlockSpec((1, width), lambda i: (0, 0)),
        ],
        out_specs=row_spec,
        scratch_shapes=[pltpu.VMEM((slots * rows, width), F32)],
        compiler_params=params(),
        cost_estimate=cost(3 * 2 * slots * rows * width * width, 1.2e7),
        name="close",
    )(gq, gk, gv, w_qkv, partial, tokens, grad_hidden, gain)


SPREAD = 4


def keep_row_sums(held, value):
    step = pl.program_id(0)
    rows = value.shape[0]
    column = jnp.sum(value, axis=-1, keepdims=True)
    held[pl.ds(pl.multiple_of(step * rows, rows), rows), :] = jnp.broadcast_to(column, (rows, 128))


def put_row_sums(norm, held, gain):
    @pl.when(pl.program_id(0) == pl.num_programs(0) - 1)
    def _():
        for r in range(norm.shape[0]):
            norm[r:r + 1, :] = held[r * 128:(r + 1) * 128, :].T[:1] / gain[r:r + 1, :]


def spread_mlp_kernel(meta, own0, own1, part0, part1, w_fc1, gain, grad_fc1, grad_fc2, norm, held):
    size, width = own0.shape[-2:]
    first = meta[1] == 0
    for half, (own, part) in enumerate(((own0, part0), (own1, part1))):
        for a in range(4):
            w = (a // 2) ^ meta[8]
            x = (a % 2) ^ meta[3]
            at = (x, 0, 0, w) if half == 0 else (0, x, 0, w)
            for place, (yes, no) in ((half, (own, part)), (2 + half, (part, own))):
                value = jnp.where(first, yes[at], no[at]).astype(F32)
                grad_fc1[a * size:(a + 1) * size, place * width:(place + 1) * width] = value[0]
                grad_fc2[place, a * size:(a + 1) * size, :] = value[1]
    keep_row_sums(held, grad_fc1[...] * w_fc1[...].astype(F32))
    put_row_sums(norm, held, gain)


def spread_mlp(meta, own0, own1, part0, part1, w_fc1, gain):
    width, hidden_width = w_fc1.shape
    size = own0.shape[-2]
    per = CHUNKS // SPREAD
    chunks = [c.reshape((2, 2, 2, 2) + c.shape[1:]) for c in (own0, own1, part0, part1)]
    block = (2, size, width)
    by_x = pl.BlockSpec((2, 1, 1, 2) + block, lambda a, meta: (0, (a % 2) ^ meta[6], (a // 2) ^ meta[7], 0, 0, 0, 0))
    by_y = pl.BlockSpec((1, 2, 1, 2) + block, lambda a, meta: ((a % 2) ^ meta[6], 0, (a // 2) ^ meta[7], 0, 0, 0, 0))
    outs = pl.pallas_call(
        spread_mlp_kernel,
        out_shape=[
            jax.ShapeDtypeStruct((width, hidden_width), F32),
            jax.ShapeDtypeStruct((4, width, width), F32),
            jax.ShapeDtypeStruct((width // 128, 128), F32),
        ],
        grid_spec=pltpu.PrefetchScalarGridSpec(
            num_scalar_prefetch=1,
            grid=(SPREAD,),
            in_specs=[by_x, by_y, by_x, by_y] + [
                pl.BlockSpec((per * size, hidden_width), lambda a, *_: (a, 0)),
                pl.BlockSpec((width // 128, 128), lambda a, *_: (0, 0)),
            ],
            out_specs=[
                pl.BlockSpec((per * size, hidden_width), lambda a, *_: (a, 0)),
                pl.BlockSpec((4, per * size, width), lambda a, *_: (0, a, 0)),
                pl.BlockSpec((width // 128, 128), lambda a, *_: (0, 0)),
            ],
            scratch_shapes=[pltpu.VMEM((width, 128), F32)],
        ),
        compiler_params=params(),
        cost_estimate=cost(1e6, 4.7e7),
        name="spread_mlp",
    )(meta, *chunks, w_fc1, gain.reshape(width // 128, 128))
    return outs[0], outs[1].reshape(hidden_width, width), outs[2].reshape(width)


def spread_qkv_kernel(meta, own0, own1, part0, part1, w_qkv, gain, grad_qkv, grad_proj, norm, held):
    width = own0.shape[-1]
    first = meta[1] == 0
    per = own0.shape[0]
    size = own0.shape[1]
    for a in range(per):
        here = slice(a * size, (a + 1) * size)
        at0 = a ^ (meta[4] % per)
        at1 = a ^ (meta[5] % per)
        grad_qkv[here, :width] = jnp.where(first, own0[at0], part0[at0]).astype(F32)
        grad_qkv[here, width:2 * width] = jnp.where(first, own1[at1], part1[at1]).astype(F32)
        grad_qkv[here, 2 * width:] = jnp.where(first, part0[at0], own0[at0]).astype(F32)
        grad_proj[here, :] = jnp.where(first, part1[at1], own1[at1]).astype(F32)
    keep_row_sums(held, grad_qkv[...] * w_qkv[...].astype(F32))
    put_row_sums(norm, held, gain)


def spread_qkv(meta, own0, own1, part0, part1, w_qkv, gain):
    width = w_qkv.shape[0]
    size = width // CHUNKS
    per = CHUNKS // SPREAD

    def chunk(place):
        return pl.BlockSpec((per, size, width), lambda a, meta: (a ^ (meta[place] // per), 0, 0))

    def rows(columns):
        return pl.BlockSpec((per * size, columns), lambda a, *_: (a, 0))

    line = pl.BlockSpec((width // 128, 128), lambda a, *_: (0, 0))
    outs = pl.pallas_call(
        spread_qkv_kernel,
        out_shape=[
            jax.ShapeDtypeStruct((width, 3 * width), F32),
            jax.ShapeDtypeStruct((width, width), F32),
            jax.ShapeDtypeStruct((width // 128, 128), F32),
        ],
        grid_spec=pltpu.PrefetchScalarGridSpec(
            num_scalar_prefetch=1,
            grid=(SPREAD,),
            in_specs=[chunk(4), chunk(5), chunk(4), chunk(5), rows(3 * width), line],
            out_specs=[rows(3 * width), rows(width), line],
            scratch_shapes=[pltpu.VMEM((width, 128), F32)],
        ),
        compiler_params=params(),
        cost_estimate=cost(1e6, 1.8e7),
        name="spread_qkv",
    )(meta, own0, own1, part0, part1, w_qkv, gain.reshape(width // 128, 128))
    return outs[0], outs[1], outs[2].reshape(width)


DIGITS = {"x": (0, 2), "y": (1, 0), "z": (2, 0), "w": (4, 0)}


def swap(value, axis, mask):
    return lax.ppermute(value, axis, [(i, i ^ mask) for i in range(lax.axis_size(axis))])


def swap_digits(value, masks):
    batch, band = masks
    if not band:
        return swap(value, "batch", batch)
    if not batch:
        return swap(value, "band", band)
    return swap(value, ("batch", "band"), batch * lax.axis_size("band") + band)


def add(*values):
    total = values[0].astype(F32)
    for value in values[1:]:
        total = total + value.astype(F32)
    return total.astype(BF)


def pack_kernel(counts, *refs):
    total = sum(counts)
    sources, refs = refs[:total], refs[total:]
    targets, refs = refs[:len(counts)], refs[len(counts):]
    held, (sems, out_sems) = refs[:len(counts)], refs[len(counts):]
    loads, stores = [], []
    for group, count in enumerate(counts):
        for i in range(count):
            at = len(loads)
            size = sources[at].shape[0]
            here = pl.ds(i * size, size)
            loads.append(pltpu.make_async_copy(sources[at], held[group].at[here], sems.at[at]))
            stores.append(pltpu.make_async_copy(held[group].at[here], targets[group].at[here], out_sems.at[at]))
    for load in loads:
        load.start()
    for load, store in zip(loads, stores):
        load.wait()
        store.start()
    for store in stores:
        store.wait()


def pack(groups):
    shapes = [(len(g) * g[0].shape[0],) + g[0].shape[1:] for g in groups]
    parts = [p for g in groups for p in g]
    return pl.pallas_call(
        functools.partial(pack_kernel, [len(g) for g in groups]),
        out_shape=[jax.ShapeDtypeStruct(shape, BF) for shape in shapes],
        in_specs=[HBM] * len(parts),
        out_specs=[HBM] * len(groups),
        scratch_shapes=[pltpu.VMEM(shape, BF) for shape in shapes]
        + [pltpu.SemaphoreType.DMA((len(parts),))] * 2,
        compiler_params=params(),
        cost_estimate=cost(0, 2e6),
        name="pack",
    )(*parts)


class Line:
    def __init__(self):
        self.mark = None

    def tie(self, value):
        if self.mark is None:
            return value
        value, self.mark = lax.optimization_barrier((value, self.mark))
        return value


class Chain:
    def __init__(self, order, terms, upper=None, inner=True, outer=True, joins=None):
        self.terms = list(terms)
        self.upper = upper
        self.steps = [("part", group) for group in order]
        mask = 8
        while inner and mask < lax.axis_size("batch"):
            self.steps.append(("full", mask))
            mask *= 2
        self.steps += [("join", group) for group in (reversed(order) if joins is None else joins)]
        if outer:
            self.steps.append(("core", None))
        self.value = None
        self.other = None

    def masks(self, group):
        count = 1 << len(group)
        masks = []
        for place in range(1, count):
            digits = [DIGITS[d] for i, d in enumerate(group) if place & (count >> (i + 1))]
            masks.append((sum(d[0] for d in digits), sum(d[1] for d in digits)))
        return masks

    def total(self):
        return add(*self.terms)

    def offers(self):
        kind, what = self.steps[0]
        if self.upper is not None:
            sent, self.upper = [self.upper], None
            return sent
        if kind == "part":
            count = 1 << len(what)
            size = self.terms[0].shape[0] // count
            sent = [add(*[t[i * size:(i + 1) * size] for t in self.terms]) for i in range(1, count)]
            self.terms = [t[:size] for t in self.terms]
            return sent
        if self.value is None or kind == "full":
            self.value = self.total() if len(self.terms) > 1 else self.terms[0]
            self.terms = [self.value]
        return [self.value]

    def start(self, sent):
        kind, what = self.steps[0]
        if kind == "full":
            return [swap(sent[0], "batch", what)]
        if kind == "core":
            return [swap(sent[0], "band", 1)]
        masks = self.masks(what)
        if kind == "join":
            sent = sent * len(masks)
        return [swap_digits(s, mask) for s, mask in zip(sent, masks)]

    def take(self, moved):
        kind, _ = self.steps.pop(0)
        if kind == "join":
            return [self.value] + moved
        if kind == "core":
            self.other = moved[0]
        else:
            self.terms = self.terms + moved
        return None


class Flight:
    def __init__(self, line):
        self.line = line
        self.parts = {}

    def land(self, *names):
        names = [n for n in (names or tuple(self.parts)) if n in self.parts]
        if not names:
            return {}
        held = [self.parts.pop(n) for n in names]
        got = self.line.tie(held)
        self.line.mark = got
        joins = []
        for name, moved in zip(names, got):
            if isinstance(name, Chain):
                parts = name.take(moved)
                if parts:
                    joins.append((name, parts))
        if joins:
            for (chain, _), value in zip(joins, pack([parts for _, parts in joins])):
                chain.value = value
        return {n: g[0] for n, g in zip(names, got) if not isinstance(n, Chain)}

    def launch(self, *items):
        items = [i for i in items if not isinstance(i, Chain) or i.steps]
        arrays = [i.offers() if isinstance(i, Chain) else [i[1]] for i in items]
        arrays = self.line.tie(arrays)
        self.line.mark = arrays
        for item, sent in zip(items, arrays):
            if isinstance(item, Chain):
                self.parts[item] = item.start(sent)
            else:
                name, _, axis, mask = item
                self.parts[name] = [swap(sent[0], axis, mask)]


def place_in(order):
    place = 0
    for digit in "".join(order):
        batch, band = DIGITS[digit]
        bit = lax.axis_index("batch") // batch if batch else lax.axis_index("band") // band
        place = place * 2 + bit % 2
    return place


ORDER = ("z", "y", "wx")
LAST_ORDERS = (("x", "y"), ("y", "x"))


def body(
    tokens, w_qkv, w_proj, w_fc1, w_fc2, gain_one, gain_two, cotangent, band_counts, slot_live
):
    slots, rows, width = tokens.shape
    flat = (slots * rows, width)
    band = lax.axis_index("band")
    core = band % 2
    meta = jnp.stack(
        [band, core] + [place_in(o) for o in (ORDER, "x") + tuple(order + ("zw",) for order in LAST_ORDERS) + ("y", "z", "w")]
    ).astype(jnp.int32)
    gain_one = gain_one[None]
    gain_two = gain_two[None]
    at = (band_counts, slot_live, meta)
    line = Line()

    tokens, *tokens_other = lax.optimization_barrier(
        (tokens,) + tuple(tokens[s:s + 1] for s in range(slots))
    )
    tokens_other = [swap(t, "band", 2) for t in tokens_other]
    cotangent_p = swap(cotangent, "band", 1)
    first_own, query, kv_own = project(tokens, w_qkv, gain_one)
    line.mark = (first_own, meta, gain_two)
    first_other, pairs = [], []
    seconds, seconds_p = [], []
    kept = ()

    def take(s):
        first, pair = project_other(s, line.tie(tokens_other[s]), kv_own, w_qkv, gain_one, first_other)
        line.mark = pair
        first_other[:] = [first]
        pairs.append((pair, swap(pair, "band", 1)))

    def look(s):
        *out, second = attend(s, *at, line.tie(query), *pairs[s], tokens, w_proj, gain_two, kept)
        line.mark = second
        seconds.append(second)
        seconds_p.append(swap(second, "band", 1))
        return tuple(out)

    take(0)
    for s in range(slots):
        if s == 1:
            for n in range(1, slots):
                take(n)
            cotangent_p = line.tie(cotangent_p)
        kept = look(s)
    attended, lse, hidden = kept

    flight = Flight(line)
    chains = []
    acts, pres = [], []
    all_seconds = seconds + seconds_p
    for half in range(2):
        act, pre, lower, upper = mlp(
            *at, [line.tie(all_seconds[0])] + all_seconds[1:], cotangent, cotangent_p, w_fc1, w_fc2, half
        )
        line.mark = upper
        acts.append(act)
        pres.append(pre)
        chains.append(Chain(ORDER, (lower,), upper, outer=False, joins=()))
        if half == 0:
            flight.launch(chains[0])
    one, two = chains
    turn_part = lend(True, meta, line.tie(pres[0]), pres[1], w_fc1)
    line.mark = turn_part
    finish_part = lend(False, meta, line.tie(acts[0]), acts[1], w_fc2)
    line.mark = finish_part
    flight.land()
    flight.launch(("turn", turn_part, "band", 1), two, one, ("finish", finish_part, "band", 1))
    got = flight.land("turn")
    branch, grad_attended, delta = turn(
        *at, line.tie(pres[0]), pres[1], w_fc1, got["turn"], hidden, cotangent, attended, gain_two, w_proj
    )
    line.mark = delta

    grad_query, sums, keeps, waiting = (), (), [], []

    def bring(s):
        *kept_sums, partial = gather(s, slots, line.tie(keeps[s]), got[f"send{s}"], w_qkv, sums)
        line.mark = partial
        return tuple(kept_sums), [(f"partial{s}", partial, "band", 2)]

    for s in range(slots):
        query_grad, keep, send = attend_back(
            s, *at, line.tie(query), *pairs[s], grad_attended, lse, delta, grad_query
        )
        line.mark = send
        grad_query = (query_grad,)
        keeps.append(keep)
        got.update(flight.land())
        if s == slots - 1:
            while one.steps or two.steps:
                flight.launch(one, two)
                flight.land(one, two)
            both = Chain((), (jnp.stack([one.total(), two.total()], axis=1),), inner=False, outer=False, joins=("w", "z"))
            flight.launch((f"send{s}", send, "band", 1), *waiting, both)
        else:
            flight.launch((f"send{s}", send, "band", 1), *waiting, two, one)
        if s > 0:
            sums, waiting = bring(s - 1)
    got.update(flight.land())
    flight.launch(*waiting, both)
    sums, waiting = bring(slots - 1)
    arrays = (first_own, first_other[0], grad_query[0], *sums, attended, branch)
    theirs = weigh(meta, core == 1, (line.tie(first_own),) + arrays[1:])
    line.mark = theirs
    got.update(flight.land())
    one = Chain((), (both.value[:, 0],), inner=False, joins=("y", "x"))
    two = Chain((), (both.value[:, 1],), inner=False, joins=("x", "y"))
    flight.launch(("theirs", theirs, "band", 1), one, two)
    ours = weigh(meta, core == 0, (line.tie(first_own),) + arrays[1:])
    line.mark = ours
    got.update(flight.land())
    theirs = got["theirs"]
    three = Chain(LAST_ORDERS[0], (ours[0], theirs[0]), inner=False)
    four = Chain(LAST_ORDERS[1], (ours[1], theirs[1]), inner=False)
    flight.launch(three, four)
    output = finish(*at, line.tie(acts[0]), acts[1], w_fc2, got["finish"], hidden)
    line.mark = output
    flight.land(three, four)
    flight.launch(three, four)
    flight.land(three, four)
    five = Chain(("zw",), (jnp.stack([three.total(), four.total()], axis=1),), outer=False)
    flight.launch(five, one, two, *waiting)
    while len(five.steps) > 1:
        flight.land(five)
        flight.launch(five)
    got.update(flight.land(one, two, f"partial{slots - 1}"))
    flight.land(five)
    three.value, four.value = five.value[:, 0], five.value[:, 1]
    flight.launch(three, four, one, two)
    partials = [got[f"partial{s}"] for s in range(slots)]
    grad_input = close(
        line.tie(grad_query[0]), sums[0], sums[1], partials, tokens, branch, gain_one, w_qkv
    )
    line.mark = grad_input
    flight.land()
    flight.launch(three, four)
    grad_fc1, grad_fc2, norm2 = spread_mlp(
        meta, line.tie(one.value), two.value, one.other, two.other, w_fc1, gain_two
    )
    line.mark = norm2
    while three.steps or four.steps:
        flight.land(three, four)
        flight.launch(three, four)
    grad_qkv, grad_proj, norm1 = spread_qkv(
        meta, line.tie(three.value), four.value, three.other, four.other, w_qkv, gain_one
    )
    return (output, grad_input, grad_qkv, grad_proj, grad_fc1, grad_fc2, norm1, norm2)


def solution(mesh):
    placed = (
        P("batch", "band", None),
        P(),
        P(),
        P(),
        P(),
        P(),
        P(),
        P("batch", "band", None),
        P("batch", None),
        P("batch"),
    )
    return jax.shard_map(
        body,
        mesh=mesh,
        in_specs=placed,
        out_specs=(
            P("batch", "band", None),
            P("batch", "band", None),
            P(),
            P(),
            P(),
            P(),
            P(),
            P(),
        ),
        check_vma=False,
    )
```

```python
import functools
import jax
import jax.numpy as jnp
from jax import lax
from jax.experimental import pallas as pl
from jax.experimental.pallas import tpu as pltpu
from jax.sharding import PartitionSpec as P

BF = jnp.bfloat16
F32 = jnp.float32
EPSILON = 1e-06
HEAD_DIM = 64
GROUP = 256
NN = (((1,), (0,)), ((), ()))
NT = (((1,), (1,)), ((), ()))
TN = (((0,), (0,)), ((), ()))


def dot(left, right, dims=NN):
    return lax.dot_general(left, right, dims, preferred_element_type=F32)


def params(mib=60):
    return pltpu.CompilerParams(vmem_limit_bytes=mib * 1024 * 1024)


def cost(flops, moved, exps=0):
    return pl.CostEstimate(flops=1, bytes_accessed=1, transcendentals=0)


HBM = pl.BlockSpec(memory_space=pl.ANY)


def normalized(values):
    centered = values - jnp.mean(values, axis=-1, keepdims=True)
    spread = jnp.mean(centered * centered, axis=-1, keepdims=True)
    scale = lax.rsqrt(spread + EPSILON)
    return centered * scale, scale


def project_kernel(tokens, weight, gain, first_in, query, both):
    normed, _ = normalized(tokens[0].astype(F32))
    first = (normed * gain[...]).astype(BF)
    first_in[0] = first
    width = first.shape[1]
    query[0] = (dot(first, weight[:, :width]) * HEAD_DIM ** -0.5).astype(BF)
    both[0, 0] = dot(first, weight[:, width:2 * width]).astype(BF)
    both[0, 1] = dot(first, weight[:, 2 * width:]).astype(BF)


def project(tokens, w_qkv, gain):
    slots, rows, width = tokens.shape
    row_spec = pl.BlockSpec((1, rows, width), lambda s: (s, 0, 0))
    return pl.pallas_call(
        project_kernel,
        out_shape=[
            jax.ShapeDtypeStruct(tokens.shape, BF),
            jax.ShapeDtypeStruct(tokens.shape, BF),
            jax.ShapeDtypeStruct((slots, 2, rows, width), BF),
        ],
        grid=(slots,),
        in_specs=[
            row_spec,
            pl.BlockSpec((width, 3 * width), lambda s: (0, 0)),
            pl.BlockSpec((1, width), lambda s: (0, 0)),
        ],
        out_specs=[row_spec, row_spec, pl.BlockSpec((1, 2, rows, width), lambda s: (s, 0, 0, 0))],
        compiler_params=params(),
        cost_estimate=cost(2 * slots * rows * width * width * 3, 8e6),
        name="project",
    )(tokens, w_qkv, gain)


def project_other_kernel(tokens, own, weight, gain, *refs):
    first_in, both = refs[-2:]
    normed, _ = normalized(tokens[0].astype(F32))
    first = (normed * gain[...]).astype(BF)
    first_in[0] = first
    width = first.shape[1]
    both[0] = own[0]
    both[1, 0] = dot(first, weight[:, :width]).astype(BF)
    both[1, 1] = dot(first, weight[:, width:]).astype(BF)


def project_other(slot, tokens, kv_own, w_qkv, gain, before):
    slots, _, rows, width = kv_own.shape
    return pl.pallas_call(
        project_other_kernel,
        out_shape=[
            jax.ShapeDtypeStruct((slots, rows, width), BF),
            jax.ShapeDtypeStruct((2, 2, rows, width), BF),
        ],
        grid=(1,),
        in_specs=[
            pl.BlockSpec((1, rows, width), lambda i: (0, 0, 0)),
            pl.BlockSpec((1, 2, rows, width), lambda i: (slot, 0, 0, 0)),
            pl.BlockSpec((pl.Element(width), pl.Element(2 * width)), lambda i: (0, width)),
            pl.BlockSpec((1, width), lambda i: (0, 0)),
        ] + [HBM] * len(before),
        out_specs=[
            pl.BlockSpec((1, rows, width), lambda i: (slot, 0, 0)),
            pl.BlockSpec((2, 2, rows, width), lambda i: (0, 0, 0, 0)),
        ],
        input_output_aliases={4 + i: i for i in range(len(before))},
        compiler_params=params(),
        cost_estimate=cost(2 * rows * width * width * 2, 5e6),
        name="project_other",
    )(tokens, kv_own, w_qkv, gain, *before)


def key_masks(counts, live, meta, slot, rows, flips, axis):
    shape = (rows, 1) if axis == 0 else (1, rows)
    place = lax.broadcasted_iota(jnp.int32, shape, axis)
    alive = live[slot] > 0
    return [place < jnp.where(alive, counts[slot, meta[0] ^ flip], 0) for flip in flips]


FLIPS = (0, 2, 1, 3)


def attend_kernel(slot, counts, live, meta, query, pair, pair_p, tokens, w_proj, gain, *refs):
    attended, lse, hidden, second, held, own_tokens, weight, sems = refs[-8:]
    group = pl.program_id(0)
    rows = query.shape[1]
    copies = (
        pltpu.make_async_copy(tokens.at[slot], own_tokens, sems.at[0]),
        pltpu.make_async_copy(w_proj, weight, sems.at[1]),
    )

    @pl.when(group == 0)
    def _():
        for copy in copies:
            copy.start()

    masks = key_masks(counts, live, meta, slot, rows, FLIPS, 1)
    q = query[0]
    lane = lax.broadcasted_iota(jnp.int32, (1, GROUP), 1)
    result = jnp.zeros((rows, GROUP), F32)
    sums = jnp.zeros((rows, 128), F32)
    lane128 = lax.broadcasted_iota(jnp.int32, (1, 128), 1)
    blocks = (pair.at[0], pair.at[1], pair_p.at[0], pair_p.at[1])
    for h in range(GROUP // HEAD_DIM):
        here = (lane // HEAD_DIM) == h
        qm = jnp.where(here, q, jnp.zeros_like(q))
        scores = [
            jnp.where(mask, dot(qm, block[0], NT), -10000.0) for mask, block in zip(masks, blocks)
        ]
        top = scores[0]
        for s in scores[1:]:
            top = jnp.maximum(top, s)
        top = jnp.max(top, axis=-1, keepdims=True)
        out = jnp.zeros((rows, GROUP), F32)
        exps = [jnp.exp(s - top) for s in scores]
        total = exps[0]
        for e in exps[1:]:
            total = total + e
        total = jnp.sum(total, axis=-1, keepdims=True)
        for e, block in zip(exps, blocks):
            out = out + dot(e.astype(BF), block[1])
        result = jnp.where(here, out * (1.0 / total), result)
        sums = jnp.where(lane128 == h, top + jnp.log(total), sums)
    low = result.astype(BF)
    attended[0] = low
    held[group] = low
    lse[0, 0] = sums.T[:8]

    @pl.when(group == pl.num_programs(0) - 1)
    def _():
        for copy in copies:
            copy.wait()
        value = own_tokens[...].astype(F32)
        for g in range(held.shape[0]):
            value = value + dot(held[g], weight[g * GROUP:(g + 1) * GROUP, :])
        hidden[0] = value
        normed, _ = normalized(value)
        second[...] = (normed * gain[...]).astype(BF)


def attend(slot, counts, live, meta, query, pair, pair_p, tokens, w_proj, gain, before):
    slots, rows, width = query.shape
    groups = width // GROUP
    at = slot
    kv_spec = pl.BlockSpec((2, 2, rows, GROUP), lambda g, *_: (0, 0, 0, g))
    piece = pl.BlockSpec((1, rows, GROUP), lambda g, *_: (at, 0, g))
    row_spec = pl.BlockSpec((1, rows, width), lambda g, *_: (at, 0, 0))
    operands = (counts, live, meta, query, pair, pair_p, tokens, w_proj, gain)
    return pl.pallas_call(
        functools.partial(attend_kernel, slot),
        out_shape=[
            jax.ShapeDtypeStruct(query.shape, BF),
            jax.ShapeDtypeStruct((slots, groups, 8, rows), F32),
            jax.ShapeDtypeStruct(query.shape, F32),
            jax.ShapeDtypeStruct((rows, width), BF),
        ],
        grid_spec=pltpu.PrefetchScalarGridSpec(
            num_scalar_prefetch=3,
            grid=(groups,),
            in_specs=[piece, kv_spec, kv_spec, HBM, HBM, pl.BlockSpec((1, width), lambda g, *_: (0, 0))]
            + [HBM] * len(before),
            out_specs=[
                piece,
                pl.BlockSpec((1, 1, 8, rows), lambda g, *_: (at, g, 0, 0)),
                row_spec,
                pl.BlockSpec((rows, width), lambda g, *_: (0, 0)),
            ],
            scratch_shapes=[
                pltpu.VMEM((groups, rows, GROUP), BF),
                pltpu.VMEM((rows, width), BF),
                pltpu.VMEM((width, width), BF),
                pltpu.SemaphoreType.DMA((2,)),
            ],
        ),
        input_output_aliases={len(operands) + i: i for i in range(len(before))},
        compiler_params=params(),
        cost_estimate=cost(2 * 2 * rows * 4 * rows * 4 * width, 1e7, 12 * rows * 4 * rows),
        name="attend",
    )(*operands, *before)


def attend_back_kernel(
    slot, counts, live, meta, query, pair, pair_p, grad, lse, delta, *refs
):
    grad_query, grad_keep, grad_send, probs, slopes, qms, gms, keys, values, keys_t = refs[-10:]
    rows = query.shape[1]
    heads = GROUP // HEAD_DIM
    masks = key_masks(counts, live, meta, slot, rows, FLIPS, 0)
    q = query[0]
    ga = grad[0]
    lane = lax.broadcasted_iota(jnp.int32, (1, GROUP), 1)
    zero = jnp.zeros_like(q)
    for h in range(heads):
        here = (lane // HEAD_DIM) == h
        qms[h * rows:(h + 1) * rows, :] = jnp.where(here, q, zero)
        gms[h * rows:(h + 1) * rows, :] = jnp.where(here, ga, zero)
    for i, mask in enumerate(masks):
        block = (pair, pair_p)[i // 2]
        keys[i * rows:(i + 1) * rows, :] = jnp.where(mask, block[i % 2, 0], zero)
        values[i * rows:(i + 1) * rows, :] = block[i % 2, 1]
    keys_t[...] = keys[...].T
    gq = []
    for h in range(heads):
        mine = slice(h * rows, (h + 1) * rows)
        for i, mask in enumerate(masks):
            at = slice(i * rows, (i + 1) * rows)
            scores = jnp.where(mask, dot(keys[at, :], qms[mine, :], NT), -10000.0)
            gp = dot(values[at, :], gms[mine, :], NT)
            p = jnp.exp(scores - lse[0, 0, h:h + 1, :])
            probs[at, mine] = p.astype(BF)
            slopes[at, mine] = (p * (gp - delta[0, 0, h:h + 1, :])).astype(BF)
        gq.append(dot(keys_t[h * HEAD_DIM:(h + 1) * HEAD_DIM, :], slopes[:, mine]))
    gk = dot(slopes[...], qms[...])
    gv = dot(probs[...], gms[...])
    outs = ((grad_keep, 0), (grad_keep, 1), (grad_send, 0), (grad_send, 1))
    for i, ((out, place), mask) in enumerate(zip(outs, masks)):
        at = slice(i * rows, (i + 1) * rows)
        out[0, place, 0] = jnp.where(mask, gk[at], 0.0).astype(BF)
        out[0, place, 1] = gv[at].astype(BF)
    grad_query[0] = (jnp.concatenate(gq, axis=0).T * HEAD_DIM ** -0.5).astype(BF)


def attend_back(slot, counts, live, meta, query, pair, pair_p, grad, lse, delta, before):
    slots, rows, width = query.shape
    groups = width // GROUP
    heads = GROUP // HEAD_DIM
    at = slot
    kv_spec = pl.BlockSpec((2, 2, rows, GROUP), lambda g, *_: (0, 0, 0, g))
    row_spec = pl.BlockSpec((1, rows, GROUP), lambda g, *_: (at, 0, g))
    stat_spec = pl.BlockSpec((1, 1, 8, rows), lambda g, *_: (at, g, 0, 0))
    out_spec = pl.BlockSpec((1, 2, 2, rows, GROUP), lambda g, *_: (0, 0, 0, 0, g))
    operands = (counts, live, meta, query, pair, pair_p, grad, lse, delta)
    return pl.pallas_call(
        functools.partial(attend_back_kernel, slot),
        out_shape=[
            jax.ShapeDtypeStruct(query.shape, BF),
            jax.ShapeDtypeStruct((1, 2, 2, rows, width), BF),
            jax.ShapeDtypeStruct((1, 2, 2, rows, width), BF),
        ],
        grid_spec=pltpu.PrefetchScalarGridSpec(
            num_scalar_prefetch=3,
            grid=(groups,),
            in_specs=[row_spec, kv_spec, kv_spec, row_spec, stat_spec, stat_spec]
            + [pl.BlockSpec(memory_space=pl.ANY)] * len(before),
            out_specs=[row_spec, out_spec, out_spec],
            scratch_shapes=[
                pltpu.VMEM((4 * rows, heads * rows), BF),
                pltpu.VMEM((4 * rows, heads * rows), BF),
                pltpu.VMEM((heads * rows, GROUP), BF),
                pltpu.VMEM((heads * rows, GROUP), BF),
                pltpu.VMEM((4 * rows, GROUP), BF),
                pltpu.VMEM((4 * rows, GROUP), BF),
                pltpu.VMEM((GROUP, 4 * rows), BF),
            ],
        ),
        input_output_aliases={len(operands) + i: i for i in range(len(before))},
        compiler_params=params(),
        cost_estimate=cost(5 * 2 * rows * 4 * rows * 4 * width, 2e7, 12 * rows * 4 * rows),
        name="attend_back",
    )(*operands, *before)


CHUNKS = 16


def row_mask(counts, live, meta, slot, rows):
    return key_masks(counts, live, meta, slot, rows, (0,), 0)[0]


def gelu_parts(v):
    size = jnp.abs(v)
    decay = jnp.exp2(v * v * (-0.5 * 1.4426950408889634))
    scale = 1.0 + (0.3275911 * 0.7071067811865476) * size
    t = pl.reciprocal(scale, approx=True)
    t = t * (2.0 - scale * t)
    poly = t * (0.127414796 + t * (-0.142248368 + t * (0.7107068705 + t * (-0.7265760135 + t * 0.5307027145))))
    tail = poly * decay
    phi = jnp.where(v >= 0, 1.0 - tail, tail)
    return phi, decay * 0.3989422804014327


def mlp_kernel(slots, half, counts, live, meta, *refs):
    seconds, rest = refs[:2 * slots], refs[2 * slots:]
    cot, cot_p, w_in, w_out, act_out, pre_out, *grads_out = rest[:8]
    sec, go, win, wout, act, pre, grads, sems, out_sems = rest[8:]
    rows = seconds[0].shape[0]
    count = slots * rows
    width = sec.shape[1]
    me = meta[2]
    part = pl.multiple_of((2 * meta[1] + half) * width, width)

    def copies_for(side):
        whole = pl.ds(side * count, count)
        out = [
            pltpu.make_async_copy(
                seconds[side * slots + s], sec.at[pl.ds(side * count + s * rows, rows)], sems.at[side * (slots + 1) + s]
            )
            for s in range(slots)
        ]
        source = (cot, cot_p)[side]
        return out, pltpu.make_async_copy(source, go.at[whole], sems.at[side * (slots + 1) + slots])

    last = 2 * (slots + 1)
    load_in = pltpu.make_async_copy(w_in.at[:, pl.ds(part, width)], win, sems.at[last])
    load_out = pltpu.make_async_copy(w_out.at[pl.ds(part, width), :], wout, sems.at[last + 1])
    sides = [copies_for(side) for side in range(2)]
    for c in sides[0][0]:
        c.start()
    load_in.start()
    sides[0][1].start()
    load_out.start()
    for c in sides[1][0]:
        c.start()
    sides[1][1].start()
    stores = []

    def store(source, target):
        copy = pltpu.make_async_copy(source, target, out_sems.at[len(stores)])
        copy.start()
        stores.append(copy)

    for side in range(2):
        at = slice(side * count, (side + 1) * count)
        for c in sides[side][0]:
            c.wait()
        if side == 0:
            load_in.wait()
        before = dot(sec[at, :], win[...])
        sides[side][1].wait()
        if side == 0:
            load_out.wait()
        for s in range(slots):
            mask = key_masks(counts, live, meta, s, rows, (side,), 0)[0]
            here = slice(side * count + s * rows, side * count + (s + 1) * rows)
            go[here, :] = jnp.where(mask, go[here, :], jnp.zeros((rows, width), BF))
        grad_act = dot(go[at, :], wout[...], NT)
        phi, density = gelu_parts(before)
        act[at, :] = (before * phi).astype(BF)
        pre[at, :] = (grad_act * (phi + before * density)).astype(BF)
        window = pl.ds(side * count, count)
        store(act.at[window], act_out.at[window])
        store(pre.at[window], pre_out.at[window])
    size = width // CHUNKS
    for kind, (left, right) in ((1, (act, go)), (0, (sec, pre))):
        value = dot(left[...], right[...], TN)
        for a in range(CHUNKS):
            grads[kind, a ^ me] = value[a * size:(a + 1) * size].astype(BF)
        for i, out in enumerate(grads_out):
            store(grads.at[kind, pl.ds(i * CHUNKS // 2, CHUNKS // 2)], out.at[:, kind])
    for copy in stores:
        copy.wait()


def mlp(counts, live, meta, seconds, cotangent, cotangent_p, w_fc1, w_fc2, half):
    rows, width = seconds[0].shape
    slots = len(seconds) // 2
    both = 2 * slots * rows
    operands = (*seconds, cotangent.reshape(slots * rows, width), cotangent_p.reshape(slots * rows, width), w_fc1, w_fc2)
    return pl.pallas_call(
        functools.partial(mlp_kernel, slots, half),
        out_shape=[
            jax.ShapeDtypeStruct((both, width), BF),
            jax.ShapeDtypeStruct((both, width), BF),
        ]
        + [jax.ShapeDtypeStruct((CHUNKS // 2, 2, width // CHUNKS, width), BF)] * 2,
        grid_spec=pltpu.PrefetchScalarGridSpec(
            num_scalar_prefetch=3,
            grid=(1,),
            in_specs=[HBM] * len(operands),
            out_specs=[HBM] * 4,
            scratch_shapes=[pltpu.VMEM((both, width), BF)] * 2
            + [pltpu.VMEM((width, width), BF)] * 2
            + [pltpu.VMEM((both, width), BF)] * 2
            + [
                pltpu.VMEM((2, CHUNKS, width // CHUNKS, width), BF),
                pltpu.SemaphoreType.DMA((2 * (slots + 1) + 2,)),
                pltpu.SemaphoreType.DMA((8,)),
            ],
        ),
        compiler_params=params(),
        cost_estimate=cost(2 * 4 * 2 * slots * rows * width * width, 2e7),
        name="mlp",
    )(counts, live, meta, *operands)


def lend_kernel(nt, meta, first, second, weight, out, left, held, sems):
    count, width = out.shape
    core = meta[1]
    loads = []
    for i, source in enumerate((first, second)):
        place = pl.ds(pl.multiple_of((2 * core + i) * width, width), width)
        loads.append(pltpu.make_async_copy(source.at[pl.ds(count, count)], left.at[i], sems.at[2 * i]))
        part = weight.at[:, place] if nt else weight.at[place, :]
        loads.append(pltpu.make_async_copy(part, held.at[i], sems.at[2 * i + 1]))
    for load in loads:
        load.start()
    dims = NT if nt else NN
    loads[0].wait()
    loads[1].wait()
    total = dot(left[0], held[0], dims)
    loads[2].wait()
    loads[3].wait()
    out[...] = (total + dot(left[1], held[1], dims)).astype(BF)


def lend(nt, meta, first, second, weight):
    both, width = first.shape
    return pl.pallas_call(
        functools.partial(lend_kernel, nt),
        out_shape=jax.ShapeDtypeStruct((both // 2, width), BF),
        grid_spec=pltpu.PrefetchScalarGridSpec(
            num_scalar_prefetch=1,
            grid=(1,),
            in_specs=[HBM] * 3,
            out_specs=pl.BlockSpec((both // 2, width), lambda i, *_: (0, 0)),
            scratch_shapes=[
                pltpu.VMEM((2, both // 2, width), BF),
                pltpu.VMEM((2, width, width), BF),
                pltpu.SemaphoreType.DMA((4,)),
            ],
        ),
        compiler_params=params(),
        cost_estimate=cost(2 * both * width * width, 6e6),
        name="lend",
    )(meta, first, second, weight)


def layer_norm_back(values, gain, grad):
    normed, scale = normalized(values)
    t = grad * gain
    return scale * (t - jnp.mean(t, axis=-1, keepdims=True) - normed * jnp.mean(t * normed, axis=-1, keepdims=True))


def turn_kernel(
    counts, live, meta, first, second, weight, got, hidden, cotangent, attended, gain, w_proj,
    grad_branch, grad_attended, delta, left, held, got_v, hidden_v, cot_v, att_v, proj_v, sems,
):
    slots, rows, width = grad_branch.shape
    count = slots * rows
    core = meta[1]
    loads = []
    for i, source in enumerate((first, second)):
        place = pl.ds(pl.multiple_of((2 * core + i) * width, width), width)
        loads.append(pltpu.make_async_copy(source.at[pl.ds(0, count)], left.at[i], sems.at[2 * i]))
        loads.append(pltpu.make_async_copy(weight.at[:, place], held.at[i], sems.at[2 * i + 1]))
    for i, (source, target) in enumerate(
        ((got, got_v), (hidden, hidden_v), (cotangent, cot_v), (w_proj, proj_v), (attended, att_v))
    ):
        loads.append(pltpu.make_async_copy(source, target, sems.at[4 + i]))
    for load in loads:
        load.start()
    loads[0].wait()
    loads[1].wait()
    total = dot(left[0], held[0], NT)
    loads[2].wait()
    loads[3].wait()
    total = total + dot(left[1], held[1], NT)
    for load in loads[4:]:
        load.wait()
    head = lax.broadcasted_iota(jnp.int32, (32, width), 0)
    column = lax.broadcasted_iota(jnp.int32, (32, width), 1) // HEAD_DIM
    per = GROUP // HEAD_DIM
    pick = (head == (column // per) * 8 + column % per).astype(BF)
    for s in range(slots):
        here = slice(s * rows, (s + 1) * rows)
        mask = row_mask(counts, live, meta, s, rows)
        grad_out = jnp.where(mask, cot_v[s].astype(F32), 0.0)
        given = total[here] + got_v[here, :].astype(F32)
        branch = (grad_out + layer_norm_back(hidden_v[s], gain[...], given)).astype(BF)
        grad_branch[s] = branch
        back = dot(branch, proj_v[...], NT).astype(BF)
        grad_attended[s] = back
        product = back.astype(F32) * att_v[s].astype(F32)
        high = product.astype(BF)
        low = (product - high.astype(F32)).astype(BF)
        sums = dot(pick, high, NT) + dot(pick, low, NT)
        for g in range(width // GROUP):
            delta[s, g] = sums[8 * g:8 * g + 8]


def turn(counts, live, meta, first, second, weight, got, hidden, cotangent, attended, gain, w_proj):
    slots, rows, width = hidden.shape
    count = slots * rows
    groups = width // GROUP
    whole = pl.BlockSpec(hidden.shape, lambda i, *_: (0, 0, 0))
    return pl.pallas_call(
        turn_kernel,
        out_shape=[
            jax.ShapeDtypeStruct(hidden.shape, BF),
            jax.ShapeDtypeStruct(hidden.shape, BF),
            jax.ShapeDtypeStruct((slots, groups, 8, rows), F32),
        ],
        grid_spec=pltpu.PrefetchScalarGridSpec(
            num_scalar_prefetch=3,
            grid=(1,),
            in_specs=[HBM] * 7 + [pl.BlockSpec((1, width), lambda i, *_: (0, 0)), HBM],
            out_specs=[whole, whole, pl.BlockSpec((slots, groups, 8, rows), lambda i, *_: (0, 0, 0, 0))],
            scratch_shapes=[
                pltpu.VMEM((2, count, width), BF),
                pltpu.VMEM((2, width, width), BF),
                pltpu.VMEM((count, width), BF),
                pltpu.VMEM(hidden.shape, F32),
                pltpu.VMEM(hidden.shape, BF),
                pltpu.VMEM(hidden.shape, BF),
                pltpu.VMEM((width, width), BF),
                pltpu.SemaphoreType.DMA((9,)),
            ],
        ),
        compiler_params=params(),
        cost_estimate=cost(3 * 2 * slots * rows * width * width, 1.5e7),
        name="turn",
    )(counts, live, meta, first, second, weight, got, hidden, cotangent, attended, gain, w_proj)


def finish_kernel(counts, live, meta, first, second, weight, got, hidden, output, left, held, got_v, hidden_v, sems):
    slots, rows, width = output.shape
    count = slots * rows
    core = meta[1]
    loads = []
    for i, source in enumerate((first, second)):
        place = pl.ds(pl.multiple_of((2 * core + i) * width, width), width)
        loads.append(pltpu.make_async_copy(source.at[pl.ds(0, count)], left.at[i], sems.at[2 * i]))
        loads.append(pltpu.make_async_copy(weight.at[place, :], held.at[i], sems.at[2 * i + 1]))
    loads.append(pltpu.make_async_copy(got, got_v, sems.at[4]))
    loads.append(pltpu.make_async_copy(hidden, hidden_v, sems.at[5]))
    for load in loads:
        load.start()
    loads[0].wait()
    loads[1].wait()
    total = dot(left[0], held[0])
    loads[2].wait()
    loads[3].wait()
    total = total + dot(left[1], held[1])
    loads[4].wait()
    loads[5].wait()
    for s in range(slots):
        here = slice(s * rows, (s + 1) * rows)
        mask = row_mask(counts, live, meta, s, rows)
        output[s] = jnp.where(mask, total[here] + got_v[here, :].astype(F32) + hidden_v[s], 0.0).astype(BF)


def finish(counts, live, meta, first, second, weight, got, hidden):
    slots, rows, width = hidden.shape
    count = slots * rows
    return pl.pallas_call(
        finish_kernel,
        out_shape=jax.ShapeDtypeStruct(hidden.shape, BF),
        grid_spec=pltpu.PrefetchScalarGridSpec(
            num_scalar_prefetch=3,
            grid=(1,),
            in_specs=[HBM] * 5,
            out_specs=pl.BlockSpec(hidden.shape, lambda i, *_: (0, 0, 0)),
            scratch_shapes=[
                pltpu.VMEM((2, count, width), BF),
                pltpu.VMEM((2, width, width), BF),
                pltpu.VMEM((count, width), BF),
                pltpu.VMEM(hidden.shape, F32),
                pltpu.SemaphoreType.DMA((6,)),
            ],
        ),
        compiler_params=params(),
        cost_estimate=cost(2 * 2 * slots * rows * width * width, 9e6),
        name="finish",
    )(counts, live, meta, first, second, weight, got, hidden)


def gather_kernel(mine, got, w_kv, *refs):
    key_own, value_own, key_other, value_other, partial = refs[-5:]
    width = partial.shape[-1]
    parts = []
    for place, out in ((0, (key_own, value_own)), (1, (key_other, value_other))):
        for i in range(2):
            total = (mine[0, place, i].astype(F32) + got[0, place, i].astype(F32)).astype(BF)
            out[i][0] = total
            parts.append(total)
    partial[0] = (dot(parts[2], w_kv[:, :width], NT) + dot(parts[3], w_kv[:, width:], NT)).astype(BF)


def gather(slot, slots, mine, got, w_qkv, before):
    _, _, _, rows, width = mine.shape
    row_spec = pl.BlockSpec((1, rows, width), lambda i: (slot, 0, 0))
    kv_spec = pl.BlockSpec((1, 2, 2, rows, width), lambda i: (0, 0, 0, 0, 0))
    return pl.pallas_call(
        gather_kernel,
        out_shape=[jax.ShapeDtypeStruct((slots, rows, width), BF)] * 4 + [jax.ShapeDtypeStruct((1, rows, width), BF)],
        grid=(1,),
        in_specs=[kv_spec, kv_spec, pl.BlockSpec((pl.Element(width), pl.Element(2 * width)), lambda s: (0, width))]
        + [pl.BlockSpec(memory_space=pl.ANY)] * len(before),
        out_specs=[row_spec] * 4 + [pl.BlockSpec((1, rows, width), lambda i: (0, 0, 0))],
        input_output_aliases={3 + i: i for i in range(len(before))},
        compiler_params=params(),
        cost_estimate=cost(2 * 2 * rows * width * width, 6e6),
        name="gather",
    )(mine, got, w_qkv, *before)


VALUE_UNITS = ((0, 4, 1, 0, 0), (1, 6, 0, 1, 0), (7, 8, 1, 1, 1))
QUERY_UNITS = ((0, 2, 1, 1, 0), (0, 3, 1, 0, 1), (1, 5, 0, 1, 1))


def weigh_steps(units):
    seen = set()
    steps = []
    for step in units:
        steps.append(step + (int(step[0] not in seen),))
        seen.add(step[0])
    return jnp.array(steps, jnp.int32)


def weigh_kernel(meta, steps, *refs):
    sources, (grads, held, total, sems) = refs[:9], refs[9:]
    step = pl.program_id(0)
    size = held.shape[1] // CHUNKS
    values = steps[0, 1] == VALUE_UNITS[0][1]

    def start(units):
        seen = []
        for unit in units:
            for i in unit[:2]:
                if i not in seen:
                    seen.append(i)
                    pltpu.make_async_copy(sources[i], held.at[i], sems.at[i]).start()

    @pl.when(jnp.logical_and(step == 0, values))
    def _():
        start(VALUE_UNITS)

    @pl.when(jnp.logical_and(step == 0, jnp.logical_not(values)))
    def _():
        start(QUERY_UNITS)

    left = steps[step, 0]
    right = steps[step, 1]

    @pl.when(steps[step, 5] == 1)
    def _():
        pltpu.make_async_copy(sources[0], held.at[left], sems.at[left]).wait()

    pltpu.make_async_copy(sources[0], held.at[right], sems.at[right]).wait()

    @pl.when(steps[step, 2] == 1)
    def _():
        total[...] = dot(held[left], held[right], TN)

    @pl.when(steps[step, 2] != 1)
    def _():
        total[...] += dot(held[left], held[right], TN)

    @pl.when(steps[step, 3] == 1)
    def _():
        unit = steps[step, 4]
        me = meta[4 + unit]
        for a in range(CHUNKS):
            grads[unit, a ^ me] = total[a * size:(a + 1) * size, :].astype(BF)


def weigh(meta, steps, arrays):
    arrays = [a.reshape(-1, a.shape[-1]) for a in arrays]
    rows, width = arrays[0].shape
    shape = (2, CHUNKS, width // CHUNKS, width)
    return pl.pallas_call(
        weigh_kernel,
        out_shape=jax.ShapeDtypeStruct(shape, BF),
        grid_spec=pltpu.PrefetchScalarGridSpec(
            num_scalar_prefetch=2,
            grid=(3,),
            in_specs=[HBM] * 9,
            out_specs=pl.BlockSpec(shape, lambda i, *_: (0, 0, 0, 0)),
            scratch_shapes=[
                pltpu.VMEM((9, rows, width), BF),
                pltpu.VMEM((rows, width), F32),
                pltpu.SemaphoreType.DMA((9,)),
            ],
        ),
        compiler_params=params(),
        cost_estimate=cost(3 * 2 * rows * width * width, 1e7),
        name="weigh",
    )(meta, steps, *arrays)


def close_kernel(gq, gk, gv, w_qkv, partial, tokens, grad_hidden, gain, out, total):
    step = pl.program_id(0)
    slots, rows, width = gq.shape
    flat = (slots * rows, width)

    @pl.when(step == 0)
    def _():
        total[...] = dot(gq[...].reshape(flat), w_qkv[...], NT)

    @pl.when(step == 1)
    def _():
        total[...] += dot(gk[...].reshape(flat), w_qkv[...], NT)

    @pl.when(step == 2)
    def _():
        total[...] += dot(gv[...].reshape(flat), w_qkv[...], NT)

    @pl.when(step > 2)
    def _():
        first = total[pl.ds(pl.multiple_of((step - 3) * rows, rows), rows), :] + partial[0].astype(F32)
        out[0] = (grad_hidden[0].astype(F32) + layer_norm_back(tokens[0].astype(F32), gain[...], first)).astype(BF)


def close(gq, gk, gv, partials, tokens, grad_hidden, gain, w_qkv):
    slots, rows, width = tokens.shape
    row_spec = pl.BlockSpec((1, rows, width), lambda i: (jnp.maximum(i - 3, 0), 0, 0))
    whole = pl.BlockSpec((slots, rows, width), lambda i: (0, 0, 0))
    (partial,) = pack((partials, False))
    return pl.pallas_call(
        close_kernel,
        out_shape=jax.ShapeDtypeStruct(tokens.shape, BF),
        grid=(3 + slots,),
        in_specs=[whole] * 3 + [pl.BlockSpec((width, width), lambda i: (0, jnp.minimum(i, 2)))] + [row_spec] * 3 + [
            pl.BlockSpec((1, width), lambda i: (0, 0)),
        ],
        out_specs=row_spec,
        scratch_shapes=[pltpu.VMEM((slots * rows, width), F32)],
        compiler_params=params(),
        cost_estimate=cost(3 * 2 * slots * rows * width * width, 1.2e7),
        name="close",
    )(gq, gk, gv, w_qkv, partial, tokens, grad_hidden, gain)


SPREAD = 4


def keep_row_sums(held, value):
    step = pl.program_id(0)
    rows = value.shape[0]
    column = jnp.sum(value, axis=-1, keepdims=True)
    held[pl.ds(pl.multiple_of(step * rows, rows), rows), :] = jnp.broadcast_to(column, (rows, 128))


def put_row_sums(norm, held, gain):
    @pl.when(pl.program_id(0) == pl.num_programs(0) - 1)
    def _():
        for r in range(norm.shape[0]):
            norm[r:r + 1, :] = held[r * 128:(r + 1) * 128, :].T[:1] / gain[r:r + 1, :]


def load_pieces(sources, held, sems, tops):
    copies = []
    count = len(sources) // 4
    for i, top in enumerate(tops):
        pieces = sources[count * i:count * (i + 1)]
        for k, piece in enumerate(pieces):
            if len(pieces) == 4:
                copies.append(pltpu.make_async_copy(piece, held.at[i, k ^ top], sems.at[i, k]))
                continue
            for low in range(4 // len(pieces)):
                place = k * (4 // len(pieces)) + low
                copies.append(
                    pltpu.make_async_copy(piece.at[pl.ds(low * 4, 4)], held.at[i, place ^ top], sems.at[i, place])
                )
    for copy in copies:
        copy.start()
    for copy in copies:
        copy.wait()


def spread_mlp_kernel(meta, *refs):
    pieces, (w_fc1, gain, grad_fc1, grad_fc2, norm, chunks, held, sems) = refs[:-8], refs[-8:]
    step = pl.program_id(0)
    size, width = chunks.shape[-2:]
    mx, my, mz, mw = meta[3], meta[6], meta[7], meta[8]

    @pl.when(step == 0)
    def _():
        load_pieces(pieces, chunks, sems, [mx * 2 + my, my * 2 + mx] * 2)

    first = meta[1] == 0
    z, y = step // 2, step % 2
    for a in range(4):
        w, x = a // 2, a % 2
        low = (z ^ mz) * 2 + (w ^ mw)
        for half, top in ((0, x * 2 + y), (1, y * 2 + x)):
            for place, core in ((half, 0), (2 + half, 1)):
                own = jnp.where(first, core, 1 - core)
                value = chunks[2 * own + half, top, low].astype(F32)
                grad_fc1[a * size:(a + 1) * size, place * width:(place + 1) * width] = value[0]
                grad_fc2[place, a * size:(a + 1) * size, :] = value[1]
    keep_row_sums(held, grad_fc1[...] * w_fc1[...].astype(F32))
    put_row_sums(norm, held, gain)


def spread_mlp(meta, pieces, w_fc1, gain):
    width, hidden_width = w_fc1.shape
    per = CHUNKS // SPREAD
    size = width // CHUNKS
    outs = pl.pallas_call(
        spread_mlp_kernel,
        out_shape=[
            jax.ShapeDtypeStruct((width, hidden_width), F32),
            jax.ShapeDtypeStruct((4, width, width), F32),
            jax.ShapeDtypeStruct((width // 128, 128), F32),
        ],
        grid_spec=pltpu.PrefetchScalarGridSpec(
            num_scalar_prefetch=1,
            grid=(SPREAD,),
            in_specs=[HBM] * len(pieces) + [
                pl.BlockSpec((per * size, hidden_width), lambda a, *_: (a, 0)),
                pl.BlockSpec((width // 128, 128), lambda a, *_: (0, 0)),
            ],
            out_specs=[
                pl.BlockSpec((per * size, hidden_width), lambda a, *_: (a, 0)),
                pl.BlockSpec((4, per * size, width), lambda a, *_: (0, a, 0)),
                pl.BlockSpec((width // 128, 128), lambda a, *_: (0, 0)),
            ],
            scratch_shapes=[
                pltpu.VMEM((4, 4, 4) + pieces[0].shape[1:], BF),
                pltpu.VMEM((width, 128), F32),
                pltpu.SemaphoreType.DMA((4, 4)),
            ],
        ),
        compiler_params=params(),
        cost_estimate=cost(1e6, 4.7e7),
        name="spread_mlp",
    )(meta, *pieces, w_fc1, gain.reshape(width // 128, 128))
    return outs[0], outs[1].reshape(hidden_width, width), outs[2].reshape(width)


def spread_qkv_kernel(meta, *refs):
    pieces, (w_qkv, gain, grad_qkv, grad_proj, norm, chunks, held, sems) = refs[:-8], refs[-8:]
    step = pl.program_id(0)
    size, width = chunks.shape[-2:]
    mx, my, mz, mw = meta[3], meta[6], meta[7], meta[8]

    @pl.when(step == 0)
    def _():
        load_pieces(pieces, chunks, sems, [mx * 2 + my, my * 2 + mx] * 2)

    first = meta[1] == 0
    own = jnp.where(first, 0, 2)
    part = 2 - own
    for a in range(4):
        here = slice(a * size, (a + 1) * size)
        low = a ^ (mz * 2 + mw)
        for i, at in enumerate((own, own + 1, part)):
            grad_qkv[here, i * width:(i + 1) * width] = chunks[at, step, low].astype(F32)
        grad_proj[here, :] = chunks[part + 1, step, low].astype(F32)
    keep_row_sums(held, grad_qkv[...] * w_qkv[...].astype(F32))
    put_row_sums(norm, held, gain)


def spread_qkv(meta, pieces, w_qkv, gain):
    width = w_qkv.shape[0]
    size = width // CHUNKS
    per = CHUNKS // SPREAD

    def rows(columns):
        return pl.BlockSpec((per * size, columns), lambda a, *_: (a, 0))

    line = pl.BlockSpec((width // 128, 128), lambda a, *_: (0, 0))
    outs = pl.pallas_call(
        spread_qkv_kernel,
        out_shape=[
            jax.ShapeDtypeStruct((width, 3 * width), F32),
            jax.ShapeDtypeStruct((width, width), F32),
            jax.ShapeDtypeStruct((width // 128, 128), F32),
        ],
        grid_spec=pltpu.PrefetchScalarGridSpec(
            num_scalar_prefetch=1,
            grid=(SPREAD,),
            in_specs=[HBM] * len(pieces) + [rows(3 * width), line],
            out_specs=[rows(3 * width), rows(width), line],
            scratch_shapes=[
                pltpu.VMEM((4, 4, 4) + pieces[0].shape[1:], BF),
                pltpu.VMEM((width, 128), F32),
                pltpu.SemaphoreType.DMA((4, 4)),
            ],
        ),
        compiler_params=params(),
        cost_estimate=cost(1e6, 1.8e7),
        name="spread_qkv",
    )(meta, *pieces, w_qkv, gain.reshape(width // 128, 128))
    return outs[0], outs[1], outs[2].reshape(width)


DIGITS = {"x": (0, 2), "y": (1, 0), "z": (2, 0), "w": (4, 0)}


def swap(value, axis, mask):
    return lax.ppermute(value, axis, [(i, i ^ mask) for i in range(lax.axis_size(axis))])


def swap_digits(value, masks):
    batch, band = masks
    if not band:
        return swap(value, "batch", batch)
    if not batch:
        return swap(value, "band", band)
    return swap(value, ("batch", "band"), batch * lax.axis_size("band") + band)


def add(*values):
    total = values[0].astype(F32)
    for value in values[1:]:
        total = total + value.astype(F32)
    return total.astype(BF)


def pack_kernel(groups, *refs):
    total = sum(count for count, _ in groups)
    sources, refs = refs[:total], refs[total:]
    outs = sum(1 + split for _, split in groups)
    targets, refs = list(refs[:outs]), refs[outs:]
    held, (sems, out_sems) = refs[:len(groups)], refs[len(groups):]
    loads, stores = [], []
    for group, (count, split) in enumerate(groups):
        mine = [targets.pop(0) for _ in range(1 + split)]
        for i in range(count):
            at = len(loads)
            size = sources[at].shape[0]
            here = pl.ds(i * size, size)
            loads.append(pltpu.make_async_copy(sources[at], held[group].at[here], sems.at[at]))
            stores.append([
                pltpu.make_async_copy(
                    held[group].at[here, j] if split else held[group].at[here], target.at[here], out_sems.at[at, j]
                )
                for j, target in enumerate(mine)
            ])
    for load in loads:
        load.start()
    for load, store in zip(loads, stores):
        load.wait()
        for copy in store:
            copy.start()
    for store in stores:
        for copy in store:
            copy.wait()


def pack(*groups):
    shapes = [(len(parts) * parts[0].shape[0],) + parts[0].shape[1:] for parts, _ in groups]
    out = []
    for shape, (_, split) in zip(shapes, groups):
        out += [shape[:1] + shape[2:]] * 2 if split else [shape]
    parts = [p for group, _ in groups for p in group]
    return list(pl.pallas_call(
        functools.partial(pack_kernel, [(len(p), int(split)) for p, split in groups]),
        out_shape=[jax.ShapeDtypeStruct(o, BF) for o in out],
        in_specs=[HBM] * len(parts),
        out_specs=[HBM] * len(out),
        scratch_shapes=[pltpu.VMEM(shape, BF) for shape in shapes]
        + [pltpu.SemaphoreType.DMA((len(parts),)), pltpu.SemaphoreType.DMA((len(parts), 2))],
        compiler_params=params(),
        cost_estimate=cost(0, 2e6),
        name="pack",
    )(*parts))


class Line:
    def __init__(self):
        self.mark = None

    def tie(self, value):
        if self.mark is None:
            return value
        value, self.mark = lax.optimization_barrier((value, self.mark))
        return value


class Chain:
    def __init__(self, terms=(), halves=(), upper=None, pieces=(), joins=()):
        self.terms = list(terms)
        self.upper = upper
        self.pieces = list(pieces)
        self.steps = [("part", group) for group in halves] + [("join", group) for group in joins]

    def masks(self, group):
        count = 1 << len(group)
        masks = []
        for place in range(1, count):
            digits = [DIGITS[d] for i, d in enumerate(group) if place & (count >> (i + 1))]
            masks.append((sum(d[0] for d in digits), sum(d[1] for d in digits)))
        return masks

    def total_here(self):
        return add(*self.terms)

    def total(self):
        value = add(*self.terms)
        mask = 8
        while mask < lax.axis_size("batch"):
            value = add(value, swap(value, "batch", mask))
            mask *= 2
        return value

    def offers(self):
        kind, what = self.steps[0]
        if kind == "join":
            return self.pieces
        if self.upper is not None:
            sent, self.upper = [self.upper], None
            return sent
        count = 1 << len(what)
        size = self.terms[0].shape[0] // count
        sent = [add(*[t[i * size:(i + 1) * size] for t in self.terms]) for i in range(1, count)]
        self.terms = [t[:size] for t in self.terms]
        return sent

    def start(self, sent):
        kind, what = self.steps[0]
        masks = self.masks(what)
        if kind == "join":
            return [swap_digits(s, mask) for mask in masks for s in sent]
        return [swap_digits(s, mask) for s, mask in zip(sent, masks)]

    def take(self, moved):
        kind, _ = self.steps.pop(0)
        if kind == "join":
            self.pieces = self.pieces + list(moved)
        else:
            self.terms = self.terms + list(moved)


class Flight:
    def __init__(self, line):
        self.line = line
        self.parts = {}

    def land(self, *names):
        names = [n for n in (names or tuple(self.parts)) if n in self.parts]
        if not names:
            return {}
        held = [self.parts.pop(n) for n in names]
        got = self.line.tie(held)
        self.line.mark = got
        for name, moved in zip(names, got):
            if isinstance(name, Chain):
                name.take(moved)
        return {n: g for n, g in zip(names, got) if not isinstance(n, Chain)}

    def launch(self, *items):
        items = [i for i in items if not isinstance(i, Chain) or i.steps]
        arrays = [i.offers() if isinstance(i, Chain) else list(i[1]) for i in items]
        arrays = self.line.tie(arrays)
        self.line.mark = arrays
        for item, sent in zip(items, arrays):
            if isinstance(item, Chain):
                self.parts[item] = item.start(sent)
            else:
                name, _, axis, mask = item
                self.parts[name] = [swap(a, axis, mask) for a in sent]


def place_in(order):
    place = 0
    for digit in "".join(order):
        batch, band = DIGITS[digit]
        bit = lax.axis_index("batch") // batch if batch else lax.axis_index("band") // band
        place = place * 2 + bit % 2
    return place


ORDER = ("z", "y", "wx")
LAST_ORDERS = (("x", "y"), ("y", "x"))


def body(
    tokens, w_qkv, w_proj, w_fc1, w_fc2, gain_one, gain_two, cotangent, band_counts, slot_live
):
    slots, rows, width = tokens.shape
    flat = (slots * rows, width)
    band = lax.axis_index("band")
    core = band % 2
    meta = jnp.stack(
        [band, core] + [place_in(o) for o in (ORDER, "x") + tuple(order + ("zw",) for order in LAST_ORDERS) + ("y", "z", "w")]
    ).astype(jnp.int32)
    gain_one = gain_one[None]
    gain_two = gain_two[None]
    at = (band_counts, slot_live, meta)
    line = Line()

    tokens, *tokens_other = lax.optimization_barrier(
        (tokens,) + tuple(tokens[s:s + 1] for s in range(slots))
    )
    tokens_other = [swap(t, "band", 2) for t in tokens_other]
    cotangent_p = swap(cotangent, "band", 1)
    first_own, query, kv_own = project(tokens, w_qkv, gain_one)
    tables = weigh_steps(QUERY_UNITS), weigh_steps(VALUE_UNITS)
    steps_theirs = jnp.where(core == 1, *tables)
    steps_ours = jnp.where(core == 0, *tables)
    line.mark = (first_own, meta, gain_two, steps_theirs, steps_ours)
    first_other, pairs = [], []
    seconds, seconds_p = [], []
    kept = ()

    def take(s):
        first, pair = project_other(s, line.tie(tokens_other[s]), kv_own, w_qkv, gain_one, first_other)
        line.mark = pair
        first_other[:] = [first]
        pairs.append((pair, swap(pair, "band", 1)))

    def look(s):
        *out, second = attend(s, *at, line.tie(query), *pairs[s], tokens, w_proj, gain_two, kept)
        line.mark = second
        seconds.append(second)
        seconds_p.append(swap(second, "band", 1))
        return tuple(out)

    take(0)
    for s in range(slots):
        if s == 1:
            for n in range(1, slots):
                take(n)
            cotangent_p = line.tie(cotangent_p)
        kept = look(s)
    attended, lse, hidden = kept

    flight = Flight(line)
    chains = []
    acts, pres = [], []
    all_seconds = seconds + seconds_p
    for half in range(2):
        act, pre, lower, upper = mlp(
            *at, [line.tie(all_seconds[0])] + all_seconds[1:], cotangent, cotangent_p, w_fc1, w_fc2, half
        )
        line.mark = upper
        acts.append(act)
        pres.append(pre)
        chains.append(Chain((lower,), ORDER, upper))
        if half == 0:
            flight.launch(chains[0])
    one, two = chains
    turn_part = lend(True, meta, line.tie(pres[0]), pres[1], w_fc1)
    line.mark = turn_part
    finish_part = lend(False, meta, line.tie(acts[0]), acts[1], w_fc2)
    line.mark = finish_part
    flight.land()
    flight.launch(("turn", [turn_part], "band", 1), two, one, ("finish", [finish_part], "band", 1))
    got = flight.land("turn")
    branch, grad_attended, delta = turn(
        *at, line.tie(pres[0]), pres[1], w_fc1, got["turn"][0], hidden, cotangent, attended, gain_two, w_proj
    )
    line.mark = delta

    grad_query, sums, keeps, waiting = (), (), [], []

    def bring(s):
        *kept_sums, partial = gather(s, slots, line.tie(keeps[s]), got[f"send{s}"][0], w_qkv, sums)
        line.mark = partial
        return tuple(kept_sums), [(f"partial{s}", [partial], "band", 2)]

    for s in range(slots):
        query_grad, keep, send = attend_back(
            s, *at, line.tie(query), *pairs[s], grad_attended, lse, delta, grad_query
        )
        line.mark = send
        grad_query = (query_grad,)
        keeps.append(keep)
        got.update(flight.land())
        if s < slots - 1:
            flight.launch((f"send{s}", [send], "band", 1), *waiting, two, one)
            waiting = []
            if s > 0:
                sums, waiting = bring(s - 1)
    assert not one.steps and not two.steps
    both = Chain(pieces=[jnp.stack([one.total(), two.total()], axis=1)], joins=("w", "z"))
    flight.launch((f"send{slots - 1}", [send], "band", 1), *waiting, both)
    waiting = []
    if slots > 1:
        sums, waiting = bring(slots - 2)
    got.update(flight.land(f"send{slots - 1}"))
    sums, last = bring(slots - 1)
    waiting += last
    got.update(flight.land())
    both.pieces = pack((both.pieces, False))
    flight.launch(*waiting, both)
    arrays = (first_own, first_other[0], grad_query[0], *sums, attended, branch)
    theirs = weigh(meta, steps_theirs, (line.tie(first_own),) + arrays[1:])
    line.mark = theirs
    got.update(flight.land())
    halves = pack((both.pieces, True))
    one = Chain(pieces=halves[:1], joins=("y", "x"))
    two = Chain(pieces=halves[1:], joins=("x", "y"))
    flight.launch(("theirs", [theirs], "band", 1), one, two)
    ours = weigh(meta, steps_ours, (line.tie(first_own),) + arrays[1:])
    line.mark = ours
    got.update(flight.land("theirs"))
    (theirs,) = got["theirs"]
    three = Chain((ours[0], theirs[0]), LAST_ORDERS[0])
    four = Chain((ours[1], theirs[1]), LAST_ORDERS[1])
    flight.launch(three, four)
    output = finish(*at, line.tie(acts[0]), acts[1], w_fc2, got["finish"][0], hidden)
    line.mark = output
    flight.land(one, two)
    flight.land(three, four)
    flight.launch(three, four)
    first, second = pack((one.pieces, False), (two.pieces, False))
    one.pieces, two.pieces = [line.tie(first)], [second]
    flight.land(three, four)
    five = Chain((jnp.stack([three.total_here(), four.total_here()], axis=1),), ("zw",))
    flight.launch(five, one, two)
    flight.land(five)
    five = Chain(pieces=[five.total()], joins=("zw",))
    flight.launch(five)
    flight.land(one, two)
    flight.land(five)
    *halves, first, second = pack((five.pieces, True), (one.pieces, False), (two.pieces, False))
    three = Chain(pieces=halves[:1], joins=("y", "x"))
    four = Chain(pieces=halves[1:], joins=("x", "y"))
    flight.launch(three, four, ("mlp", [first, second], "band", 1))
    partials = [got[f"partial{s}"][0] for s in range(slots)]
    grad_input = close(
        line.tie(grad_query[0]), sums[0], sums[1], partials, tokens, branch, gain_one, w_qkv
    )
    line.mark = grad_input
    got.update(flight.land())
    held = pack((three.pieces, False), (four.pieces, False))
    three.pieces, four.pieces = held[:1], held[1:]
    flight.launch(three, four, ("held", held, "band", 1))
    grad_fc1, grad_fc2, norm2 = spread_mlp(meta, [line.tie(first), second, *got["mlp"]], w_fc1, gain_two)
    line.mark = norm2
    got.update(flight.land())
    flight.launch(("rest", [three.pieces[1], four.pieces[1]], "band", 1))
    got.update(flight.land())
    last_pieces = three.pieces + four.pieces + [p for pair in zip(got["held"], got["rest"]) for p in pair]
    grad_qkv, grad_proj, norm1 = spread_qkv(meta, last_pieces, w_qkv, gain_one)
    return (output, grad_input, grad_qkv, grad_proj, grad_fc1, grad_fc2, norm1, norm2)


def solution(mesh):
    placed = (
        P("batch", "band", None),
        P(),
        P(),
        P(),
        P(),
        P(),
        P(),
        P("batch", "band", None),
        P("batch", None),
        P("batch"),
    )
    return jax.shard_map(
        body,
        mesh=mesh,
        in_specs=placed,
        out_specs=(
            P("batch", "band", None),
            P("batch", "band", None),
            P(),
            P(),
            P(),
            P(),
            P(),
            P(),
        ),
        check_vma=False,
    )
```

```python
import functools
import jax
import jax.numpy as jnp
from jax import lax
from jax.experimental import pallas as pl
from jax.experimental.pallas import tpu as pltpu
from jax.sharding import PartitionSpec as P

BF = jnp.bfloat16
F32 = jnp.float32
EPSILON = 1e-06
HEAD_DIM = 64
GROUP = 256
NN = (((1,), (0,)), ((), ()))
NT = (((1,), (1,)), ((), ()))
TN = (((0,), (0,)), ((), ()))


def dot(left, right, dims=NN):
    return lax.dot_general(left, right, dims, preferred_element_type=F32)


def params(mib=60):
    return pltpu.CompilerParams(vmem_limit_bytes=mib * 1024 * 1024)


def cost(flops, moved, exps=0):
    return pl.CostEstimate(flops=1, bytes_accessed=1, transcendentals=0)


HBM = pl.BlockSpec(memory_space=pl.ANY)
STAY = pl.BlockSpec(memory_space=pltpu.HBM)


def normalized(values):
    centered = values - jnp.mean(values, axis=-1, keepdims=True)
    spread = jnp.mean(centered * centered, axis=-1, keepdims=True)
    scale = lax.rsqrt(spread + EPSILON)
    return centered * scale, scale


def project_kernel(tokens, weight, gain, first_in, query, both):
    normed, _ = normalized(tokens[0].astype(F32))
    first = (normed * gain[...]).astype(BF)
    first_in[0] = first
    width = first.shape[1]
    query[0] = (dot(first, weight[:, :width]) * HEAD_DIM ** -0.5).astype(BF)
    both[0, 0] = dot(first, weight[:, width:2 * width]).astype(BF)
    both[0, 1] = dot(first, weight[:, 2 * width:]).astype(BF)


def project(tokens, w_qkv, gain):
    slots, rows, width = tokens.shape
    row_spec = pl.BlockSpec((1, rows, width), lambda s: (s, 0, 0))
    return pl.pallas_call(
        project_kernel,
        out_shape=[
            jax.ShapeDtypeStruct(tokens.shape, BF),
            jax.ShapeDtypeStruct(tokens.shape, BF),
            jax.ShapeDtypeStruct((slots, 2, rows, width), BF),
        ],
        grid=(slots,),
        in_specs=[
            row_spec,
            pl.BlockSpec((width, 3 * width), lambda s: (0, 0)),
            pl.BlockSpec((1, width), lambda s: (0, 0)),
        ],
        out_specs=[row_spec, row_spec, pl.BlockSpec((1, 2, rows, width), lambda s: (s, 0, 0, 0))],
        compiler_params=params(14),
        cost_estimate=cost(2 * slots * rows * width * width * 3, 8e6),
        name="project",
    )(tokens, w_qkv, gain)


def project_other_kernel(tokens, own, weight, gain, *refs):
    first_in, both = refs[-2:]
    normed, _ = normalized(tokens[0].astype(F32))
    first = (normed * gain[...]).astype(BF)
    first_in[0] = first
    width = first.shape[1]
    both[0] = own[0]
    both[1, 0] = dot(first, weight[:, :width]).astype(BF)
    both[1, 1] = dot(first, weight[:, width:]).astype(BF)


def project_other(slot, tokens, kv_own, w_qkv, gain, before):
    slots, _, rows, width = kv_own.shape
    return pl.pallas_call(
        project_other_kernel,
        out_shape=[
            jax.ShapeDtypeStruct((slots, rows, width), BF),
            jax.ShapeDtypeStruct((2, 2, rows, width), BF),
        ],
        grid=(1,),
        in_specs=[
            pl.BlockSpec((1, rows, width), lambda i: (0, 0, 0)),
            pl.BlockSpec((1, 2, rows, width), lambda i: (slot, 0, 0, 0)),
            pl.BlockSpec((pl.Element(width), pl.Element(2 * width)), lambda i: (0, width)),
            pl.BlockSpec((1, width), lambda i: (0, 0)),
        ] + [HBM] * len(before),
        out_specs=[
            pl.BlockSpec((1, rows, width), lambda i: (slot, 0, 0)),
            pl.BlockSpec((2, 2, rows, width), lambda i: (0, 0, 0, 0)),
        ],
        input_output_aliases={4 + i: i for i in range(len(before))},
        compiler_params=params(10),
        cost_estimate=cost(2 * rows * width * width * 2, 5e6),
        name="project_other",
    )(tokens, kv_own, w_qkv, gain, *before)


def key_masks(counts, live, meta, slot, rows, flips, axis):
    shape = (rows, 1) if axis == 0 else (1, rows)
    place = lax.broadcasted_iota(jnp.int32, shape, axis)
    alive = live[slot] > 0
    return [place < jnp.where(alive, counts[slot, meta[0] ^ flip], 0) for flip in flips]


FLIPS = (0, 2, 1, 3)


def attend_kernel(slot, counts, live, meta, query, pair, pair_p, tokens, w_proj, gain, *refs):
    attended, lse, hidden, second, held, own_tokens, weight, sems = refs[-8:]
    group = pl.program_id(0)
    rows = query.shape[1]
    copies = (
        pltpu.make_async_copy(tokens.at[slot], own_tokens, sems.at[0]),
        pltpu.make_async_copy(w_proj, weight, sems.at[1]),
    )

    @pl.when(group == 0)
    def _():
        for copy in copies:
            copy.start()

    masks = key_masks(counts, live, meta, slot, rows, FLIPS, 1)
    q = query[0]
    lane = lax.broadcasted_iota(jnp.int32, (1, GROUP), 1)
    result = jnp.zeros((rows, GROUP), F32)
    sums = jnp.zeros((rows, 128), F32)
    lane128 = lax.broadcasted_iota(jnp.int32, (1, 128), 1)
    blocks = (pair.at[0], pair.at[1], pair_p.at[0], pair_p.at[1])
    for h in range(GROUP // HEAD_DIM):
        here = (lane // HEAD_DIM) == h
        qm = jnp.where(here, q, jnp.zeros_like(q))
        scores = [
            jnp.where(mask, dot(qm, block[0], NT), -10000.0) for mask, block in zip(masks, blocks)
        ]
        top = scores[0]
        for s in scores[1:]:
            top = jnp.maximum(top, s)
        top = jnp.max(top, axis=-1, keepdims=True)
        out = jnp.zeros((rows, GROUP), F32)
        exps = [jnp.exp(s - top) for s in scores]
        total = exps[0]
        for e in exps[1:]:
            total = total + e
        total = jnp.sum(total, axis=-1, keepdims=True)
        for e, block in zip(exps, blocks):
            out = out + dot(e.astype(BF), block[1])
        result = jnp.where(here, out * (1.0 / total), result)
        sums = jnp.where(lane128 == h, top + jnp.log(total), sums)
    low = result.astype(BF)
    attended[0] = low
    held[group] = low
    lse[0, 0] = sums.T[:8]

    @pl.when(group == pl.num_programs(0) - 1)
    def _():
        for copy in copies:
            copy.wait()
        value = own_tokens[...].astype(F32)
        for g in range(held.shape[0]):
            value = value + dot(held[g], weight[g * GROUP:(g + 1) * GROUP, :])
        hidden[0] = value
        normed, _ = normalized(value)
        second[...] = (normed * gain[...]).astype(BF)


def attend(slot, counts, live, meta, query, pair, pair_p, tokens, w_proj, gain, before):
    slots, rows, width = query.shape
    groups = width // GROUP
    at = slot
    kv_spec = pl.BlockSpec((2, 2, rows, GROUP), lambda g, *_: (0, 0, 0, g))
    piece = pl.BlockSpec((1, rows, GROUP), lambda g, *_: (at, 0, g))
    row_spec = pl.BlockSpec((1, rows, width), lambda g, *_: (at, 0, 0))
    operands = (counts, live, meta, query, pair, pair_p, tokens, w_proj, gain)
    return pl.pallas_call(
        functools.partial(attend_kernel, slot),
        out_shape=[
            jax.ShapeDtypeStruct(query.shape, BF),
            jax.ShapeDtypeStruct((slots, groups, 8, rows), F32),
            jax.ShapeDtypeStruct(query.shape, F32),
            jax.ShapeDtypeStruct((rows, width), BF),
        ],
        grid_spec=pltpu.PrefetchScalarGridSpec(
            num_scalar_prefetch=3,
            grid=(groups,),
            in_specs=[piece, kv_spec, kv_spec, HBM, HBM, pl.BlockSpec((1, width), lambda g, *_: (0, 0))]
            + [HBM] * len(before),
            out_specs=[
                piece,
                pl.BlockSpec((1, 1, 8, rows), lambda g, *_: (at, g, 0, 0)),
                row_spec,
                pl.BlockSpec((rows, width), lambda g, *_: (0, 0)),
            ],
            scratch_shapes=[
                pltpu.VMEM((groups, rows, GROUP), BF),
                pltpu.VMEM((rows, width), BF),
                pltpu.VMEM((width, width), BF),
                pltpu.SemaphoreType.DMA((2,)),
            ],
        ),
        input_output_aliases={len(operands) + i: i for i in range(len(before))},
        compiler_params=params(14),
        cost_estimate=cost(2 * 2 * rows * 4 * rows * 4 * width, 1e7, 12 * rows * 4 * rows),
        name="attend",
    )(*operands, *before)


def attend_back_kernel(
    slot, counts, live, meta, query, pair, pair_p, grad, lse, delta, *refs
):
    grad_query, grad_keep, grad_send, probs, slopes, qms, gms, keys, values, keys_t = refs[-10:]
    rows = query.shape[1]
    heads = GROUP // HEAD_DIM
    masks = key_masks(counts, live, meta, slot, rows, FLIPS, 0)
    q = query[0]
    ga = grad[0]
    lane = lax.broadcasted_iota(jnp.int32, (1, GROUP), 1)
    zero = jnp.zeros_like(q)
    for h in range(heads):
        here = (lane // HEAD_DIM) == h
        qms[h * rows:(h + 1) * rows, :] = jnp.where(here, q, zero)
        gms[h * rows:(h + 1) * rows, :] = jnp.where(here, ga, zero)
    for i, mask in enumerate(masks):
        block = (pair, pair_p)[i // 2]
        keys[i * rows:(i + 1) * rows, :] = jnp.where(mask, block[i % 2, 0], zero)
        values[i * rows:(i + 1) * rows, :] = block[i % 2, 1]
    keys_t[...] = keys[...].T
    gq = []
    for h in range(heads):
        mine = slice(h * rows, (h + 1) * rows)
        for i, mask in enumerate(masks):
            at = slice(i * rows, (i + 1) * rows)
            scores = jnp.where(mask, dot(keys[at, :], qms[mine, :], NT), -10000.0)
            gp = dot(values[at, :], gms[mine, :], NT)
            p = jnp.exp(scores - lse[0, 0, h:h + 1, :])
            probs[at, mine] = p.astype(BF)
            slopes[at, mine] = (p * (gp - delta[0, 0, h:h + 1, :])).astype(BF)
        gq.append(dot(keys_t[h * HEAD_DIM:(h + 1) * HEAD_DIM, :], slopes[:, mine]))
    gk = dot(slopes[...], qms[...])
    gv = dot(probs[...], gms[...])
    outs = ((grad_keep, 0), (grad_keep, 1), (grad_send, 0), (grad_send, 1))
    for i, ((out, place), mask) in enumerate(zip(outs, masks)):
        at = slice(i * rows, (i + 1) * rows)
        out[0, place, 0] = jnp.where(mask, gk[at], 0.0).astype(BF)
        out[0, place, 1] = gv[at].astype(BF)
    grad_query[0] = (jnp.concatenate(gq, axis=0).T * HEAD_DIM ** -0.5).astype(BF)


def attend_back(slot, counts, live, meta, query, pair, pair_p, grad, lse, delta, before):
    slots, rows, width = query.shape
    groups = width // GROUP
    heads = GROUP // HEAD_DIM
    at = slot
    kv_spec = pl.BlockSpec((2, 2, rows, GROUP), lambda g, *_: (0, 0, 0, g))
    row_spec = pl.BlockSpec((1, rows, GROUP), lambda g, *_: (at, 0, g))
    stat_spec = pl.BlockSpec((1, 1, 8, rows), lambda g, *_: (at, g, 0, 0))
    out_spec = pl.BlockSpec((1, 2, 2, rows, GROUP), lambda g, *_: (0, 0, 0, 0, g))
    operands = (counts, live, meta, query, pair, pair_p, grad, lse, delta)
    return pl.pallas_call(
        functools.partial(attend_back_kernel, slot),
        out_shape=[
            jax.ShapeDtypeStruct(query.shape, BF),
            jax.ShapeDtypeStruct((1, 2, 2, rows, width), BF),
            jax.ShapeDtypeStruct((1, 2, 2, rows, width), BF),
        ],
        grid_spec=pltpu.PrefetchScalarGridSpec(
            num_scalar_prefetch=3,
            grid=(groups,),
            in_specs=[row_spec, kv_spec, kv_spec, row_spec, stat_spec, stat_spec]
            + [pl.BlockSpec(memory_space=pl.ANY)] * len(before),
            out_specs=[row_spec, out_spec, out_spec],
            scratch_shapes=[
                pltpu.VMEM((4 * rows, heads * rows), BF),
                pltpu.VMEM((4 * rows, heads * rows), BF),
                pltpu.VMEM((heads * rows, GROUP), BF),
                pltpu.VMEM((heads * rows, GROUP), BF),
                pltpu.VMEM((4 * rows, GROUP), BF),
                pltpu.VMEM((4 * rows, GROUP), BF),
                pltpu.VMEM((GROUP, 4 * rows), BF),
            ],
        ),
        input_output_aliases={len(operands) + i: i for i in range(len(before))},
        compiler_params=params(18),
        cost_estimate=cost(5 * 2 * rows * 4 * rows * 4 * width, 2e7, 12 * rows * 4 * rows),
        name="attend_back",
    )(*operands, *before)


CHUNKS = 16


def row_mask(counts, live, meta, slot, rows):
    return key_masks(counts, live, meta, slot, rows, (0,), 0)[0]


def gelu_parts(v):
    size = jnp.abs(v)
    decay = jnp.exp2(v * v * (-0.5 * 1.4426950408889634))
    scale = 1.0 + (0.3275911 * 0.7071067811865476) * size
    t = pl.reciprocal(scale, approx=True)
    t = t * (2.0 - scale * t)
    poly = t * (0.127414796 + t * (-0.142248368 + t * (0.7107068705 + t * (-0.7265760135 + t * 0.5307027145))))
    tail = poly * decay
    phi = jnp.where(v >= 0, 1.0 - tail, tail)
    return phi, decay * 0.3989422804014327


def mlp_kernel(slots, half, counts, live, meta, *refs):
    seconds, rest = refs[:2 * slots], refs[2 * slots:]
    cot, cot_p, w_in, w_out, act_out, pre_out, *grads_out = rest[:8]
    sec, go, win, wout, act, pre, grads, sems, out_sems = rest[8:]
    rows = seconds[0].shape[0]
    count = slots * rows
    width = sec.shape[1]
    me = meta[2]
    part = pl.multiple_of((2 * meta[1] + half) * width, width)

    def copies_for(side):
        whole = pl.ds(side * count, count)
        out = [
            pltpu.make_async_copy(
                seconds[side * slots + s], sec.at[pl.ds(side * count + s * rows, rows)], sems.at[side * (slots + 1) + s]
            )
            for s in range(slots)
        ]
        source = (cot, cot_p)[side]
        return out, pltpu.make_async_copy(source, go.at[whole], sems.at[side * (slots + 1) + slots])

    last = 2 * (slots + 1)
    load_in = pltpu.make_async_copy(w_in.at[:, pl.ds(part, width)], win, sems.at[last])
    load_out = pltpu.make_async_copy(w_out.at[pl.ds(part, width), :], wout, sems.at[last + 1])
    sides = [copies_for(side) for side in range(2)]
    for c in sides[0][0]:
        c.start()
    load_in.start()
    sides[0][1].start()
    load_out.start()
    for c in sides[1][0]:
        c.start()
    sides[1][1].start()
    stores = []

    def store(source, target):
        copy = pltpu.make_async_copy(source, target, out_sems.at[len(stores)])
        copy.start()
        stores.append(copy)

    def activate(at, before, grad_act):
        phi, density = gelu_parts(before)
        act[at, :] = (before * phi).astype(BF)
        pre[at, :] = (grad_act * (phi + before * density)).astype(BF)

    own = slice(0, count)
    for c in sides[0][0]:
        c.wait()
    load_in.wait()
    before = dot(sec[own, :], win[...])
    sides[0][1].wait()
    load_out.wait()
    for c in sides[1][0]:
        c.wait()
    sides[1][1].wait()
    for side in range(2):
        for s in range(slots):
            mask = key_masks(counts, live, meta, s, rows, (side,), 0)[0]
            here = slice(side * count + s * rows, side * count + (s + 1) * rows)
            go[here, :] = jnp.where(mask, go[here, :], jnp.zeros((rows, width), BF))
    activate(own, before, dot(go[own, :], wout[...], NT))
    for s in range(slots):
        at = slice(count + s * rows, count + (s + 1) * rows)
        activate(at, dot(sec[at, :], win[...]), dot(go[at, :], wout[...], NT))
    for side in range(2):
        window = pl.ds(side * count, count)
        store(act.at[window], act_out.at[window])
        store(pre.at[window], pre_out.at[window])
    size = width // CHUNKS
    for kind, (left, right) in ((1, (act, go)), (0, (sec, pre))):
        value = dot(left[...], right[...], TN)
        for a in range(CHUNKS):
            grads[kind, a ^ me] = value[a * size:(a + 1) * size].astype(BF)
        for i, out in enumerate(grads_out):
            store(grads.at[kind, pl.ds(i * CHUNKS // 2, CHUNKS // 2)], out.at[:, kind])
    for copy in stores:
        copy.wait()


def mlp(counts, live, meta, seconds, cotangent, cotangent_p, w_fc1, w_fc2, half):
    rows, width = seconds[0].shape
    slots = len(seconds) // 2
    both = 2 * slots * rows
    operands = (*seconds, cotangent.reshape(slots * rows, width), cotangent_p.reshape(slots * rows, width), w_fc1, w_fc2)
    return pl.pallas_call(
        functools.partial(mlp_kernel, slots, half),
        out_shape=[
            jax.ShapeDtypeStruct((both, width), BF),
            jax.ShapeDtypeStruct((both, width), BF),
        ]
        + [jax.ShapeDtypeStruct((CHUNKS // 2, 2, width // CHUNKS, width), BF)] * 2,
        grid_spec=pltpu.PrefetchScalarGridSpec(
            num_scalar_prefetch=3,
            grid=(1,),
            in_specs=[HBM] * (len(operands) - 2) + [STAY] * 2,
            out_specs=[STAY] * 2 + [HBM] * 2,
            scratch_shapes=[pltpu.VMEM((both, width), BF)] * 2
            + [pltpu.VMEM((width, width), BF)] * 2
            + [pltpu.VMEM((both, width), BF)] * 2
            + [
                pltpu.VMEM((2, CHUNKS, width // CHUNKS, width), BF),
                pltpu.SemaphoreType.DMA((2 * (slots + 1) + 2,)),
                pltpu.SemaphoreType.DMA((8,)),
            ],
        ),
        compiler_params=params(20),
        cost_estimate=cost(2 * 4 * 2 * slots * rows * width * width, 2e7),
        name="mlp",
    )(counts, live, meta, *operands)


def lend_kernel(nt, meta, first, second, weight, out, left, held, sems):
    count, width = out.shape
    core = meta[1]
    loads = []
    for i, source in enumerate((first, second)):
        place = pl.ds(pl.multiple_of((2 * core + i) * width, width), width)
        loads.append(pltpu.make_async_copy(source.at[pl.ds(count, count)], left.at[i], sems.at[2 * i]))
        part = weight.at[:, place] if nt else weight.at[place, :]
        loads.append(pltpu.make_async_copy(part, held.at[i], sems.at[2 * i + 1]))
    for load in loads:
        load.start()
    dims = NT if nt else NN
    loads[0].wait()
    loads[1].wait()
    total = dot(left[0], held[0], dims)
    loads[2].wait()
    loads[3].wait()
    out[...] = (total + dot(left[1], held[1], dims)).astype(BF)


def lend(nt, meta, first, second, weight):
    both, width = first.shape
    return pl.pallas_call(
        functools.partial(lend_kernel, nt),
        out_shape=jax.ShapeDtypeStruct((both // 2, width), BF),
        grid_spec=pltpu.PrefetchScalarGridSpec(
            num_scalar_prefetch=1,
            grid=(1,),
            in_specs=[STAY] * 3,
            out_specs=pl.BlockSpec((both // 2, width), lambda i, *_: (0, 0)),
            scratch_shapes=[
                pltpu.VMEM((2, both // 2, width), BF),
                pltpu.VMEM((2, width, width), BF),
                pltpu.SemaphoreType.DMA((4,)),
            ],
        ),
        compiler_params=params(10),
        cost_estimate=cost(2 * both * width * width, 6e6),
        name="lend",
    )(meta, first, second, weight)


def layer_norm_back(values, gain, grad):
    normed, scale = normalized(values)
    t = grad * gain
    return scale * (t - jnp.mean(t, axis=-1, keepdims=True) - normed * jnp.mean(t * normed, axis=-1, keepdims=True))


def turn_kernel(
    counts, live, meta, first, second, weight, got, hidden, cotangent, attended, gain, w_proj,
    grad_branch, grad_attended, delta, left, held, got_v, hidden_v, cot_v, att_v, proj_v, sems,
):
    slots, rows, width = grad_branch.shape
    count = slots * rows
    core = meta[1]
    loads = []
    for i, source in enumerate((first, second)):
        place = pl.ds(pl.multiple_of((2 * core + i) * width, width), width)
        loads.append(pltpu.make_async_copy(source.at[pl.ds(0, count)], left.at[i], sems.at[2 * i]))
        loads.append(pltpu.make_async_copy(weight.at[:, place], held.at[i], sems.at[2 * i + 1]))
    for i, (source, target) in enumerate(
        ((got, got_v), (hidden, hidden_v), (cotangent, cot_v), (w_proj, proj_v), (attended, att_v))
    ):
        loads.append(pltpu.make_async_copy(source, target, sems.at[4 + i]))
    for load in loads:
        load.start()
    loads[0].wait()
    loads[1].wait()
    total = dot(left[0], held[0], NT)
    loads[2].wait()
    loads[3].wait()
    total = total + dot(left[1], held[1], NT)
    for load in loads[4:]:
        load.wait()
    head = lax.broadcasted_iota(jnp.int32, (32, width), 0)
    column = lax.broadcasted_iota(jnp.int32, (32, width), 1) // HEAD_DIM
    per = GROUP // HEAD_DIM
    pick = (head == (column // per) * 8 + column % per).astype(BF)
    for s in range(slots):
        here = slice(s * rows, (s + 1) * rows)
        mask = row_mask(counts, live, meta, s, rows)
        grad_out = jnp.where(mask, cot_v[s].astype(F32), 0.0)
        given = total[here] + got_v[here, :].astype(F32)
        branch = (grad_out + layer_norm_back(hidden_v[s], gain[...], given)).astype(BF)
        grad_branch[s] = branch
        back = dot(branch, proj_v[...], NT).astype(BF)
        grad_attended[s] = back
        product = back.astype(F32) * att_v[s].astype(F32)
        high = product.astype(BF)
        low = (product - high.astype(F32)).astype(BF)
        sums = dot(pick, high, NT) + dot(pick, low, NT)
        for g in range(width // GROUP):
            delta[s, g] = sums[8 * g:8 * g + 8]


def turn(counts, live, meta, first, second, weight, got, hidden, cotangent, attended, gain, w_proj):
    slots, rows, width = hidden.shape
    count = slots * rows
    groups = width // GROUP
    whole = pl.BlockSpec(hidden.shape, lambda i, *_: (0, 0, 0))
    return pl.pallas_call(
        turn_kernel,
        out_shape=[
            jax.ShapeDtypeStruct(hidden.shape, BF),
            jax.ShapeDtypeStruct(hidden.shape, BF),
            jax.ShapeDtypeStruct((slots, groups, 8, rows), F32),
        ],
        grid_spec=pltpu.PrefetchScalarGridSpec(
            num_scalar_prefetch=3,
            grid=(1,),
            in_specs=[STAY] * 3 + [HBM] * 4 + [pl.BlockSpec((1, width), lambda i, *_: (0, 0)), HBM],
            out_specs=[whole, whole, pl.BlockSpec((slots, groups, 8, rows), lambda i, *_: (0, 0, 0, 0))],
            scratch_shapes=[
                pltpu.VMEM((2, count, width), BF),
                pltpu.VMEM((2, width, width), BF),
                pltpu.VMEM((count, width), BF),
                pltpu.VMEM(hidden.shape, F32),
                pltpu.VMEM(hidden.shape, BF),
                pltpu.VMEM(hidden.shape, BF),
                pltpu.VMEM((width, width), BF),
                pltpu.SemaphoreType.DMA((9,)),
            ],
        ),
        compiler_params=params(20),
        cost_estimate=cost(3 * 2 * slots * rows * width * width, 1.5e7),
        name="turn",
    )(counts, live, meta, first, second, weight, got, hidden, cotangent, attended, gain, w_proj)


def finish_kernel(counts, live, meta, first, second, weight, got, hidden, output, left, held, got_v, hidden_v, sems):
    slots, rows, width = output.shape
    count = slots * rows
    core = meta[1]
    loads = []
    for i, source in enumerate((first, second)):
        place = pl.ds(pl.multiple_of((2 * core + i) * width, width), width)
        loads.append(pltpu.make_async_copy(source.at[pl.ds(0, count)], left.at[i], sems.at[2 * i]))
        loads.append(pltpu.make_async_copy(weight.at[place, :], held.at[i], sems.at[2 * i + 1]))
    loads.append(pltpu.make_async_copy(got, got_v, sems.at[4]))
    loads.append(pltpu.make_async_copy(hidden, hidden_v, sems.at[5]))
    for load in loads:
        load.start()
    loads[0].wait()
    loads[1].wait()
    total = dot(left[0], held[0])
    loads[2].wait()
    loads[3].wait()
    total = total + dot(left[1], held[1])
    loads[4].wait()
    loads[5].wait()
    for s in range(slots):
        here = slice(s * rows, (s + 1) * rows)
        mask = row_mask(counts, live, meta, s, rows)
        output[s] = jnp.where(mask, total[here] + got_v[here, :].astype(F32) + hidden_v[s], 0.0).astype(BF)


def finish(counts, live, meta, first, second, weight, got, hidden):
    slots, rows, width = hidden.shape
    count = slots * rows
    return pl.pallas_call(
        finish_kernel,
        out_shape=jax.ShapeDtypeStruct(hidden.shape, BF),
        grid_spec=pltpu.PrefetchScalarGridSpec(
            num_scalar_prefetch=3,
            grid=(1,),
            in_specs=[STAY] * 3 + [HBM] * 2,
            out_specs=pl.BlockSpec(hidden.shape, lambda i, *_: (0, 0, 0)),
            scratch_shapes=[
                pltpu.VMEM((2, count, width), BF),
                pltpu.VMEM((2, width, width), BF),
                pltpu.VMEM((count, width), BF),
                pltpu.VMEM(hidden.shape, F32),
                pltpu.SemaphoreType.DMA((6,)),
            ],
        ),
        compiler_params=params(16),
        cost_estimate=cost(2 * 2 * slots * rows * width * width, 9e6),
        name="finish",
    )(counts, live, meta, first, second, weight, got, hidden)


def gather_kernel(mine, got, w_kv, *refs):
    key_own, value_own, key_other, value_other, partial = refs[-5:]
    width = partial.shape[-1]
    parts = []
    for place, out in ((0, (key_own, value_own)), (1, (key_other, value_other))):
        for i in range(2):
            total = (mine[0, place, i].astype(F32) + got[0, place, i].astype(F32)).astype(BF)
            out[i][0] = total
            parts.append(total)
    partial[0] = (dot(parts[2], w_kv[:, :width], NT) + dot(parts[3], w_kv[:, width:], NT)).astype(BF)


def gather(slot, slots, mine, got, w_qkv, before):
    _, _, _, rows, width = mine.shape
    row_spec = pl.BlockSpec((1, rows, width), lambda i: (slot, 0, 0))
    kv_spec = pl.BlockSpec((1, 2, 2, rows, width), lambda i: (0, 0, 0, 0, 0))
    return pl.pallas_call(
        gather_kernel,
        out_shape=[jax.ShapeDtypeStruct((slots, rows, width), BF)] * 4 + [jax.ShapeDtypeStruct((1, rows, width), BF)],
        grid=(1,),
        in_specs=[kv_spec, kv_spec, pl.BlockSpec((pl.Element(width), pl.Element(2 * width)), lambda s: (0, width))]
        + [pl.BlockSpec(memory_space=pl.ANY)] * len(before),
        out_specs=[row_spec] * 4 + [pl.BlockSpec((1, rows, width), lambda i: (0, 0, 0))],
        input_output_aliases={3 + i: i for i in range(len(before))},
        compiler_params=params(10),
        cost_estimate=cost(2 * 2 * rows * width * width, 6e6),
        name="gather",
    )(mine, got, w_qkv, *before)


VALUE_UNITS = ((0, 4, 1, 0, 0), (1, 6, 0, 1, 0), (7, 8, 1, 1, 1))
QUERY_UNITS = ((0, 2, 1, 1, 0), (0, 3, 1, 0, 1), (1, 5, 0, 1, 1))


def weigh_steps(units):
    seen = set()
    steps = []
    for step in units:
        steps.append(step + (int(step[0] not in seen),))
        seen.add(step[0])
    return jnp.array(steps, jnp.int32)


def weigh_kernel(meta, steps, *refs):
    sources, (grads, held, total, sems) = refs[:9], refs[9:]
    step = pl.program_id(0)
    size = held.shape[1] // CHUNKS
    values = steps[0, 1] == VALUE_UNITS[0][1]

    def start(units):
        seen = []
        for unit in units:
            for i in unit[:2]:
                if i not in seen:
                    seen.append(i)
                    pltpu.make_async_copy(sources[i], held.at[i], sems.at[i]).start()

    @pl.when(jnp.logical_and(step == 0, values))
    def _():
        start(VALUE_UNITS)

    @pl.when(jnp.logical_and(step == 0, jnp.logical_not(values)))
    def _():
        start(QUERY_UNITS)

    left = steps[step, 0]
    right = steps[step, 1]

    @pl.when(steps[step, 5] == 1)
    def _():
        pltpu.make_async_copy(sources[0], held.at[left], sems.at[left]).wait()

    pltpu.make_async_copy(sources[0], held.at[right], sems.at[right]).wait()

    @pl.when(steps[step, 2] == 1)
    def _():
        total[...] = dot(held[left], held[right], TN)

    @pl.when(steps[step, 2] != 1)
    def _():
        total[...] += dot(held[left], held[right], TN)

    @pl.when(steps[step, 3] == 1)
    def _():
        unit = steps[step, 4]
        me = meta[4 + unit]
        for a in range(CHUNKS):
            grads[unit, a ^ me] = total[a * size:(a + 1) * size, :].astype(BF)


def weigh(meta, steps, arrays):
    arrays = [a.reshape(-1, a.shape[-1]) for a in arrays]
    rows, width = arrays[0].shape
    shape = (2, CHUNKS, width // CHUNKS, width)
    return pl.pallas_call(
        weigh_kernel,
        out_shape=jax.ShapeDtypeStruct(shape, BF),
        grid_spec=pltpu.PrefetchScalarGridSpec(
            num_scalar_prefetch=2,
            grid=(3,),
            in_specs=[HBM] * 9,
            out_specs=pl.BlockSpec(shape, lambda i, *_: (0, 0, 0, 0)),
            scratch_shapes=[
                pltpu.VMEM((9, rows, width), BF),
                pltpu.VMEM((rows, width), F32),
                pltpu.SemaphoreType.DMA((9,)),
            ],
        ),
        compiler_params=params(19),
        cost_estimate=cost(3 * 2 * rows * width * width, 1e7),
        name="weigh",
    )(meta, steps, *arrays)


def close_kernel(gq, gk, gv, w_qkv, tokens, grad_hidden, gain, *refs):
    partials, (out, total) = refs[:-2], refs[-2:]
    step = pl.program_id(0)
    slots, rows, width = gq.shape
    flat = (slots * rows, width)

    @pl.when(step == 0)
    def _():
        total[...] = dot(gq[...].reshape(flat), w_qkv[...], NT)

    @pl.when(step == 1)
    def _():
        total[...] += dot(gk[...].reshape(flat), w_qkv[...], NT)

    @pl.when(step == 2)
    def _():
        total[...] += dot(gv[...].reshape(flat), w_qkv[...], NT)
        for s, partial in enumerate(partials):
            total[s * rows:(s + 1) * rows, :] += partial[0].astype(F32)

    @pl.when(step > 2)
    def _():
        first = total[pl.ds(pl.multiple_of((step - 3) * rows, rows), rows), :]
        out[0] = (grad_hidden[0].astype(F32) + layer_norm_back(tokens[0].astype(F32), gain[...], first)).astype(BF)


def close(gq, gk, gv, partials, tokens, grad_hidden, gain, w_qkv):
    slots, rows, width = tokens.shape
    row_spec = pl.BlockSpec((1, rows, width), lambda i: (jnp.maximum(i - 3, 0), 0, 0))
    whole = pl.BlockSpec((slots, rows, width), lambda i: (0, 0, 0))
    return pl.pallas_call(
        close_kernel,
        out_shape=jax.ShapeDtypeStruct(tokens.shape, BF),
        grid=(3 + slots,),
        in_specs=[whole] * 3 + [pl.BlockSpec((width, width), lambda i: (0, jnp.minimum(i, 2)))] + [row_spec] * 2 + [
            pl.BlockSpec((1, width), lambda i: (0, 0)),
        ] + [pl.BlockSpec((1, rows, width), lambda i: (0, 0, 0))] * slots,
        out_specs=row_spec,
        scratch_shapes=[pltpu.VMEM((slots * rows, width), F32)],
        compiler_params=params(18),
        cost_estimate=cost(3 * 2 * slots * rows * width * width, 1.2e7),
        name="close",
    )(gq, gk, gv, w_qkv, tokens, grad_hidden, gain, *partials)


SPREAD = 4


def keep_row_sums(held, value):
    step = pl.program_id(0)
    rows = value.shape[0]
    column = jnp.sum(value, axis=-1, keepdims=True)
    held[pl.ds(pl.multiple_of(step * rows, rows), rows), :] = jnp.broadcast_to(column, (rows, 128))


def put_row_sums(norm, held, gain):
    @pl.when(pl.program_id(0) == pl.num_programs(0) - 1)
    def _():
        for r in range(norm.shape[0]):
            norm[r:r + 1, :] = held[r * 128:(r + 1) * 128, :].T[:1] / gain[r:r + 1, :]


def load_pieces(sources, held, sems, tops):
    copies = []
    count = len(sources) // 4
    for i, top in enumerate(tops):
        pieces = sources[count * i:count * (i + 1)]
        for k, piece in enumerate(pieces):
            if len(pieces) == 4:
                copies.append(pltpu.make_async_copy(piece, held.at[i, k ^ top], sems.at[i, k]))
                continue
            for low in range(4 // len(pieces)):
                place = k * (4 // len(pieces)) + low
                copies.append(
                    pltpu.make_async_copy(piece.at[pl.ds(low * 4, 4)], held.at[i, place ^ top], sems.at[i, place])
                )
    for copy in copies:
        copy.start()
    for copy in copies:
        copy.wait()


def spread_mlp_kernel(meta, *refs):
    pieces, (w_fc1, gain, grad_fc1, grad_fc2, norm, chunks, held, sems) = refs[:-8], refs[-8:]
    step = pl.program_id(0)
    size, width = chunks.shape[-2:]
    mx, my, mz, mw = meta[3], meta[6], meta[7], meta[8]

    @pl.when(step == 0)
    def _():
        load_pieces(pieces, chunks, sems, [mx * 2 + my, my * 2 + mx] * 2)

    first = meta[1] == 0
    z, y = step // 2, step % 2
    for a in range(4):
        w, x = a // 2, a % 2
        low = (z ^ mz) * 2 + (w ^ mw)
        for half, top in ((0, x * 2 + y), (1, y * 2 + x)):
            for place, core in ((half, 0), (2 + half, 1)):
                own = jnp.where(first, core, 1 - core)
                value = chunks[2 * own + half, top, low].astype(F32)
                grad_fc1[a * size:(a + 1) * size, place * width:(place + 1) * width] = value[0]
                grad_fc2[place, a * size:(a + 1) * size, :] = value[1]
    keep_row_sums(held, grad_fc1[...] * w_fc1[...].astype(F32))
    put_row_sums(norm, held, gain)


def spread_mlp(meta, pieces, w_fc1, gain):
    width, hidden_width = w_fc1.shape
    per = CHUNKS // SPREAD
    size = width // CHUNKS
    outs = pl.pallas_call(
        spread_mlp_kernel,
        out_shape=[
            jax.ShapeDtypeStruct((width, hidden_width), F32),
            jax.ShapeDtypeStruct((4, width, width), F32),
            jax.ShapeDtypeStruct((width // 128, 128), F32),
        ],
        grid_spec=pltpu.PrefetchScalarGridSpec(
            num_scalar_prefetch=1,
            grid=(SPREAD,),
            in_specs=[HBM] * len(pieces) + [
                pl.BlockSpec((per * size, hidden_width), lambda a, *_: (a, 0)),
                pl.BlockSpec((width // 128, 128), lambda a, *_: (0, 0)),
            ],
            out_specs=[
                pl.BlockSpec((per * size, hidden_width), lambda a, *_: (a, 0)),
                pl.BlockSpec((4, per * size, width), lambda a, *_: (0, a, 0)),
                pl.BlockSpec((width // 128, 128), lambda a, *_: (0, 0)),
            ],
            scratch_shapes=[
                pltpu.VMEM((4, 4, 4) + pieces[0].shape[1:], BF),
                pltpu.VMEM((width, 128), F32),
                pltpu.SemaphoreType.DMA((4, 4)),
            ],
        ),
        compiler_params=params(26),
        cost_estimate=cost(1e6, 4.7e7),
        name="spread_mlp",
    )(meta, *pieces, w_fc1, gain.reshape(width // 128, 128))
    return outs[0], outs[1].reshape(hidden_width, width), outs[2].reshape(width)


def spread_qkv_kernel(meta, *refs):
    pieces, (w_qkv, gain, grad_qkv, grad_proj, norm, chunks, held, sems) = refs[:-8], refs[-8:]
    step = pl.program_id(0)
    size, width = chunks.shape[-2:]
    mx, my, mz, mw = meta[3], meta[6], meta[7], meta[8]

    @pl.when(step == 0)
    def _():
        load_pieces(pieces, chunks, sems, [mx * 2 + my, my * 2 + mx] * 2)

    first = meta[1] == 0
    own = jnp.where(first, 0, 2)
    part = 2 - own
    for a in range(4):
        here = slice(a * size, (a + 1) * size)
        low = a ^ (mz * 2 + mw)
        for i, at in enumerate((own, own + 1, part)):
            grad_qkv[here, i * width:(i + 1) * width] = chunks[at, step, low].astype(F32)
        grad_proj[here, :] = chunks[part + 1, step, low].astype(F32)
    keep_row_sums(held, grad_qkv[...] * w_qkv[...].astype(F32))
    put_row_sums(norm, held, gain)


def spread_qkv(meta, pieces, w_qkv, gain):
    width = w_qkv.shape[0]
    size = width // CHUNKS
    per = CHUNKS // SPREAD

    def rows(columns):
        return pl.BlockSpec((per * size, columns), lambda a, *_: (a, 0))

    line = pl.BlockSpec((width // 128, 128), lambda a, *_: (0, 0))
    outs = pl.pallas_call(
        spread_qkv_kernel,
        out_shape=[
            jax.ShapeDtypeStruct((width, 3 * width), F32),
            jax.ShapeDtypeStruct((width, width), F32),
            jax.ShapeDtypeStruct((width // 128, 128), F32),
        ],
        grid_spec=pltpu.PrefetchScalarGridSpec(
            num_scalar_prefetch=1,
            grid=(SPREAD,),
            in_specs=[HBM] * len(pieces) + [rows(3 * width), line],
            out_specs=[rows(3 * width), rows(width), line],
            scratch_shapes=[
                pltpu.VMEM((4, 4, 4) + pieces[0].shape[1:], BF),
                pltpu.VMEM((width, 128), F32),
                pltpu.SemaphoreType.DMA((4, 4)),
            ],
        ),
        compiler_params=params(18),
        cost_estimate=cost(1e6, 1.8e7),
        name="spread_qkv",
    )(meta, *pieces, w_qkv, gain.reshape(width // 128, 128))
    return outs[0], outs[1], outs[2].reshape(width)


DIGITS = {"x": (0, 2), "y": (1, 0), "z": (2, 0), "w": (4, 0)}


def swap(value, axis, mask):
    return lax.ppermute(value, axis, [(i, i ^ mask) for i in range(lax.axis_size(axis))])


def swap_digits(value, masks):
    batch, band = masks
    if not band:
        return swap(value, "batch", batch)
    if not batch:
        return swap(value, "band", band)
    return swap(value, ("batch", "band"), batch * lax.axis_size("band") + band)


def add(*values):
    total = values[0].astype(F32)
    for value in values[1:]:
        total = total + value.astype(F32)
    return total.astype(BF)


def pack_kernel(groups, *refs):
    total = sum(count for count, _ in groups)
    sources, refs = refs[:total], refs[total:]
    outs = sum(1 + split for _, split in groups)
    targets, refs = list(refs[:outs]), refs[outs:]
    held, (sems, out_sems) = refs[:len(groups)], refs[len(groups):]
    loads, stores = [], []
    for group, (count, split) in enumerate(groups):
        mine = [targets.pop(0) for _ in range(1 + split)]
        for i in range(count):
            at = len(loads)
            size = sources[at].shape[0]
            here = pl.ds(i * size, size)
            loads.append(pltpu.make_async_copy(sources[at], held[group].at[here], sems.at[at]))
            stores.append([
                pltpu.make_async_copy(
                    held[group].at[here, j] if split else held[group].at[here], target.at[here], out_sems.at[at, j]
                )
                for j, target in enumerate(mine)
            ])
    for load in loads:
        load.start()
    for load, store in zip(loads, stores):
        load.wait()
        for copy in store:
            copy.start()
    for store in stores:
        for copy in store:
            copy.wait()


def pack(*groups):
    shapes = [(len(parts) * parts[0].shape[0],) + parts[0].shape[1:] for parts, _ in groups]
    out = []
    for shape, (_, split) in zip(shapes, groups):
        out += [shape[:1] + shape[2:]] * 2 if split else [shape]
    parts = [p for group, _ in groups for p in group]
    return list(pl.pallas_call(
        functools.partial(pack_kernel, [(len(p), int(split)) for p, split in groups]),
        out_shape=[jax.ShapeDtypeStruct(o, BF) for o in out],
        in_specs=[HBM] * len(parts),
        out_specs=[HBM] * len(out),
        scratch_shapes=[pltpu.VMEM(shape, BF) for shape in shapes]
        + [pltpu.SemaphoreType.DMA((len(parts),)), pltpu.SemaphoreType.DMA((len(parts), 2))],
        compiler_params=params(12),
        cost_estimate=cost(0, 2e6),
        name="pack",
    )(*parts))


class Line:
    def __init__(self):
        self.mark = None

    def tie(self, value):
        if self.mark is None:
            return value
        value, self.mark = lax.optimization_barrier((value, self.mark))
        return value


class Chain:
    def __init__(self, terms=(), halves=(), upper=None, pieces=(), joins=()):
        self.terms = list(terms)
        self.upper = upper
        self.pieces = list(pieces)
        self.steps = [("part", group) for group in halves] + [("join", group) for group in joins]

    def masks(self, group):
        count = 1 << len(group)
        masks = []
        for place in range(1, count):
            digits = [DIGITS[d] for i, d in enumerate(group) if place & (count >> (i + 1))]
            masks.append((sum(d[0] for d in digits), sum(d[1] for d in digits)))
        return masks

    def total_here(self):
        return add(*self.terms)

    def total(self):
        value = add(*self.terms)
        mask = 8
        while mask < lax.axis_size("batch"):
            value = add(value, swap(value, "batch", mask))
            mask *= 2
        return value

    def offers(self):
        kind, what = self.steps[0]
        if kind == "join":
            return self.pieces
        if self.upper is not None:
            sent, self.upper = [self.upper], None
            return sent
        count = 1 << len(what)
        size = self.terms[0].shape[0] // count
        sent = [add(*[t[i * size:(i + 1) * size] for t in self.terms]) for i in range(1, count)]
        self.terms = [t[:size] for t in self.terms]
        return sent

    def start(self, sent):
        kind, what = self.steps[0]
        masks = self.masks(what)
        if kind == "join":
            return [swap_digits(s, mask) for mask in masks for s in sent]
        return [swap_digits(s, mask) for s, mask in zip(sent, masks)]

    def take(self, moved):
        kind, _ = self.steps.pop(0)
        if kind == "join":
            self.pieces = self.pieces + list(moved)
        else:
            self.terms = self.terms + list(moved)


class Flight:
    def __init__(self, line):
        self.line = line
        self.parts = {}

    def land(self, *names):
        names = [n for n in (names or tuple(self.parts)) if n in self.parts]
        if not names:
            return {}
        held = [self.parts.pop(n) for n in names]
        got = self.line.tie(held)
        self.line.mark = got
        for name, moved in zip(names, got):
            if isinstance(name, Chain):
                name.take(moved)
        return {n: g for n, g in zip(names, got) if not isinstance(n, Chain)}

    def launch(self, *items):
        items = [i for i in items if not isinstance(i, Chain) or i.steps]
        arrays = [i.offers() if isinstance(i, Chain) else list(i[1]) for i in items]
        arrays = self.line.tie(arrays)
        self.line.mark = arrays
        for item, sent in zip(items, arrays):
            if isinstance(item, Chain):
                self.parts[item] = item.start(sent)
            else:
                name, _, axis, mask = item
                self.parts[name] = [swap(a, axis, mask) for a in sent]


def place_in(order):
    place = 0
    for digit in "".join(order):
        batch, band = DIGITS[digit]
        bit = lax.axis_index("batch") // batch if batch else lax.axis_index("band") // band
        place = place * 2 + bit % 2
    return place


ORDER = ("z", "y", "wx")
LAST_ORDERS = (("x", "y"), ("y", "x"))


def body(
    tokens, w_qkv, w_proj, w_fc1, w_fc2, gain_one, gain_two, cotangent, band_counts, slot_live
):
    slots, rows, width = tokens.shape
    flat = (slots * rows, width)
    band = lax.axis_index("band")
    core = band % 2
    meta = jnp.stack(
        [band, core] + [place_in(o) for o in (ORDER, "x") + tuple(order + ("zw",) for order in LAST_ORDERS) + ("y", "z", "w")]
    ).astype(jnp.int32)
    gain_one = gain_one[None]
    gain_two = gain_two[None]
    at = (band_counts, slot_live, meta)
    line = Line()

    tokens, *tokens_other = lax.optimization_barrier(
        (tokens,) + tuple(tokens[s:s + 1] for s in range(slots))
    )
    tokens_other = [swap(t, "band", 2) for t in tokens_other]
    cotangent_p = swap(cotangent, "band", 1)
    first_own, query, kv_own = project(tokens, w_qkv, gain_one)
    tables = weigh_steps(QUERY_UNITS), weigh_steps(VALUE_UNITS)
    steps_theirs = jnp.where(core == 1, *tables)
    steps_ours = jnp.where(core == 0, *tables)
    line.mark = (first_own, meta, gain_two, steps_theirs, steps_ours)
    first_other, pairs = [], []
    seconds, seconds_p = [], []
    kept = ()

    def take(s):
        first, pair = project_other(s, line.tie(tokens_other[s]), kv_own, w_qkv, gain_one, first_other)
        line.mark = pair
        first_other[:] = [first]
        pairs.append((pair, swap(pair, "band", 1)))

    def look(s):
        *out, second = attend(s, *at, line.tie(query), *pairs[s], tokens, w_proj, gain_two, kept)
        line.mark = second
        seconds.append(second)
        seconds_p.append(swap(second, "band", 1))
        return tuple(out)

    take(0)
    for s in range(slots):
        if s == 1:
            for n in range(1, slots):
                take(n)
            cotangent_p = line.tie(cotangent_p)
        kept = look(s)
    attended, lse, hidden = kept

    flight = Flight(line)
    chains = []
    acts, pres = [], []
    all_seconds = seconds + seconds_p
    for half in range(2):
        act, pre, lower, upper = mlp(
            *at, [line.tie(all_seconds[0])] + all_seconds[1:], cotangent, cotangent_p, w_fc1, w_fc2, half
        )
        line.mark = upper
        acts.append(act)
        pres.append(pre)
        chains.append(Chain((lower,), ORDER, upper))
        if half == 0:
            flight.launch(chains[0])
    one, two = chains
    turn_part = lend(True, meta, line.tie(pres[0]), pres[1], w_fc1)
    line.mark = turn_part
    finish_part = lend(False, meta, line.tie(acts[0]), acts[1], w_fc2)
    line.mark = finish_part
    flight.land()
    flight.launch(("turn", [turn_part], "band", 1), two, one, ("finish", [finish_part], "band", 1))
    got = flight.land("turn")
    branch, grad_attended, delta = turn(
        *at, line.tie(pres[0]), pres[1], w_fc1, got["turn"][0], hidden, cotangent, attended, gain_two, w_proj
    )
    line.mark = delta

    grad_query, sums, keeps, waiting = (), (), [], []

    def bring(s):
        *kept_sums, partial = gather(s, slots, line.tie(keeps[s]), got[f"send{s}"][0], w_qkv, sums)
        line.mark = partial
        return tuple(kept_sums), [(f"partial{s}", [partial], "band", 2)]

    for s in range(slots):
        query_grad, keep, send = attend_back(
            s, *at, line.tie(query), *pairs[s], grad_attended, lse, delta, grad_query
        )
        line.mark = send
        grad_query = (query_grad,)
        keeps.append(keep)
        got.update(flight.land())
        if s < slots - 1:
            flight.launch((f"send{s}", [send], "band", 1), *waiting, two, one)
            waiting = []
            if s > 0:
                sums, waiting = bring(s - 1)
    assert not one.steps and not two.steps
    both = Chain(pieces=[jnp.stack([one.total(), two.total()], axis=1)], joins=("w", "z"))
    flight.launch((f"send{slots - 1}", [send], "band", 1), *waiting, both)
    waiting = []
    if slots > 1:
        sums, waiting = bring(slots - 2)
    got.update(flight.land(f"send{slots - 1}"))
    sums, last = bring(slots - 1)
    waiting += last
    got.update(flight.land())
    both.pieces = pack((both.pieces, False))
    flight.launch(*waiting, both)
    arrays = (first_own, first_other[0], grad_query[0], *sums, attended, branch)
    theirs = weigh(meta, steps_theirs, (line.tie(first_own),) + arrays[1:])
    line.mark = theirs
    got.update(flight.land())
    halves = pack((both.pieces, True))
    one = Chain(pieces=halves[:1], joins=("y", "x"))
    two = Chain(pieces=halves[1:], joins=("x", "y"))
    flight.launch(("theirs", [theirs], "band", 1), one, two)
    ours = weigh(meta, steps_ours, (line.tie(first_own),) + arrays[1:])
    line.mark = ours
    got.update(flight.land("theirs"))
    (theirs,) = got["theirs"]
    three = Chain((ours[0], theirs[0]), LAST_ORDERS[0])
    four = Chain((ours[1], theirs[1]), LAST_ORDERS[1])
    flight.launch(three, four)
    partials = [got[f"partial{s}"][0] for s in range(slots)]
    grad_input = close(
        line.tie(grad_query[0]), sums[0], sums[1], partials, tokens, branch, gain_one, w_qkv
    )
    line.mark = grad_input
    flight.land(one, two)
    held = pack((one.pieces, False), (two.pieces, False))
    line.mark = held
    flight.land(three, four)
    one.pieces, two.pieces = held[:1], held[1:]
    flight.launch(three, four, ("mlp_held", held, "band", 1))
    got.update(flight.land())
    five = Chain((jnp.stack([three.total_here(), four.total_here()], axis=1),), ("zw",))
    flight.launch(five, one, two)
    output = finish(*at, line.tie(acts[0]), acts[1], w_fc2, got["finish"][0], hidden)
    line.mark = output
    flight.land(five)
    five = Chain(pieces=[five.total()], joins=("zw",))
    flight.launch(five)
    flight.land(one, two)
    flight.land(five)
    halves = pack((five.pieces, True))
    three = Chain(pieces=halves[:1], joins=("y", "x"))
    four = Chain(pieces=halves[1:], joins=("x", "y"))
    flight.launch(three, four, ("mlp_rest", [one.pieces[1], two.pieces[1]], "band", 1))
    got.update(flight.land())

    def gathered(first, second, name):
        parts = [p for pair in zip(got[name + "_held"], got[name + "_rest"]) for p in pair]
        return first.pieces + second.pieces + parts

    mlp_pieces = gathered(one, two, "mlp")
    held = pack((three.pieces, False), (four.pieces, False))
    three.pieces, four.pieces = held[:1], held[1:]
    flight.launch(three, four, ("qkv_held", held, "band", 1))
    mlp_pieces[0] = line.tie(mlp_pieces[0])
    grad_fc1, grad_fc2, norm2 = spread_mlp(meta, mlp_pieces, w_fc1, gain_two)
    line.mark = norm2
    got.update(flight.land())
    flight.launch(("qkv_rest", [three.pieces[1], four.pieces[1]], "band", 1))
    got.update(flight.land())
    grad_qkv, grad_proj, norm1 = spread_qkv(meta, gathered(three, four, "qkv"), w_qkv, gain_one)
    return (output, grad_input, grad_qkv, grad_proj, grad_fc1, grad_fc2, norm1, norm2)


def solution(mesh):
    placed = (
        P("batch", "band", None),
        P(),
        P(),
        P(),
        P(),
        P(),
        P(),
        P("batch", "band", None),
        P("batch", None),
        P("batch"),
    )
    return jax.shard_map(
        body,
        mesh=mesh,
        in_specs=placed,
        out_specs=(
            P("batch", "band", None),
            P("batch", "band", None),
            P(),
            P(),
            P(),
            P(),
            P(),
            P(),
        ),
        check_vma=False,
    )
```

```python
import functools
import jax
import jax.numpy as jnp
from jax import lax
from jax.experimental import pallas as pl
from jax.experimental.pallas import tpu as pltpu
from jax.sharding import PartitionSpec as P

BF = jnp.bfloat16
F32 = jnp.float32
EPSILON = 1e-06
HEAD_DIM = 64
GROUP = 256
NN = (((1,), (0,)), ((), ()))
NT = (((1,), (1,)), ((), ()))
TN = (((0,), (0,)), ((), ()))


def dot(left, right, dims=NN):
    return lax.dot_general(left, right, dims, preferred_element_type=F32)


def params(mib=60):
    return pltpu.CompilerParams(vmem_limit_bytes=mib * 1024 * 1024)


def cost(flops, moved, exps=0):
    return pl.CostEstimate(flops=1, bytes_accessed=1, transcendentals=0)


HBM = pl.BlockSpec(memory_space=pl.ANY)
STAY = pl.BlockSpec(memory_space=pltpu.HBM)


def normalized(values):
    centered = values - jnp.mean(values, axis=-1, keepdims=True)
    spread = jnp.mean(centered * centered, axis=-1, keepdims=True)
    scale = lax.rsqrt(spread + EPSILON)
    return centered * scale, scale


def project_kernel(tokens, weight, gain, first_in, query, both):
    normed, _ = normalized(tokens[0].astype(F32))
    first = (normed * gain[...]).astype(BF)
    first_in[0] = first
    width = first.shape[1]
    query[0] = (dot(first, weight[:, :width]) * HEAD_DIM ** -0.5).astype(BF)
    both[0, 0] = dot(first, weight[:, width:2 * width]).astype(BF)
    both[0, 1] = dot(first, weight[:, 2 * width:]).astype(BF)


def project(tokens, w_qkv, gain):
    slots, rows, width = tokens.shape
    row_spec = pl.BlockSpec((1, rows, width), lambda s: (s, 0, 0))
    return pl.pallas_call(
        project_kernel,
        out_shape=[
            pltpu.HBM(tokens.shape, BF),
            jax.ShapeDtypeStruct(tokens.shape, BF),
            jax.ShapeDtypeStruct((slots, 2, rows, width), BF),
        ],
        grid=(slots,),
        in_specs=[
            row_spec,
            pl.BlockSpec((width, 3 * width), lambda s: (0, 0)),
            pl.BlockSpec((1, width), lambda s: (0, 0)),
        ],
        out_specs=[row_spec, row_spec, pl.BlockSpec((1, 2, rows, width), lambda s: (s, 0, 0, 0))],
        compiler_params=params(14),
        cost_estimate=cost(2 * slots * rows * width * width * 3, 8e6),
        name="project",
    )(tokens, w_qkv, gain)


def project_other_kernel(tokens, own, weight, gain, *refs):
    first_in, both = refs[-2:]
    normed, _ = normalized(tokens[0].astype(F32))
    first = (normed * gain[...]).astype(BF)
    first_in[0] = first
    width = first.shape[1]
    both[0] = own[0]
    both[1, 0] = dot(first, weight[:, :width]).astype(BF)
    both[1, 1] = dot(first, weight[:, width:]).astype(BF)


def project_other(slot, tokens, kv_own, w_qkv, gain, before):
    slots, _, rows, width = kv_own.shape
    return pl.pallas_call(
        project_other_kernel,
        out_shape=[
            jax.ShapeDtypeStruct((slots, rows, width), BF),
            jax.ShapeDtypeStruct((2, 2, rows, width), BF),
        ],
        grid=(1,),
        in_specs=[
            pl.BlockSpec((1, rows, width), lambda i: (0, 0, 0)),
            pl.BlockSpec((1, 2, rows, width), lambda i: (slot, 0, 0, 0)),
            pl.BlockSpec((pl.Element(width), pl.Element(2 * width)), lambda i: (0, width)),
            pl.BlockSpec((1, width), lambda i: (0, 0)),
        ] + [HBM] * len(before),
        out_specs=[
            pl.BlockSpec((1, rows, width), lambda i: (slot, 0, 0)),
            pl.BlockSpec((2, 2, rows, width), lambda i: (0, 0, 0, 0)),
        ],
        input_output_aliases={4 + i: i for i in range(len(before))},
        compiler_params=params(10),
        cost_estimate=cost(2 * rows * width * width * 2, 5e6),
        name="project_other",
    )(tokens, kv_own, w_qkv, gain, *before)


def key_masks(counts, live, meta, slot, rows, flips, axis):
    shape = (rows, 1) if axis == 0 else (1, rows)
    place = lax.broadcasted_iota(jnp.int32, shape, axis)
    alive = live[slot] > 0
    return [place < jnp.where(alive, counts[slot, meta[0] ^ flip], 0) for flip in flips]


FLIPS = (0, 2, 1, 3)


def attend_kernel(slot, counts, live, meta, query, pair, pair_p, tokens, w_proj, gain, *refs):
    attended, lse, hidden, second, held, own_tokens, weight, sems = refs[-8:]
    group = pl.program_id(0)
    rows = query.shape[1]
    copies = (
        pltpu.make_async_copy(tokens.at[slot], own_tokens, sems.at[0]),
        pltpu.make_async_copy(w_proj, weight, sems.at[1]),
    )

    @pl.when(group == 0)
    def _():
        for copy in copies:
            copy.start()

    masks = key_masks(counts, live, meta, slot, rows, FLIPS, 1)
    q = query[0]
    lane = lax.broadcasted_iota(jnp.int32, (1, GROUP), 1)
    result = jnp.zeros((rows, GROUP), F32)
    sums = jnp.zeros((rows, 128), F32)
    lane128 = lax.broadcasted_iota(jnp.int32, (1, 128), 1)
    blocks = (pair.at[0], pair.at[1], pair_p.at[0], pair_p.at[1])
    for h in range(GROUP // HEAD_DIM):
        here = (lane // HEAD_DIM) == h
        qm = jnp.where(here, q, jnp.zeros_like(q))
        scores = [
            jnp.where(mask, dot(qm, block[0], NT), -10000.0) for mask, block in zip(masks, blocks)
        ]
        top = scores[0]
        for s in scores[1:]:
            top = jnp.maximum(top, s)
        top = jnp.max(top, axis=-1, keepdims=True)
        out = jnp.zeros((rows, GROUP), F32)
        exps = [jnp.exp(s - top) for s in scores]
        total = exps[0]
        for e in exps[1:]:
            total = total + e
        total = jnp.sum(total, axis=-1, keepdims=True)
        for e, block in zip(exps, blocks):
            out = out + dot(e.astype(BF), block[1])
        result = jnp.where(here, out * (1.0 / total), result)
        sums = jnp.where(lane128 == h, top + jnp.log(total), sums)
    low = result.astype(BF)
    attended[0] = low
    held[group] = low
    lse[0, 0] = sums.T[:8]

    @pl.when(group == pl.num_programs(0) - 1)
    def _():
        for copy in copies:
            copy.wait()
        value = own_tokens[...].astype(F32)
        for g in range(held.shape[0]):
            value = value + dot(held[g], weight[g * GROUP:(g + 1) * GROUP, :])
        hidden[0] = value
        normed, _ = normalized(value)
        second[...] = (normed * gain[...]).astype(BF)


def attend(slot, counts, live, meta, query, pair, pair_p, tokens, w_proj, gain, before):
    slots, rows, width = query.shape
    groups = width // GROUP
    at = slot
    kv_spec = pl.BlockSpec((2, 2, rows, GROUP), lambda g, *_: (0, 0, 0, g))
    piece = pl.BlockSpec((1, rows, GROUP), lambda g, *_: (at, 0, g))
    row_spec = pl.BlockSpec((1, rows, width), lambda g, *_: (at, 0, 0))
    operands = (counts, live, meta, query, pair, pair_p, tokens, w_proj, gain)
    return pl.pallas_call(
        functools.partial(attend_kernel, slot),
        out_shape=[
            jax.ShapeDtypeStruct(query.shape, BF),
            jax.ShapeDtypeStruct((slots, groups, 8, rows), F32),
            jax.ShapeDtypeStruct(query.shape, F32),
            jax.ShapeDtypeStruct((rows, width), BF),
        ],
        grid_spec=pltpu.PrefetchScalarGridSpec(
            num_scalar_prefetch=3,
            grid=(groups,),
            in_specs=[piece, kv_spec, kv_spec, HBM, HBM, pl.BlockSpec((1, width), lambda g, *_: (0, 0))]
            + [HBM] * len(before),
            out_specs=[
                piece,
                pl.BlockSpec((1, 1, 8, rows), lambda g, *_: (at, g, 0, 0)),
                row_spec,
                pl.BlockSpec((rows, width), lambda g, *_: (0, 0)),
            ],
            scratch_shapes=[
                pltpu.VMEM((groups, rows, GROUP), BF),
                pltpu.VMEM((rows, width), BF),
                pltpu.VMEM((width, width), BF),
                pltpu.SemaphoreType.DMA((2,)),
            ],
        ),
        input_output_aliases={len(operands) + i: i for i in range(len(before))},
        compiler_params=params(14),
        cost_estimate=cost(2 * 2 * rows * 4 * rows * 4 * width, 1e7, 12 * rows * 4 * rows),
        name="attend",
    )(*operands, *before)


def attend_back_kernel(
    slot, counts, live, meta, query, pair, pair_p, grad, lse, delta, *refs
):
    grad_query, grad_keep, grad_send, probs, slopes, qms, gms, keys, values, keys_t = refs[-10:]
    rows = query.shape[1]
    heads = GROUP // HEAD_DIM
    masks = key_masks(counts, live, meta, slot, rows, FLIPS, 0)
    q = query[0]
    ga = grad[0]
    lane = lax.broadcasted_iota(jnp.int32, (1, GROUP), 1)
    zero = jnp.zeros_like(q)
    for h in range(heads):
        here = (lane // HEAD_DIM) == h
        qms[h * rows:(h + 1) * rows, :] = jnp.where(here, q, zero)
        gms[h * rows:(h + 1) * rows, :] = jnp.where(here, ga, zero)
    for i, mask in enumerate(masks):
        block = (pair, pair_p)[i // 2]
        keys[i * rows:(i + 1) * rows, :] = jnp.where(mask, block[i % 2, 0], zero)
        values[i * rows:(i + 1) * rows, :] = block[i % 2, 1]
    keys_t[...] = keys[...].T
    gq = []
    for h in range(heads):
        mine = slice(h * rows, (h + 1) * rows)
        for i, mask in enumerate(masks):
            at = slice(i * rows, (i + 1) * rows)
            scores = jnp.where(mask, dot(keys[at, :], qms[mine, :], NT), -10000.0)
            gp = dot(values[at, :], gms[mine, :], NT)
            p = jnp.exp(scores - lse[0, 0, h:h + 1, :])
            probs[at, mine] = p.astype(BF)
            slopes[at, mine] = (p * (gp - delta[0, 0, h:h + 1, :])).astype(BF)
        gq.append(dot(keys_t[h * HEAD_DIM:(h + 1) * HEAD_DIM, :], slopes[:, mine]))
    gk = dot(slopes[...], qms[...])
    gv = dot(probs[...], gms[...])
    outs = ((grad_keep, 0), (grad_keep, 1), (grad_send, 0), (grad_send, 1))
    for i, ((out, place), mask) in enumerate(zip(outs, masks)):
        at = slice(i * rows, (i + 1) * rows)
        out[0, place, 0] = jnp.where(mask, gk[at], 0.0).astype(BF)
        out[0, place, 1] = gv[at].astype(BF)
    grad_query[0] = (jnp.concatenate(gq, axis=0).T * HEAD_DIM ** -0.5).astype(BF)


def attend_back(slot, counts, live, meta, query, pair, pair_p, grad, lse, delta, before):
    slots, rows, width = query.shape
    groups = width // GROUP
    heads = GROUP // HEAD_DIM
    at = slot
    kv_spec = pl.BlockSpec((2, 2, rows, GROUP), lambda g, *_: (0, 0, 0, g))
    row_spec = pl.BlockSpec((1, rows, GROUP), lambda g, *_: (at, 0, g))
    stat_spec = pl.BlockSpec((1, 1, 8, rows), lambda g, *_: (at, g, 0, 0))
    out_spec = pl.BlockSpec((1, 2, 2, rows, GROUP), lambda g, *_: (0, 0, 0, 0, g))
    operands = (counts, live, meta, query, pair, pair_p, grad, lse, delta)
    return pl.pallas_call(
        functools.partial(attend_back_kernel, slot),
        out_shape=[
            jax.ShapeDtypeStruct(query.shape, BF),
            jax.ShapeDtypeStruct((1, 2, 2, rows, width), BF),
            jax.ShapeDtypeStruct((1, 2, 2, rows, width), BF),
        ],
        grid_spec=pltpu.PrefetchScalarGridSpec(
            num_scalar_prefetch=3,
            grid=(groups,),
            in_specs=[row_spec, kv_spec, kv_spec, row_spec, stat_spec, stat_spec]
            + [pl.BlockSpec(memory_space=pl.ANY)] * len(before),
            out_specs=[row_spec, out_spec, out_spec],
            scratch_shapes=[
                pltpu.VMEM((4 * rows, heads * rows), BF),
                pltpu.VMEM((4 * rows, heads * rows), BF),
                pltpu.VMEM((heads * rows, GROUP), BF),
                pltpu.VMEM((heads * rows, GROUP), BF),
                pltpu.VMEM((4 * rows, GROUP), BF),
                pltpu.VMEM((4 * rows, GROUP), BF),
                pltpu.VMEM((GROUP, 4 * rows), BF),
            ],
        ),
        input_output_aliases={len(operands) + i: i for i in range(len(before))},
        compiler_params=params(18),
        cost_estimate=cost(5 * 2 * rows * 4 * rows * 4 * width, 2e7, 12 * rows * 4 * rows),
        name="attend_back",
    )(*operands, *before)


CHUNKS = 16


def row_mask(counts, live, meta, slot, rows):
    return key_masks(counts, live, meta, slot, rows, (0,), 0)[0]


def gelu_parts(v):
    size = jnp.abs(v)
    decay = jnp.exp2(v * v * (-0.5 * 1.4426950408889634))
    scale = 1.0 + (0.3275911 * 0.7071067811865476) * size
    t = pl.reciprocal(scale, approx=True)
    t = t * (2.0 - scale * t)
    poly = t * (0.127414796 + t * (-0.142248368 + t * (0.7107068705 + t * (-0.7265760135 + t * 0.5307027145))))
    tail = poly * decay
    phi = jnp.where(v >= 0, 1.0 - tail, tail)
    return phi, decay * 0.3989422804014327


def mlp_kernel(slots, half, counts, live, meta, *refs):
    seconds, rest = refs[:2 * slots], refs[2 * slots:]
    cot, cot_p, w_in, w_out, act_out, pre_out, *grads_out = rest[:8]
    sec, go, win, wout, act, pre, grads, sems, out_sems = rest[8:]
    rows = seconds[0].shape[0]
    count = slots * rows
    width = sec.shape[1]
    me = meta[2]
    part = pl.multiple_of((2 * meta[1] + half) * width, width)

    def copies_for(side):
        whole = pl.ds(side * count, count)
        out = [
            pltpu.make_async_copy(
                seconds[side * slots + s], sec.at[pl.ds(side * count + s * rows, rows)], sems.at[side * (slots + 1) + s]
            )
            for s in range(slots)
        ]
        source = (cot, cot_p)[side]
        return out, pltpu.make_async_copy(source, go.at[whole], sems.at[side * (slots + 1) + slots])

    last = 2 * (slots + 1)
    load_in = pltpu.make_async_copy(w_in.at[:, pl.ds(part, width)], win, sems.at[last])
    load_out = pltpu.make_async_copy(w_out.at[pl.ds(part, width), :], wout, sems.at[last + 1])
    sides = [copies_for(side) for side in range(2)]
    for c in sides[0][0]:
        c.start()
    load_in.start()
    sides[0][1].start()
    load_out.start()
    for c in sides[1][0]:
        c.start()
    sides[1][1].start()
    stores = []

    def store(source, target):
        copy = pltpu.make_async_copy(source, target, out_sems.at[len(stores)])
        copy.start()
        stores.append(copy)

    def activate(at, before, grad_act):
        phi, density = gelu_parts(before)
        act[at, :] = (before * phi).astype(BF)
        pre[at, :] = (grad_act * (phi + before * density)).astype(BF)

    own = slice(0, count)
    for c in sides[0][0]:
        c.wait()
    load_in.wait()
    before = dot(sec[own, :], win[...])
    sides[0][1].wait()
    load_out.wait()
    for c in sides[1][0]:
        c.wait()
    sides[1][1].wait()
    for side in range(2):
        for s in range(slots):
            mask = key_masks(counts, live, meta, s, rows, (side,), 0)[0]
            here = slice(side * count + s * rows, side * count + (s + 1) * rows)
            go[here, :] = jnp.where(mask, go[here, :], jnp.zeros((rows, width), BF))
    activate(own, before, dot(go[own, :], wout[...], NT))
    for s in range(slots):
        at = slice(count + s * rows, count + (s + 1) * rows)
        activate(at, dot(sec[at, :], win[...]), dot(go[at, :], wout[...], NT))
    for side in range(2):
        window = pl.ds(side * count, count)
        store(act.at[window], act_out.at[window])
        store(pre.at[window], pre_out.at[window])
    size = width // CHUNKS
    for kind, (left, right) in ((1, (act, go)), (0, (sec, pre))):
        value = dot(left[...], right[...], TN)
        for a in range(CHUNKS):
            grads[kind, a ^ me] = value[a * size:(a + 1) * size].astype(BF)
        for i, out in enumerate(grads_out):
            store(grads.at[kind, pl.ds(i * CHUNKS // 2, CHUNKS // 2)], out.at[:, kind])
    for copy in stores:
        copy.wait()


def mlp(counts, live, meta, seconds, cotangent, cotangent_p, w_fc1, w_fc2, half):
    rows, width = seconds[0].shape
    slots = len(seconds) // 2
    both = 2 * slots * rows
    operands = (*seconds, cotangent.reshape(slots * rows, width), cotangent_p.reshape(slots * rows, width), w_fc1, w_fc2)
    return pl.pallas_call(
        functools.partial(mlp_kernel, slots, half),
        out_shape=[
            pltpu.HBM((both, width), BF),
            pltpu.HBM((both, width), BF),
        ]
        + [jax.ShapeDtypeStruct((CHUNKS // 2, 2, width // CHUNKS, width), BF)] * 2,
        grid_spec=pltpu.PrefetchScalarGridSpec(
            num_scalar_prefetch=3,
            grid=(1,),
            in_specs=[HBM] * (len(operands) - 2) + [STAY] * 2,
            out_specs=[STAY] * 2 + [HBM] * 2,
            scratch_shapes=[pltpu.VMEM((both, width), BF)] * 2
            + [pltpu.VMEM((width, width), BF)] * 2
            + [pltpu.VMEM((both, width), BF)] * 2
            + [
                pltpu.VMEM((2, CHUNKS, width // CHUNKS, width), BF),
                pltpu.SemaphoreType.DMA((2 * (slots + 1) + 2,)),
                pltpu.SemaphoreType.DMA((8,)),
            ],
        ),
        compiler_params=params(20),
        cost_estimate=cost(2 * 4 * 2 * slots * rows * width * width, 2e7),
        name="mlp",
    )(counts, live, meta, *operands)


def lend_kernel(nt, meta, first, second, weight, out, left, held, sems):
    count, width = out.shape
    core = meta[1]
    loads = []
    for i, source in enumerate((first, second)):
        place = pl.ds(pl.multiple_of((2 * core + i) * width, width), width)
        loads.append(pltpu.make_async_copy(source.at[pl.ds(count, count)], left.at[i], sems.at[2 * i]))
        part = weight.at[:, place] if nt else weight.at[place, :]
        loads.append(pltpu.make_async_copy(part, held.at[i], sems.at[2 * i + 1]))
    for load in loads:
        load.start()
    dims = NT if nt else NN
    loads[0].wait()
    loads[1].wait()
    total = dot(left[0], held[0], dims)
    loads[2].wait()
    loads[3].wait()
    out[...] = (total + dot(left[1], held[1], dims)).astype(BF)


def lend(nt, meta, first, second, weight):
    both, width = first.shape
    return pl.pallas_call(
        functools.partial(lend_kernel, nt),
        out_shape=jax.ShapeDtypeStruct((both // 2, width), BF),
        grid_spec=pltpu.PrefetchScalarGridSpec(
            num_scalar_prefetch=1,
            grid=(1,),
            in_specs=[STAY] * 3,
            out_specs=pl.BlockSpec((both // 2, width), lambda i, *_: (0, 0)),
            scratch_shapes=[
                pltpu.VMEM((2, both // 2, width), BF),
                pltpu.VMEM((2, width, width), BF),
                pltpu.SemaphoreType.DMA((4,)),
            ],
        ),
        compiler_params=params(10),
        cost_estimate=cost(2 * both * width * width, 6e6),
        name="lend",
    )(meta, first, second, weight)


def layer_norm_back(values, gain, grad):
    normed, scale = normalized(values)
    t = grad * gain
    return scale * (t - jnp.mean(t, axis=-1, keepdims=True) - normed * jnp.mean(t * normed, axis=-1, keepdims=True))


def turn_kernel(
    counts, live, meta, first, second, weight, got, hidden, cotangent, attended, gain, w_proj,
    grad_branch, grad_attended, delta, left, held, got_v, hidden_v, cot_v, att_v, proj_v, sems,
):
    slots, rows, width = grad_branch.shape
    count = slots * rows
    core = meta[1]
    loads = []
    for i, source in enumerate((first, second)):
        place = pl.ds(pl.multiple_of((2 * core + i) * width, width), width)
        loads.append(pltpu.make_async_copy(source.at[pl.ds(0, count)], left.at[i], sems.at[2 * i]))
        loads.append(pltpu.make_async_copy(weight.at[:, place], held.at[i], sems.at[2 * i + 1]))
    for i, (source, target) in enumerate(
        ((got, got_v), (hidden, hidden_v), (cotangent, cot_v), (w_proj, proj_v), (attended, att_v))
    ):
        loads.append(pltpu.make_async_copy(source, target, sems.at[4 + i]))
    for load in loads:
        load.start()
    loads[0].wait()
    loads[1].wait()
    total = dot(left[0], held[0], NT)
    loads[2].wait()
    loads[3].wait()
    total = total + dot(left[1], held[1], NT)
    for load in loads[4:]:
        load.wait()
    head = lax.broadcasted_iota(jnp.int32, (32, width), 0)
    column = lax.broadcasted_iota(jnp.int32, (32, width), 1) // HEAD_DIM
    per = GROUP // HEAD_DIM
    pick = (head == (column // per) * 8 + column % per).astype(BF)
    for s in range(slots):
        here = slice(s * rows, (s + 1) * rows)
        mask = row_mask(counts, live, meta, s, rows)
        grad_out = jnp.where(mask, cot_v[s].astype(F32), 0.0)
        given = total[here] + got_v[here, :].astype(F32)
        branch = (grad_out + layer_norm_back(hidden_v[s], gain[...], given)).astype(BF)
        grad_branch[s] = branch
        back = dot(branch, proj_v[...], NT).astype(BF)
        grad_attended[s] = back
        product = back.astype(F32) * att_v[s].astype(F32)
        high = product.astype(BF)
        low = (product - high.astype(F32)).astype(BF)
        sums = dot(pick, high, NT) + dot(pick, low, NT)
        for g in range(width // GROUP):
            delta[s, g] = sums[8 * g:8 * g + 8]


def turn(counts, live, meta, first, second, weight, got, hidden, cotangent, attended, gain, w_proj):
    slots, rows, width = hidden.shape
    count = slots * rows
    groups = width // GROUP
    whole = pl.BlockSpec(hidden.shape, lambda i, *_: (0, 0, 0))
    return pl.pallas_call(
        turn_kernel,
        out_shape=[
            jax.ShapeDtypeStruct(hidden.shape, BF),
            jax.ShapeDtypeStruct(hidden.shape, BF),
            jax.ShapeDtypeStruct((slots, groups, 8, rows), F32),
        ],
        grid_spec=pltpu.PrefetchScalarGridSpec(
            num_scalar_prefetch=3,
            grid=(1,),
            in_specs=[STAY] * 3 + [HBM] * 4 + [pl.BlockSpec((1, width), lambda i, *_: (0, 0)), HBM],
            out_specs=[whole, whole, pl.BlockSpec((slots, groups, 8, rows), lambda i, *_: (0, 0, 0, 0))],
            scratch_shapes=[
                pltpu.VMEM((2, count, width), BF),
                pltpu.VMEM((2, width, width), BF),
                pltpu.VMEM((count, width), BF),
                pltpu.VMEM(hidden.shape, F32),
                pltpu.VMEM(hidden.shape, BF),
                pltpu.VMEM(hidden.shape, BF),
                pltpu.VMEM((width, width), BF),
                pltpu.SemaphoreType.DMA((9,)),
            ],
        ),
        compiler_params=params(20),
        cost_estimate=cost(3 * 2 * slots * rows * width * width, 1.5e7),
        name="turn",
    )(counts, live, meta, first, second, weight, got, hidden, cotangent, attended, gain, w_proj)


def finish_kernel(counts, live, meta, first, second, weight, got, hidden, output, left, held, got_v, hidden_v, sems):
    slots, rows, width = output.shape
    count = slots * rows
    core = meta[1]
    loads = []
    for i, source in enumerate((first, second)):
        place = pl.ds(pl.multiple_of((2 * core + i) * width, width), width)
        loads.append(pltpu.make_async_copy(source.at[pl.ds(0, count)], left.at[i], sems.at[2 * i]))
        loads.append(pltpu.make_async_copy(weight.at[place, :], held.at[i], sems.at[2 * i + 1]))
    loads.append(pltpu.make_async_copy(got, got_v, sems.at[4]))
    loads.append(pltpu.make_async_copy(hidden, hidden_v, sems.at[5]))
    for load in loads:
        load.start()
    loads[0].wait()
    loads[1].wait()
    total = dot(left[0], held[0])
    loads[2].wait()
    loads[3].wait()
    total = total + dot(left[1], held[1])
    loads[4].wait()
    loads[5].wait()
    for s in range(slots):
        here = slice(s * rows, (s + 1) * rows)
        mask = row_mask(counts, live, meta, s, rows)
        output[s] = jnp.where(mask, total[here] + got_v[here, :].astype(F32) + hidden_v[s], 0.0).astype(BF)


def finish(counts, live, meta, first, second, weight, got, hidden):
    slots, rows, width = hidden.shape
    count = slots * rows
    return pl.pallas_call(
        finish_kernel,
        out_shape=jax.ShapeDtypeStruct(hidden.shape, BF),
        grid_spec=pltpu.PrefetchScalarGridSpec(
            num_scalar_prefetch=3,
            grid=(1,),
            in_specs=[STAY] * 3 + [HBM] * 2,
            out_specs=pl.BlockSpec(hidden.shape, lambda i, *_: (0, 0, 0)),
            scratch_shapes=[
                pltpu.VMEM((2, count, width), BF),
                pltpu.VMEM((2, width, width), BF),
                pltpu.VMEM((count, width), BF),
                pltpu.VMEM(hidden.shape, F32),
                pltpu.SemaphoreType.DMA((6,)),
            ],
        ),
        compiler_params=params(16),
        cost_estimate=cost(2 * 2 * slots * rows * width * width, 9e6),
        name="finish",
    )(counts, live, meta, first, second, weight, got, hidden)


def gather_kernel(mine, got, w_kv, *refs):
    key_own, value_own, key_other, value_other, partial = refs[-5:]
    width = partial.shape[-1]
    parts = []
    for place, out in ((0, (key_own, value_own)), (1, (key_other, value_other))):
        for i in range(2):
            total = (mine[0, place, i].astype(F32) + got[0, place, i].astype(F32)).astype(BF)
            out[i][0] = total
            parts.append(total)
    partial[0] = (dot(parts[2], w_kv[:, :width], NT) + dot(parts[3], w_kv[:, width:], NT)).astype(BF)


def gather(slot, slots, mine, got, w_qkv, before):
    _, _, _, rows, width = mine.shape
    row_spec = pl.BlockSpec((1, rows, width), lambda i: (slot, 0, 0))
    kv_spec = pl.BlockSpec((1, 2, 2, rows, width), lambda i: (0, 0, 0, 0, 0))
    return pl.pallas_call(
        gather_kernel,
        out_shape=[jax.ShapeDtypeStruct((slots, rows, width), BF)] * 4 + [jax.ShapeDtypeStruct((1, rows, width), BF)],
        grid=(1,),
        in_specs=[kv_spec, kv_spec, pl.BlockSpec((pl.Element(width), pl.Element(2 * width)), lambda s: (0, width))]
        + [pl.BlockSpec(memory_space=pl.ANY)] * len(before),
        out_specs=[row_spec] * 4 + [pl.BlockSpec((1, rows, width), lambda i: (0, 0, 0))],
        input_output_aliases={3 + i: i for i in range(len(before))},
        compiler_params=params(10),
        cost_estimate=cost(2 * 2 * rows * width * width, 6e6),
        name="gather",
    )(mine, got, w_qkv, *before)


VALUE_UNITS = ((0, 4, 1, 0, 0), (1, 6, 0, 1, 0), (7, 8, 1, 1, 1))
QUERY_UNITS = ((0, 2, 1, 1, 0), (0, 3, 1, 0, 1), (1, 5, 0, 1, 1))


def weigh_steps(units):
    seen = set()
    steps = []
    for step in units:
        steps.append(step + (int(step[0] not in seen),))
        seen.add(step[0])
    return jnp.array(steps, jnp.int32)


def weigh_kernel(meta, steps, *refs):
    sources, (grads, held, total, sems) = refs[:9], refs[9:]
    step = pl.program_id(0)
    size = held.shape[1] // CHUNKS
    values = steps[0, 1] == VALUE_UNITS[0][1]

    def start(units):
        seen = []
        for unit in units:
            for i in unit[:2]:
                if i not in seen:
                    seen.append(i)
                    pltpu.make_async_copy(sources[i], held.at[i], sems.at[i]).start()

    @pl.when(jnp.logical_and(step == 0, values))
    def _():
        start(VALUE_UNITS)

    @pl.when(jnp.logical_and(step == 0, jnp.logical_not(values)))
    def _():
        start(QUERY_UNITS)

    left = steps[step, 0]
    right = steps[step, 1]

    @pl.when(steps[step, 5] == 1)
    def _():
        pltpu.make_async_copy(sources[0], held.at[left], sems.at[left]).wait()

    pltpu.make_async_copy(sources[0], held.at[right], sems.at[right]).wait()

    @pl.when(steps[step, 2] == 1)
    def _():
        total[...] = dot(held[left], held[right], TN)

    @pl.when(steps[step, 2] != 1)
    def _():
        total[...] += dot(held[left], held[right], TN)

    @pl.when(steps[step, 3] == 1)
    def _():
        unit = steps[step, 4]
        me = meta[4 + unit]
        for a in range(CHUNKS):
            grads[unit, a ^ me] = total[a * size:(a + 1) * size, :].astype(BF)


def weigh(meta, steps, arrays):
    arrays = [a.reshape(-1, a.shape[-1]) for a in arrays]
    rows, width = arrays[0].shape
    shape = (2, CHUNKS, width // CHUNKS, width)
    return pl.pallas_call(
        weigh_kernel,
        out_shape=jax.ShapeDtypeStruct(shape, BF),
        grid_spec=pltpu.PrefetchScalarGridSpec(
            num_scalar_prefetch=2,
            grid=(3,),
            in_specs=[HBM] * 9,
            out_specs=pl.BlockSpec(shape, lambda i, *_: (0, 0, 0, 0)),
            scratch_shapes=[
                pltpu.VMEM((9, rows, width), BF),
                pltpu.VMEM((rows, width), F32),
                pltpu.SemaphoreType.DMA((9,)),
            ],
        ),
        compiler_params=params(19),
        cost_estimate=cost(3 * 2 * rows * width * width, 1e7),
        name="weigh",
    )(meta, steps, *arrays)


def close_kernel(gq, gk, gv, w_qkv, tokens, grad_hidden, gain, *refs):
    partials, (out, total) = refs[:-2], refs[-2:]
    step = pl.program_id(0)
    slots, rows, width = gq.shape
    flat = (slots * rows, width)

    @pl.when(step == 0)
    def _():
        total[...] = dot(gq[...].reshape(flat), w_qkv[...], NT)

    @pl.when(step == 1)
    def _():
        total[...] += dot(gk[...].reshape(flat), w_qkv[...], NT)

    @pl.when(step == 2)
    def _():
        total[...] += dot(gv[...].reshape(flat), w_qkv[...], NT)
        for s, partial in enumerate(partials):
            total[s * rows:(s + 1) * rows, :] += partial[0].astype(F32)

    @pl.when(step > 2)
    def _():
        first = total[pl.ds(pl.multiple_of((step - 3) * rows, rows), rows), :]
        out[0] = (grad_hidden[0].astype(F32) + layer_norm_back(tokens[0].astype(F32), gain[...], first)).astype(BF)


def close(gq, gk, gv, partials, tokens, grad_hidden, gain, w_qkv):
    slots, rows, width = tokens.shape
    row_spec = pl.BlockSpec((1, rows, width), lambda i: (jnp.maximum(i - 3, 0), 0, 0))
    whole = pl.BlockSpec((slots, rows, width), lambda i: (0, 0, 0))
    return pl.pallas_call(
        close_kernel,
        out_shape=jax.ShapeDtypeStruct(tokens.shape, BF),
        grid=(3 + slots,),
        in_specs=[whole] * 3 + [pl.BlockSpec((width, width), lambda i: (0, jnp.minimum(i, 2)))] + [row_spec] * 2 + [
            pl.BlockSpec((1, width), lambda i: (0, 0)),
        ] + [pl.BlockSpec((1, rows, width), lambda i: (0, 0, 0))] * slots,
        out_specs=row_spec,
        scratch_shapes=[pltpu.VMEM((slots * rows, width), F32)],
        compiler_params=params(18),
        cost_estimate=cost(3 * 2 * slots * rows * width * width, 1.2e7),
        name="close",
    )(gq, gk, gv, w_qkv, tokens, grad_hidden, gain, *partials)


SPREAD = 4


def keep_row_sums(held, value):
    step = pl.program_id(0)
    rows = value.shape[0]
    column = jnp.sum(value, axis=-1, keepdims=True)
    held[pl.ds(pl.multiple_of(step * rows, rows), rows), :] = jnp.broadcast_to(column, (rows, 128))


def put_row_sums(norm, held, gain):
    @pl.when(pl.program_id(0) == pl.num_programs(0) - 1)
    def _():
        for r in range(norm.shape[0]):
            norm[r:r + 1, :] = held[r * 128:(r + 1) * 128, :].T[:1] / gain[r:r + 1, :]


def load_pieces(groups, targets, sems):
    copies = []
    for group, target in zip(groups, targets):
        place = 0
        for piece in group:
            size = piece.shape[0]
            copies.append(pltpu.make_async_copy(piece, target.at[pl.ds(place, size)], sems.at[len(copies)]))
            place += size
    for copy in copies:
        copy.start()
    for copy in copies:
        copy.wait()


def spread_mlp_kernel(meta, *refs):
    pieces, (w_fc1, gain, grad_fc1, grad_fc2, norm, one, two, held, sems) = refs[:6], refs[6:]
    step = pl.program_id(0)
    size, width = one.shape[-2:]

    @pl.when(step == 0)
    def _():
        own_one, own_two, own_rest, part_one, part_two, part_rest = pieces
        groups = ((own_one,), (part_one,), (own_two, own_rest), (part_two, part_rest))
        load_pieces(groups, (one.at[0], one.at[1], two.at[0], two.at[1]), sems)

    z = (step // 2) ^ meta[7]
    y = (step % 2) ^ meta[6]
    for a in range(4):
        w = (a // 2) ^ meta[8]
        x = (a % 2) ^ meta[3]
        here = slice(a * size, (a + 1) * size)
        for core in range(2):
            at = core ^ meta[1]
            first = one[at, x * 8 + z * 4 + y * 2 + w].astype(F32)
            second = two[at, y * 8 + z * 4 + x * 2 + w].astype(F32)
            for place, value in ((2 * core, first), (2 * core + 1, second)):
                grad_fc1[here, place * width:(place + 1) * width] = value[0]
                grad_fc2[place, here, :] = value[1]
    keep_row_sums(held, grad_fc1[...] * w_fc1[...].astype(F32))
    put_row_sums(norm, held, gain)


def spread_mlp(meta, pieces, w_fc1, gain):
    width, hidden_width = w_fc1.shape
    per = CHUNKS // SPREAD
    size = width // CHUNKS
    outs = pl.pallas_call(
        spread_mlp_kernel,
        out_shape=[
            jax.ShapeDtypeStruct((width, hidden_width), F32),
            jax.ShapeDtypeStruct((4, width, width), F32),
            jax.ShapeDtypeStruct((width // 128, 128), F32),
        ],
        grid_spec=pltpu.PrefetchScalarGridSpec(
            num_scalar_prefetch=1,
            grid=(SPREAD,),
            in_specs=[HBM] * 6 + [
                pl.BlockSpec((per * size, hidden_width), lambda a, *_: (a, 0)),
                pl.BlockSpec((width // 128, 128), lambda a, *_: (0, 0)),
            ],
            out_specs=[
                pl.BlockSpec((per * size, hidden_width), lambda a, *_: (a, 0)),
                pl.BlockSpec((4, per * size, width), lambda a, *_: (0, a, 0)),
                pl.BlockSpec((width // 128, 128), lambda a, *_: (0, 0)),
            ],
            scratch_shapes=[
                pltpu.VMEM((2, CHUNKS, 2, size, width), BF),
                pltpu.VMEM((2, CHUNKS, 2, size, width), BF),
                pltpu.VMEM((width, 128), F32),
                pltpu.SemaphoreType.DMA((6,)),
            ],
        ),
        compiler_params=params(26),
        cost_estimate=cost(1e6, 4.7e7),
        name="spread_mlp",
    )(meta, *pieces, w_fc1, gain.reshape(width // 128, 128))
    return outs[0], outs[1].reshape(hidden_width, width), outs[2].reshape(width)


def spread_qkv_kernel(meta, *refs):
    pieces, (w_qkv, gain, grad_qkv, grad_proj, norm, chunks, held, sems) = refs[:8], refs[8:]
    step = pl.program_id(0)
    size, width = chunks.shape[-2:]

    @pl.when(step == 0)
    def _():
        load_pieces([pieces[2 * i:2 * i + 2] for i in range(4)], [chunks.at[i] for i in range(4)], sems)

    high, low = step // 2, step % 2
    tops = (((high ^ meta[3]) * 2 + (low ^ meta[6])) * 4, ((high ^ meta[6]) * 2 + (low ^ meta[3])) * 4)
    own = 2 * meta[1]
    part = 2 - own
    for a in range(4):
        here = slice(a * size, (a + 1) * size)
        last = a ^ (meta[7] * 2 + meta[8])
        for i in range(3):
            unit = i % 2
            grad_qkv[here, i * width:(i + 1) * width] = chunks[
                (own if i < 2 else part) + unit, tops[unit] + last
            ].astype(F32)
        grad_proj[here, :] = chunks[part + 1, tops[1] + last].astype(F32)
    keep_row_sums(held, grad_qkv[...] * w_qkv[...].astype(F32))
    put_row_sums(norm, held, gain)


def spread_qkv(meta, pieces, w_qkv, gain):
    width = w_qkv.shape[0]
    size = width // CHUNKS
    per = CHUNKS // SPREAD

    def rows(columns):
        return pl.BlockSpec((per * size, columns), lambda a, *_: (a, 0))

    line = pl.BlockSpec((width // 128, 128), lambda a, *_: (0, 0))
    outs = pl.pallas_call(
        spread_qkv_kernel,
        out_shape=[
            jax.ShapeDtypeStruct((width, 3 * width), F32),
            jax.ShapeDtypeStruct((width, width), F32),
            jax.ShapeDtypeStruct((width // 128, 128), F32),
        ],
        grid_spec=pltpu.PrefetchScalarGridSpec(
            num_scalar_prefetch=1,
            grid=(SPREAD,),
            in_specs=[HBM] * 8 + [rows(3 * width), line],
            out_specs=[rows(3 * width), rows(width), line],
            scratch_shapes=[
                pltpu.VMEM((4, CHUNKS, size, width), BF),
                pltpu.VMEM((width, 128), F32),
                pltpu.SemaphoreType.DMA((8,)),
            ],
        ),
        compiler_params=params(18),
        cost_estimate=cost(1e6, 1.8e7),
        name="spread_qkv",
    )(meta, *pieces, w_qkv, gain.reshape(width // 128, 128))
    return outs[0], outs[1], outs[2].reshape(width)


DIGITS = {"x": (0, 2), "y": (1, 0), "z": (2, 0), "w": (4, 0)}


def swap(value, axis, mask):
    return lax.ppermute(value, axis, [(i, i ^ mask) for i in range(lax.axis_size(axis))])


def swap_digits(value, masks):
    batch, band = masks
    if not band:
        return swap(value, "batch", batch)
    if not batch:
        return swap(value, "band", band)
    return swap(value, ("batch", "band"), batch * lax.axis_size("band") + band)


def add(*values):
    total = values[0].astype(F32)
    for value in values[1:]:
        total = total + value.astype(F32)
    return total.astype(BF)


def pack_kernel(groups, *refs):
    total = sum(count for count, _ in groups)
    sources, refs = refs[:total], refs[total:]
    outs = sum(1 + split for _, split in groups)
    targets, refs = list(refs[:outs]), refs[outs:]
    held, (sems, out_sems) = refs[:len(groups)], refs[len(groups):]
    loads, stores = [], []
    for group, (count, split) in enumerate(groups):
        mine = [targets.pop(0) for _ in range(1 + split)]
        for i in range(count):
            at = len(loads)
            size = sources[at].shape[0]
            here = pl.ds(i * size, size)
            loads.append(pltpu.make_async_copy(sources[at], held[group].at[here], sems.at[at]))
            stores.append([
                pltpu.make_async_copy(
                    held[group].at[here, j] if split else held[group].at[here], target.at[here], out_sems.at[at, j]
                )
                for j, target in enumerate(mine)
            ])
    for load in loads:
        load.start()
    for load, store in zip(loads, stores):
        load.wait()
        for copy in store:
            copy.start()
    for store in stores:
        for copy in store:
            copy.wait()


def pack(*groups):
    shapes = [(len(parts) * parts[0].shape[0],) + parts[0].shape[1:] for parts, _ in groups]
    out = []
    for shape, (_, split) in zip(shapes, groups):
        out += [shape[:1] + shape[2:]] * 2 if split else [shape]
    parts = [p for group, _ in groups for p in group]
    return list(pl.pallas_call(
        functools.partial(pack_kernel, [(len(p), int(split)) for p, split in groups]),
        out_shape=[jax.ShapeDtypeStruct(o, BF) for o in out],
        in_specs=[HBM] * len(parts),
        out_specs=[HBM] * len(out),
        scratch_shapes=[pltpu.VMEM(shape, BF) for shape in shapes]
        + [pltpu.SemaphoreType.DMA((len(parts),)), pltpu.SemaphoreType.DMA((len(parts), 2))],
        compiler_params=params(12),
        cost_estimate=cost(0, 2e6),
        name="pack",
    )(*parts))


class Line:
    def __init__(self):
        self.mark = None

    def tie(self, value):
        if self.mark is None:
            return value
        value, self.mark = lax.optimization_barrier((value, self.mark))
        return value


class Chain:
    def __init__(self, terms=(), halves=(), upper=None, pieces=(), joins=()):
        self.terms = list(terms)
        self.upper = upper
        self.pieces = list(pieces)
        self.steps = [("part", group) for group in halves] + [("join", group) for group in joins]

    def masks(self, group):
        count = 1 << len(group)
        masks = []
        for place in range(1, count):
            digits = [DIGITS[d] for i, d in enumerate(group) if place & (count >> (i + 1))]
            masks.append((sum(d[0] for d in digits), sum(d[1] for d in digits)))
        return masks

    def total_here(self):
        return add(*self.terms)

    def total(self):
        value = add(*self.terms)
        mask = 8
        while mask < lax.axis_size("batch"):
            value = add(value, swap(value, "batch", mask))
            mask *= 2
        return value

    def offers(self):
        kind, what = self.steps[0]
        if kind == "join":
            return self.pieces
        if self.upper is not None:
            sent, self.upper = [self.upper], None
            return sent
        count = 1 << len(what)
        size = self.terms[0].shape[0] // count
        sent = [add(*[t[i * size:(i + 1) * size] for t in self.terms]) for i in range(1, count)]
        self.terms = [t[:size] for t in self.terms]
        return sent

    def start(self, sent):
        kind, what = self.steps[0]
        masks = self.masks(what)
        if kind == "join":
            return [swap_digits(s, mask) for mask in masks for s in sent]
        return [swap_digits(s, mask) for s, mask in zip(sent, masks)]

    def take(self, moved):
        kind, _ = self.steps.pop(0)
        if kind == "join":
            self.pieces = self.pieces + list(moved)
        else:
            self.terms = self.terms + list(moved)


class Flight:
    def __init__(self, line):
        self.line = line
        self.parts = {}

    def land(self, *names):
        names = [n for n in (names or tuple(self.parts)) if n in self.parts]
        if not names:
            return {}
        held = [self.parts.pop(n) for n in names]
        got = self.line.tie(held)
        self.line.mark = got
        for name, moved in zip(names, got):
            if isinstance(name, Chain):
                name.take(moved)
        return {n: g for n, g in zip(names, got) if not isinstance(n, Chain)}

    def launch(self, *items):
        items = [i for i in items if not isinstance(i, Chain) or i.steps]
        arrays = [i.offers() if isinstance(i, Chain) else list(i[1]) for i in items]
        arrays = self.line.tie(arrays)
        self.line.mark = arrays
        for item, sent in zip(items, arrays):
            if isinstance(item, Chain):
                self.parts[item] = item.start(sent)
            else:
                name, _, axis, mask = item
                self.parts[name] = [swap(a, axis, mask) for a in sent]


def place_in(order):
    place = 0
    for digit in "".join(order):
        batch, band = DIGITS[digit]
        bit = lax.axis_index("batch") // batch if batch else lax.axis_index("band") // band
        place = place * 2 + bit % 2
    return place


ORDER = ("z", "y", "wx")
LAST_ORDERS = (("x", "y"), ("y", "x"))


def body(
    tokens, w_qkv, w_proj, w_fc1, w_fc2, gain_one, gain_two, cotangent, band_counts, slot_live
):
    slots, rows, width = tokens.shape
    flat = (slots * rows, width)
    band = lax.axis_index("band")
    core = band % 2
    meta = jnp.stack(
        [band, core] + [place_in(o) for o in (ORDER, "x") + tuple(order + ("zw",) for order in LAST_ORDERS) + ("y", "z", "w")]
    ).astype(jnp.int32)
    gain_one = gain_one[None]
    gain_two = gain_two[None]
    at = (band_counts, slot_live, meta)
    line = Line()

    tokens, *tokens_other = lax.optimization_barrier(
        (tokens,) + tuple(tokens[s:s + 1] for s in range(slots))
    )
    tokens_other = [swap(t, "band", 2) for t in tokens_other]
    cotangent_p = swap(cotangent, "band", 1)
    first_own, query, kv_own = project(tokens, w_qkv, gain_one)
    tables = weigh_steps(QUERY_UNITS), weigh_steps(VALUE_UNITS)
    steps_theirs = jnp.where(core == 1, *tables)
    steps_ours = jnp.where(core == 0, *tables)
    line.mark = (first_own, meta, gain_two, steps_theirs, steps_ours)
    first_other, pairs = [], []
    seconds, seconds_p = [], []
    kept = ()

    def take(s):
        first, pair = project_other(s, line.tie(tokens_other[s]), kv_own, w_qkv, gain_one, first_other)
        line.mark = pair
        first_other[:] = [first]
        pairs.append((pair, swap(pair, "band", 1)))

    def look(s):
        *out, second = attend(s, *at, line.tie(query), *pairs[s], tokens, w_proj, gain_two, kept)
        line.mark = second
        seconds.append(second)
        seconds_p.append(swap(second, "band", 1))
        return tuple(out)

    take(0)
    for s in range(slots):
        if s == 1:
            for n in range(1, slots):
                take(n)
            cotangent_p = line.tie(cotangent_p)
        kept = look(s)
    attended, lse, hidden = kept

    flight = Flight(line)
    chains = []
    acts, pres = [], []
    all_seconds = seconds + seconds_p
    for half in range(2):
        act, pre, lower, upper = mlp(
            *at, [line.tie(all_seconds[0])] + all_seconds[1:], cotangent, cotangent_p, w_fc1, w_fc2, half
        )
        line.mark = upper
        acts.append(act)
        pres.append(pre)
        chains.append(Chain((lower,), ORDER, upper))
        if half == 0:
            flight.launch(chains[0])
    one, two = chains
    turn_part = lend(True, meta, line.tie(pres[0]), pres[1], w_fc1)
    line.mark = turn_part
    finish_part = lend(False, meta, line.tie(acts[0]), acts[1], w_fc2)
    line.mark = finish_part
    flight.land()
    flight.launch(("turn", [turn_part], "band", 1), two, one, ("finish", [finish_part], "band", 1))
    got = flight.land("turn")
    branch, grad_attended, delta = turn(
        *at, line.tie(pres[0]), pres[1], w_fc1, got["turn"][0], hidden, cotangent, attended, gain_two, w_proj
    )
    line.mark = delta

    grad_query, sums, keeps, waiting = (), (), [], []

    def bring(s):
        *kept_sums, partial = gather(s, slots, line.tie(keeps[s]), got[f"send{s}"][0], w_qkv, sums)
        line.mark = partial
        return tuple(kept_sums), [(f"partial{s}", [partial], "band", 2)]

    for s in range(slots):
        query_grad, keep, send = attend_back(
            s, *at, line.tie(query), *pairs[s], grad_attended, lse, delta, grad_query
        )
        line.mark = send
        grad_query = (query_grad,)
        keeps.append(keep)
        got.update(flight.land())
        if s < slots - 1:
            flight.launch((f"send{s}", [send], "band", 1), two, one)
            if s > 0:
                sums, waiting = bring(s - 1)
                flight.launch(*waiting)
    both = Chain(pieces=[jnp.stack([one.total(), two.total()], axis=1)], joins=("w",))
    flight.launch((f"send{slots - 1}", [send], "band", 1), both)
    if slots > 1:
        sums, waiting = bring(slots - 2)
        flight.launch(*waiting)
    got.update(flight.land(f"send{slots - 1}"))
    sums, waiting = bring(slots - 1)
    arrays = (first_own, first_other[0], grad_query[0], *sums, attended, branch)
    theirs = weigh(meta, steps_theirs, (line.tie(first_own),) + arrays[1:])
    line.mark = theirs

    got.update(flight.land())
    left, right = pack((both.pieces, True))
    one = Chain(pieces=[left], joins=("y", "z", "x"))
    two = Chain(pieces=[right], joins=("x", "z", "y"))
    flight.launch(("theirs", [theirs], "band", 1), one, two)
    ours = weigh(meta, steps_ours, (line.tie(first_own),) + arrays[1:])
    line.mark = ours

    got.update(flight.land())
    (theirs,) = got["theirs"]
    three = Chain((ours[0], theirs[0]), LAST_ORDERS[0])
    four = Chain((ours[1], theirs[1]), LAST_ORDERS[1])
    left, right = pack((one.pieces, False), (two.pieces, False))
    one.pieces, two.pieces = [left], [right]
    flight.launch(three, four, one, two, *waiting)
    output = finish(*at, line.tie(acts[0]), acts[1], w_fc2, got["finish"][0], hidden)
    line.mark = output

    flight.land(three, four)
    flight.launch(three, four)

    got.update(flight.land(one, two, f"partial{slots - 1}"))
    left, right = pack((one.pieces, False), (two.pieces, False))
    one.pieces, two.pieces = [left], [right]
    line.mark = (left, right)
    flight.land(three, four)
    five = Chain((jnp.stack([three.total_here(), four.total_here()], axis=1),), ("zw",))
    flight.launch(five, one, two)
    partials = [got[f"partial{s}"][0] for s in range(slots)]
    grad_input = close(
        line.tie(grad_query[0]), sums[0], sums[1], partials, tokens, branch, gain_one, w_qkv
    )
    line.mark = grad_input

    flight.land(five)
    five = Chain(pieces=[five.total()], joins=("zw",))
    flight.launch(five)

    flight.land(one, two)
    flight.land(five)
    *halves, whole = pack((five.pieces, True), (one.pieces, False))
    three = Chain(pieces=halves[:1], joins=("y", "x"))
    four = Chain(pieces=halves[1:], joins=("x", "y"))
    flight.launch(three, four, ("one", [whole], "band", 1), ("two_held", two.pieces[:1], "band", 1))

    got.update(flight.land())
    held = pack((three.pieces, False), (four.pieces, False))
    three.pieces, four.pieces = held[:1], held[1:]
    flight.launch(three, four, ("two_rest", two.pieces[1:], "band", 1), ("qkv_held", held, "band", 1))
    got.update(flight.land("two_rest"))
    mlp_pieces = [line.tie(whole), *two.pieces, got["one"][0], got["two_held"][0], got["two_rest"][0]]
    grad_fc1, grad_fc2, norm2 = spread_mlp(meta, mlp_pieces, w_fc1, gain_two)
    line.mark = norm2

    got.update(flight.land())
    flight.launch(("qkv_rest", [three.pieces[1], four.pieces[1]], "band", 1))
    got.update(flight.land())
    last_pieces = three.pieces + four.pieces + [p for pair in zip(got["qkv_held"], got["qkv_rest"]) for p in pair]
    grad_qkv, grad_proj, norm1 = spread_qkv(meta, last_pieces, w_qkv, gain_one)
    return (output, grad_input, grad_qkv, grad_proj, grad_fc1, grad_fc2, norm1, norm2)


def solution(mesh):
    placed = (
        P("batch", "band", None),
        P(),
        P(),
        P(),
        P(),
        P(),
        P(),
        P("batch", "band", None),
        P("batch", None),
        P("batch"),
    )
    return jax.shard_map(
        body,
        mesh=mesh,
        in_specs=placed,
        out_specs=(
            P("batch", "band", None),
            P("batch", "band", None),
            P(),
            P(),
            P(),
            P(),
            P(),
            P(),
        ),
        check_vma=False,
    )
```

```python
import functools
import jax
import jax.numpy as jnp
from jax import lax
from jax.experimental import pallas as pl
from jax.experimental.pallas import tpu as pltpu
from jax.sharding import PartitionSpec as P

BF = jnp.bfloat16
F32 = jnp.float32
EPSILON = 1e-06
HEAD_DIM = 64
GROUP = 256
NN = (((1,), (0,)), ((), ()))
NT = (((1,), (1,)), ((), ()))
TN = (((0,), (0,)), ((), ()))


def dot(left, right, dims=NN):
    return lax.dot_general(left, right, dims, preferred_element_type=F32)


def params(mib=60):
    return pltpu.CompilerParams(vmem_limit_bytes=mib * 1024 * 1024)


def cost(flops, moved, exps=0):
    return pl.CostEstimate(flops=1, bytes_accessed=1, transcendentals=0)


HBM = pl.BlockSpec(memory_space=pl.ANY)
STAY = pl.BlockSpec(memory_space=pltpu.HBM)


def normalized(values):
    centered = values - jnp.mean(values, axis=-1, keepdims=True)
    spread = jnp.mean(centered * centered, axis=-1, keepdims=True)
    scale = lax.rsqrt(spread + EPSILON)
    return centered * scale, scale


def project_kernel(tokens, weight, gain, first_in, query, both):
    normed, _ = normalized(tokens[0].astype(F32))
    first = (normed * gain[...]).astype(BF)
    first_in[0] = first
    width = first.shape[1]
    query[0] = (dot(first, weight[:, :width]) * HEAD_DIM ** -0.5).astype(BF)
    both[0, 0] = dot(first, weight[:, width:2 * width]).astype(BF)
    both[0, 1] = dot(first, weight[:, 2 * width:]).astype(BF)


def project(tokens, w_qkv, gain):
    slots, rows, width = tokens.shape
    row_spec = pl.BlockSpec((1, rows, width), lambda s: (s, 0, 0))
    return pl.pallas_call(
        project_kernel,
        out_shape=[
            pltpu.HBM(tokens.shape, BF),
            jax.ShapeDtypeStruct(tokens.shape, BF),
            jax.ShapeDtypeStruct((slots, 2, rows, width), BF),
        ],
        grid=(slots,),
        in_specs=[
            row_spec,
            pl.BlockSpec((width, 3 * width), lambda s: (0, 0)),
            pl.BlockSpec((1, width), lambda s: (0, 0)),
        ],
        out_specs=[row_spec, row_spec, pl.BlockSpec((1, 2, rows, width), lambda s: (s, 0, 0, 0))],
        compiler_params=params(14),
        cost_estimate=cost(2 * slots * rows * width * width * 3, 8e6),
        name="project",
    )(tokens, w_qkv, gain)


def project_other_kernel(tokens, own, weight, gain, *refs):
    first_in, both = refs[-2:]
    normed, _ = normalized(tokens[0].astype(F32))
    first = (normed * gain[...]).astype(BF)
    first_in[0] = first
    width = first.shape[1]
    both[0] = own[0]
    both[1, 0] = dot(first, weight[:, :width]).astype(BF)
    both[1, 1] = dot(first, weight[:, width:]).astype(BF)


def project_other(slot, tokens, kv_own, w_qkv, gain, before):
    slots, _, rows, width = kv_own.shape
    return pl.pallas_call(
        project_other_kernel,
        out_shape=[
            jax.ShapeDtypeStruct((slots, rows, width), BF),
            jax.ShapeDtypeStruct((2, 2, rows, width), BF),
        ],
        grid=(1,),
        in_specs=[
            pl.BlockSpec((1, rows, width), lambda i: (0, 0, 0)),
            pl.BlockSpec((1, 2, rows, width), lambda i: (slot, 0, 0, 0)),
            pl.BlockSpec((pl.Element(width), pl.Element(2 * width)), lambda i: (0, width)),
            pl.BlockSpec((1, width), lambda i: (0, 0)),
        ] + [HBM] * len(before),
        out_specs=[
            pl.BlockSpec((1, rows, width), lambda i: (slot, 0, 0)),
            pl.BlockSpec((2, 2, rows, width), lambda i: (0, 0, 0, 0)),
        ],
        input_output_aliases={4 + i: i for i in range(len(before))},
        compiler_params=params(10),
        cost_estimate=cost(2 * rows * width * width * 2, 5e6),
        name="project_other",
    )(tokens, kv_own, w_qkv, gain, *before)


def key_masks(counts, live, meta, slot, rows, flips, axis):
    shape = (rows, 1) if axis == 0 else (1, rows)
    place = lax.broadcasted_iota(jnp.int32, shape, axis)
    alive = live[slot] > 0
    return [place < jnp.where(alive, counts[slot, meta[0] ^ flip], 0) for flip in flips]


FLIPS = (0, 2, 1, 3)


def attend_kernel(slot, counts, live, meta, query, pair, pair_p, tokens, w_proj, gain, *refs):
    attended, lse, hidden, second, held, own_tokens, weight, sems = refs[-8:]
    group = pl.program_id(0)
    rows = query.shape[1]
    copies = (
        pltpu.make_async_copy(tokens.at[slot], own_tokens, sems.at[0]),
        pltpu.make_async_copy(w_proj, weight, sems.at[1]),
    )

    @pl.when(group == 0)
    def _():
        for copy in copies:
            copy.start()

    masks = key_masks(counts, live, meta, slot, rows, FLIPS, 1)
    q = query[0]
    lane = lax.broadcasted_iota(jnp.int32, (1, GROUP), 1)
    result = jnp.zeros((rows, GROUP), F32)
    sums = jnp.zeros((rows, 128), F32)
    lane128 = lax.broadcasted_iota(jnp.int32, (1, 128), 1)
    blocks = (pair.at[0], pair.at[1], pair_p.at[0], pair_p.at[1])
    for h in range(GROUP // HEAD_DIM):
        here = (lane // HEAD_DIM) == h
        qm = jnp.where(here, q, jnp.zeros_like(q))
        scores = [
            jnp.where(mask, dot(qm, block[0], NT), -10000.0) for mask, block in zip(masks, blocks)
        ]
        top = scores[0]
        for s in scores[1:]:
            top = jnp.maximum(top, s)
        top = jnp.max(top, axis=-1, keepdims=True)
        out = jnp.zeros((rows, GROUP), F32)
        exps = [jnp.exp(s - top) for s in scores]
        total = exps[0]
        for e in exps[1:]:
            total = total + e
        total = jnp.sum(total, axis=-1, keepdims=True)
        for e, block in zip(exps, blocks):
            out = out + dot(e.astype(BF), block[1])
        result = jnp.where(here, out * (1.0 / total), result)
        sums = jnp.where(lane128 == h, top + jnp.log(total), sums)
    low = result.astype(BF)
    attended[0] = low
    held[group] = low
    lse[0, 0] = sums.T[:8]

    @pl.when(group == pl.num_programs(0) - 1)
    def _():
        for copy in copies:
            copy.wait()
        value = own_tokens[...].astype(F32)
        for g in range(held.shape[0]):
            value = value + dot(held[g], weight[g * GROUP:(g + 1) * GROUP, :])
        hidden[0] = value
        normed, _ = normalized(value)
        second[...] = (normed * gain[...]).astype(BF)


def attend(slot, counts, live, meta, query, pair, pair_p, tokens, w_proj, gain, before):
    slots, rows, width = query.shape
    groups = width // GROUP
    at = slot
    kv_spec = pl.BlockSpec((2, 2, rows, GROUP), lambda g, *_: (0, 0, 0, g))
    piece = pl.BlockSpec((1, rows, GROUP), lambda g, *_: (at, 0, g))
    row_spec = pl.BlockSpec((1, rows, width), lambda g, *_: (at, 0, 0))
    operands = (counts, live, meta, query, pair, pair_p, tokens, w_proj, gain)
    return pl.pallas_call(
        functools.partial(attend_kernel, slot),
        out_shape=[
            jax.ShapeDtypeStruct(query.shape, BF),
            jax.ShapeDtypeStruct((slots, groups, 8, rows), F32),
            jax.ShapeDtypeStruct(query.shape, F32),
            jax.ShapeDtypeStruct((rows, width), BF),
        ],
        grid_spec=pltpu.PrefetchScalarGridSpec(
            num_scalar_prefetch=3,
            grid=(groups,),
            in_specs=[piece, kv_spec, kv_spec, HBM, HBM, pl.BlockSpec((1, width), lambda g, *_: (0, 0))]
            + [HBM] * len(before),
            out_specs=[
                piece,
                pl.BlockSpec((1, 1, 8, rows), lambda g, *_: (at, g, 0, 0)),
                row_spec,
                pl.BlockSpec((rows, width), lambda g, *_: (0, 0)),
            ],
            scratch_shapes=[
                pltpu.VMEM((groups, rows, GROUP), BF),
                pltpu.VMEM((rows, width), BF),
                pltpu.VMEM((width, width), BF),
                pltpu.SemaphoreType.DMA((2,)),
            ],
        ),
        input_output_aliases={len(operands) + i: i for i in range(len(before))},
        compiler_params=params(14),
        cost_estimate=cost(2 * 2 * rows * 4 * rows * 4 * width, 1e7, 12 * rows * 4 * rows),
        name="attend",
    )(*operands, *before)


def attend_back_kernel(
    slot, counts, live, meta, query, pair, pair_p, grad, lse, delta, *refs
):
    grad_query, grad_keep, grad_send, probs, slopes, qms, gms, keys, values, keys_t = refs[-10:]
    rows = query.shape[1]
    heads = GROUP // HEAD_DIM
    masks = key_masks(counts, live, meta, slot, rows, FLIPS, 0)
    q = query[0]
    ga = grad[0]
    lane = lax.broadcasted_iota(jnp.int32, (1, GROUP), 1)
    zero = jnp.zeros_like(q)
    for h in range(heads):
        here = (lane // HEAD_DIM) == h
        qms[h * rows:(h + 1) * rows, :] = jnp.where(here, q, zero)
        gms[h * rows:(h + 1) * rows, :] = jnp.where(here, ga, zero)
    for i, mask in enumerate(masks):
        block = (pair, pair_p)[i // 2]
        keys[i * rows:(i + 1) * rows, :] = jnp.where(mask, block[i % 2, 0], zero)
        values[i * rows:(i + 1) * rows, :] = block[i % 2, 1]
    keys_t[...] = keys[...].T
    gq = []
    for h in range(heads):
        mine = slice(h * rows, (h + 1) * rows)
        for i, mask in enumerate(masks):
            at = slice(i * rows, (i + 1) * rows)
            scores = jnp.where(mask, dot(keys[at, :], qms[mine, :], NT), -10000.0)
            gp = dot(values[at, :], gms[mine, :], NT)
            p = jnp.exp(scores - lse[0, 0, h:h + 1, :])
            probs[at, mine] = p.astype(BF)
            slopes[at, mine] = (p * (gp - delta[0, 0, h:h + 1, :])).astype(BF)
        gq.append(dot(keys_t[h * HEAD_DIM:(h + 1) * HEAD_DIM, :], slopes[:, mine]))
    gk = dot(slopes[...], qms[...])
    gv = dot(probs[...], gms[...])
    outs = ((grad_keep, 0), (grad_keep, 1), (grad_send, 0), (grad_send, 1))
    for i, ((out, place), mask) in enumerate(zip(outs, masks)):
        at = slice(i * rows, (i + 1) * rows)
        out[0, place, 0] = jnp.where(mask, gk[at], 0.0).astype(BF)
        out[0, place, 1] = gv[at].astype(BF)
    grad_query[0] = (jnp.concatenate(gq, axis=0).T * HEAD_DIM ** -0.5).astype(BF)


def attend_back(slot, counts, live, meta, query, pair, pair_p, grad, lse, delta, before):
    slots, rows, width = query.shape
    groups = width // GROUP
    heads = GROUP // HEAD_DIM
    at = slot
    kv_spec = pl.BlockSpec((2, 2, rows, GROUP), lambda g, *_: (0, 0, 0, g))
    row_spec = pl.BlockSpec((1, rows, GROUP), lambda g, *_: (at, 0, g))
    stat_spec = pl.BlockSpec((1, 1, 8, rows), lambda g, *_: (at, g, 0, 0))
    out_spec = pl.BlockSpec((1, 2, 2, rows, GROUP), lambda g, *_: (0, 0, 0, 0, g))
    operands = (counts, live, meta, query, pair, pair_p, grad, lse, delta)
    return pl.pallas_call(
        functools.partial(attend_back_kernel, slot),
        out_shape=[
            jax.ShapeDtypeStruct(query.shape, BF),
            jax.ShapeDtypeStruct((1, 2, 2, rows, width), BF),
            jax.ShapeDtypeStruct((1, 2, 2, rows, width), BF),
        ],
        grid_spec=pltpu.PrefetchScalarGridSpec(
            num_scalar_prefetch=3,
            grid=(groups,),
            in_specs=[row_spec, kv_spec, kv_spec, row_spec, stat_spec, stat_spec]
            + [pl.BlockSpec(memory_space=pl.ANY)] * len(before),
            out_specs=[row_spec, out_spec, out_spec],
            scratch_shapes=[
                pltpu.VMEM((4 * rows, heads * rows), BF),
                pltpu.VMEM((4 * rows, heads * rows), BF),
                pltpu.VMEM((heads * rows, GROUP), BF),
                pltpu.VMEM((heads * rows, GROUP), BF),
                pltpu.VMEM((4 * rows, GROUP), BF),
                pltpu.VMEM((4 * rows, GROUP), BF),
                pltpu.VMEM((GROUP, 4 * rows), BF),
            ],
        ),
        input_output_aliases={len(operands) + i: i for i in range(len(before))},
        compiler_params=params(18),
        cost_estimate=cost(5 * 2 * rows * 4 * rows * 4 * width, 2e7, 12 * rows * 4 * rows),
        name="attend_back",
    )(*operands, *before)


CHUNKS = 16


def row_mask(counts, live, meta, slot, rows):
    return key_masks(counts, live, meta, slot, rows, (0,), 0)[0]


def gelu_parts(v):
    size = jnp.abs(v)
    decay = jnp.exp2(v * v * (-0.5 * 1.4426950408889634))
    scale = 1.0 + (0.3275911 * 0.7071067811865476) * size
    t = pl.reciprocal(scale, approx=True)
    t = t * (2.0 - scale * t)
    poly = t * (0.127414796 + t * (-0.142248368 + t * (0.7107068705 + t * (-0.7265760135 + t * 0.5307027145))))
    tail = poly * decay
    phi = jnp.where(v >= 0, 1.0 - tail, tail)
    return phi, decay * 0.3989422804014327


def mlp_kernel(slots, half, counts, live, meta, *refs):
    seconds, rest = refs[:2 * slots], refs[2 * slots:]
    cot, cot_p, w_in, w_out, act_out, pre_out, *grads_out = rest[:8]
    sec, go, win, wout, act, pre, grads, sems, out_sems = rest[8:]
    rows = seconds[0].shape[0]
    count = slots * rows
    width = sec.shape[1]
    me = meta[2 + half]
    part = pl.multiple_of((2 * meta[1] + half) * width, width)

    def copies_for(side):
        whole = pl.ds(side * count, count)
        out = [
            pltpu.make_async_copy(
                seconds[side * slots + s], sec.at[pl.ds(side * count + s * rows, rows)], sems.at[side * (slots + 1) + s]
            )
            for s in range(slots)
        ]
        source = (cot, cot_p)[side]
        return out, pltpu.make_async_copy(source, go.at[whole], sems.at[side * (slots + 1) + slots])

    last = 2 * (slots + 1)
    load_in = pltpu.make_async_copy(w_in.at[:, pl.ds(part, width)], win, sems.at[last])
    load_out = pltpu.make_async_copy(w_out.at[pl.ds(part, width), :], wout, sems.at[last + 1])
    sides = [copies_for(side) for side in range(2)]
    for c in sides[0][0]:
        c.start()
    load_in.start()
    sides[0][1].start()
    load_out.start()
    for c in sides[1][0]:
        c.start()
    sides[1][1].start()
    stores = []

    def store(source, target):
        copy = pltpu.make_async_copy(source, target, out_sems.at[len(stores)])
        copy.start()
        stores.append(copy)

    def activate(at, before, grad_act):
        phi, density = gelu_parts(before)
        act[at, :] = (before * phi).astype(BF)
        pre[at, :] = (grad_act * (phi + before * density)).astype(BF)

    own = slice(0, count)
    for c in sides[0][0]:
        c.wait()
    load_in.wait()
    before = dot(sec[own, :], win[...])
    sides[0][1].wait()
    load_out.wait()
    for c in sides[1][0]:
        c.wait()
    sides[1][1].wait()
    for side in range(2):
        for s in range(slots):
            mask = key_masks(counts, live, meta, s, rows, (side,), 0)[0]
            here = slice(side * count + s * rows, side * count + (s + 1) * rows)
            go[here, :] = jnp.where(mask, go[here, :], jnp.zeros((rows, width), BF))
    activate(own, before, dot(go[own, :], wout[...], NT))
    for s in range(slots):
        at = slice(count + s * rows, count + (s + 1) * rows)
        activate(at, dot(sec[at, :], win[...]), dot(go[at, :], wout[...], NT))
    for side in range(2):
        window = pl.ds(side * count, count)
        store(act.at[window], act_out.at[window])
        store(pre.at[window], pre_out.at[window])
    size = width // CHUNKS
    for kind, (left, right) in ((1, (act, go)), (0, (sec, pre))):
        value = dot(left[...], right[...], TN)
        for a in range(CHUNKS):
            grads[kind, a ^ me] = value[a * size:(a + 1) * size].astype(BF)
        for i, out in enumerate(grads_out):
            store(grads.at[kind, pl.ds(i * CHUNKS // 2, CHUNKS // 2)], out.at[:, kind])
    for copy in stores:
        copy.wait()


def mlp(counts, live, meta, seconds, cotangent, cotangent_p, w_fc1, w_fc2, half):
    rows, width = seconds[0].shape
    slots = len(seconds) // 2
    both = 2 * slots * rows
    operands = (*seconds, cotangent.reshape(slots * rows, width), cotangent_p.reshape(slots * rows, width), w_fc1, w_fc2)
    return pl.pallas_call(
        functools.partial(mlp_kernel, slots, half),
        out_shape=[
            pltpu.HBM((both, width), BF),
            pltpu.HBM((both, width), BF),
        ]
        + [jax.ShapeDtypeStruct((CHUNKS // 2, 2, width // CHUNKS, width), BF)] * 2,
        grid_spec=pltpu.PrefetchScalarGridSpec(
            num_scalar_prefetch=3,
            grid=(1,),
            in_specs=[HBM] * (len(operands) - 2) + [STAY] * 2,
            out_specs=[STAY] * 2 + [HBM] * 2,
            scratch_shapes=[pltpu.VMEM((both, width), BF)] * 2
            + [pltpu.VMEM((width, width), BF)] * 2
            + [pltpu.VMEM((both, width), BF)] * 2
            + [
                pltpu.VMEM((2, CHUNKS, width // CHUNKS, width), BF),
                pltpu.SemaphoreType.DMA((2 * (slots + 1) + 2,)),
                pltpu.SemaphoreType.DMA((8,)),
            ],
        ),
        compiler_params=params(24),
        cost_estimate=cost(2 * 4 * 2 * slots * rows * width * width, 2e7),
        name="mlp",
    )(counts, live, meta, *operands)


def lend_kernel(nt, meta, first, second, weight, *refs):
    outs, (left, held, sems) = refs[:-3], refs[-3:]
    _, count, width = left.shape
    core = meta[1]
    loads = []
    for i, source in enumerate((first, second)):
        place = pl.ds(pl.multiple_of((2 * core + i) * width, width), width)
        loads.append(pltpu.make_async_copy(source.at[pl.ds(count, count)], left.at[i], sems.at[2 * i]))
        part = weight.at[:, place] if nt else weight.at[place, :]
        loads.append(pltpu.make_async_copy(part, held.at[i], sems.at[2 * i + 1]))
    for load in loads:
        load.start()
    dims = NT if nt else NN
    loads[0].wait()
    loads[1].wait()
    total = dot(left[0], held[0], dims)
    loads[2].wait()
    loads[3].wait()
    total = (total + dot(left[1], held[1], dims)).astype(BF)
    size = count // len(outs)
    for i, out in enumerate(outs):
        out[...] = total[i * size:(i + 1) * size]


def lend(nt, parts, meta, first, second, weight):
    both, width = first.shape
    size = both // 2 // parts
    return pl.pallas_call(
        functools.partial(lend_kernel, nt),
        out_shape=[jax.ShapeDtypeStruct((size, width), BF)] * parts,
        grid_spec=pltpu.PrefetchScalarGridSpec(
            num_scalar_prefetch=1,
            grid=(1,),
            in_specs=[STAY] * 3,
            out_specs=[pl.BlockSpec((size, width), lambda i, *_: (0, 0))] * parts,
            scratch_shapes=[
                pltpu.VMEM((2, both // 2, width), BF),
                pltpu.VMEM((2, width, width), BF),
                pltpu.SemaphoreType.DMA((4,)),
            ],
        ),
        compiler_params=params(10),
        cost_estimate=cost(2 * both * width * width, 6e6),
        name="lend",
    )(meta, first, second, weight)


def layer_norm_back(values, gain, grad):
    normed, scale = normalized(values)
    t = grad * gain
    return scale * (t - jnp.mean(t, axis=-1, keepdims=True) - normed * jnp.mean(t * normed, axis=-1, keepdims=True))


def turn_kernel(
    counts, live, meta, first, second, weight, got, also, hidden, cotangent, attended, gain, w_proj,
    grad_branch, grad_attended, delta, left, held, got_v, hidden_v, cot_v, att_v, proj_v, sems,
):
    slots, rows, width = grad_branch.shape
    count = slots * rows
    core = meta[1]
    loads = []
    for i, source in enumerate((first, second)):
        place = pl.ds(pl.multiple_of((2 * core + i) * width, width), width)
        loads.append(pltpu.make_async_copy(source.at[pl.ds(0, count)], left.at[i], sems.at[2 * i]))
        loads.append(pltpu.make_async_copy(weight.at[:, place], held.at[i], sems.at[2 * i + 1]))
    for i, (source, target) in enumerate(
        (
            (got, got_v.at[pl.ds(0, count // 2)]), (also, got_v.at[pl.ds(count // 2, count // 2)]),
            (hidden, hidden_v), (cotangent, cot_v), (w_proj, proj_v), (attended, att_v),
        )
    ):
        loads.append(pltpu.make_async_copy(source, target, sems.at[4 + i]))
    for load in loads:
        load.start()
    loads[0].wait()
    loads[1].wait()
    total = dot(left[0], held[0], NT)
    loads[2].wait()
    loads[3].wait()
    total = total + dot(left[1], held[1], NT)
    for load in loads[4:]:
        load.wait()
    head = lax.broadcasted_iota(jnp.int32, (32, width), 0)
    column = lax.broadcasted_iota(jnp.int32, (32, width), 1) // HEAD_DIM
    per = GROUP // HEAD_DIM
    pick = (head == (column // per) * 8 + column % per).astype(BF)
    for s in range(slots):
        here = slice(s * rows, (s + 1) * rows)
        mask = row_mask(counts, live, meta, s, rows)
        grad_out = jnp.where(mask, cot_v[s].astype(F32), 0.0)
        given = total[here] + got_v[here, :].astype(F32)
        branch = (grad_out + layer_norm_back(hidden_v[s], gain[...], given)).astype(BF)
        grad_branch[s] = branch
        back = dot(branch, proj_v[...], NT).astype(BF)
        grad_attended[s] = back
        product = back.astype(F32) * att_v[s].astype(F32)
        high = product.astype(BF)
        low = (product - high.astype(F32)).astype(BF)
        sums = dot(pick, high, NT) + dot(pick, low, NT)
        for g in range(width // GROUP):
            delta[s, g] = sums[8 * g:8 * g + 8]


def turn(counts, live, meta, first, second, weight, got, also, hidden, cotangent, attended, gain, w_proj):
    slots, rows, width = hidden.shape
    count = slots * rows
    groups = width // GROUP
    whole = pl.BlockSpec(hidden.shape, lambda i, *_: (0, 0, 0))
    return pl.pallas_call(
        turn_kernel,
        out_shape=[
            jax.ShapeDtypeStruct(hidden.shape, BF),
            jax.ShapeDtypeStruct(hidden.shape, BF),
            jax.ShapeDtypeStruct((slots, groups, 8, rows), F32),
        ],
        grid_spec=pltpu.PrefetchScalarGridSpec(
            num_scalar_prefetch=3,
            grid=(1,),
            in_specs=[STAY] * 3 + [HBM] * 5 + [pl.BlockSpec((1, width), lambda i, *_: (0, 0)), HBM],
            out_specs=[whole, whole, pl.BlockSpec((slots, groups, 8, rows), lambda i, *_: (0, 0, 0, 0))],
            scratch_shapes=[
                pltpu.VMEM((2, count, width), BF),
                pltpu.VMEM((2, width, width), BF),
                pltpu.VMEM((count, width), BF),
                pltpu.VMEM(hidden.shape, F32),
                pltpu.VMEM(hidden.shape, BF),
                pltpu.VMEM(hidden.shape, BF),
                pltpu.VMEM((width, width), BF),
                pltpu.SemaphoreType.DMA((10,)),
            ],
        ),
        compiler_params=params(20),
        cost_estimate=cost(3 * 2 * slots * rows * width * width, 1.5e7),
        name="turn",
    )(counts, live, meta, first, second, weight, got, also, hidden, cotangent, attended, gain, w_proj)


def finish_kernel(counts, live, meta, first, second, weight, got, hidden, output, left, held, got_v, hidden_v, sems):
    slots, rows, width = output.shape
    count = slots * rows
    core = meta[1]
    loads = []
    for i, source in enumerate((first, second)):
        place = pl.ds(pl.multiple_of((2 * core + i) * width, width), width)
        loads.append(pltpu.make_async_copy(source.at[pl.ds(0, count)], left.at[i], sems.at[2 * i]))
        loads.append(pltpu.make_async_copy(weight.at[place, :], held.at[i], sems.at[2 * i + 1]))
    loads.append(pltpu.make_async_copy(got, got_v, sems.at[4]))
    loads.append(pltpu.make_async_copy(hidden, hidden_v, sems.at[5]))
    for load in loads:
        load.start()
    loads[0].wait()
    loads[1].wait()
    total = dot(left[0], held[0])
    loads[2].wait()
    loads[3].wait()
    total = total + dot(left[1], held[1])
    loads[4].wait()
    loads[5].wait()
    for s in range(slots):
        here = slice(s * rows, (s + 1) * rows)
        mask = row_mask(counts, live, meta, s, rows)
        output[s] = jnp.where(mask, total[here] + got_v[here, :].astype(F32) + hidden_v[s], 0.0).astype(BF)


def finish(counts, live, meta, first, second, weight, got, hidden):
    slots, rows, width = hidden.shape
    count = slots * rows
    return pl.pallas_call(
        finish_kernel,
        out_shape=jax.ShapeDtypeStruct(hidden.shape, BF),
        grid_spec=pltpu.PrefetchScalarGridSpec(
            num_scalar_prefetch=3,
            grid=(1,),
            in_specs=[STAY] * 3 + [HBM] * 2,
            out_specs=pl.BlockSpec(hidden.shape, lambda i, *_: (0, 0, 0)),
            scratch_shapes=[
                pltpu.VMEM((2, count, width), BF),
                pltpu.VMEM((2, width, width), BF),
                pltpu.VMEM((count, width), BF),
                pltpu.VMEM(hidden.shape, F32),
                pltpu.SemaphoreType.DMA((6,)),
            ],
        ),
        compiler_params=params(16),
        cost_estimate=cost(2 * 2 * slots * rows * width * width, 9e6),
        name="finish",
    )(counts, live, meta, first, second, weight, got, hidden)


def gather_kernel(mine, got, w_kv, *refs):
    key_own, value_own, key_other, value_other, partial = refs[-5:]
    width = partial.shape[-1]
    parts = []
    for place, out in ((0, (key_own, value_own)), (1, (key_other, value_other))):
        for i in range(2):
            total = (mine[0, place, i].astype(F32) + got[0, place, i].astype(F32)).astype(BF)
            out[i][0] = total
            parts.append(total)
    partial[0] = (dot(parts[2], w_kv[:, :width], NT) + dot(parts[3], w_kv[:, width:], NT)).astype(BF)


def gather(slot, slots, mine, got, w_qkv, before):
    _, _, _, rows, width = mine.shape
    row_spec = pl.BlockSpec((1, rows, width), lambda i: (slot, 0, 0))
    kv_spec = pl.BlockSpec((1, 2, 2, rows, width), lambda i: (0, 0, 0, 0, 0))
    return pl.pallas_call(
        gather_kernel,
        out_shape=[jax.ShapeDtypeStruct((slots, rows, width), BF)] * 4 + [jax.ShapeDtypeStruct((1, rows, width), BF)],
        grid=(1,),
        in_specs=[kv_spec, kv_spec, pl.BlockSpec((pl.Element(width), pl.Element(2 * width)), lambda s: (0, width))]
        + [pl.BlockSpec(memory_space=pl.ANY)] * len(before),
        out_specs=[row_spec] * 4 + [pl.BlockSpec((1, rows, width), lambda i: (0, 0, 0))],
        input_output_aliases={3 + i: i for i in range(len(before))},
        compiler_params=params(10),
        cost_estimate=cost(2 * 2 * rows * width * width, 6e6),
        name="gather",
    )(mine, got, w_qkv, *before)


VALUE_UNITS = ((0, 4, 1, 0, 0), (1, 6, 0, 1, 0), (7, 8, 1, 1, 1))
QUERY_UNITS = ((0, 2, 1, 1, 0), (0, 3, 1, 0, 1), (1, 5, 0, 1, 1))


def weigh_steps(units):
    seen = set()
    steps = []
    for step in units:
        steps.append(step + (int(step[0] not in seen),))
        seen.add(step[0])
    return jnp.array(steps, jnp.int32)


def weigh_kernel(meta, steps, *refs):
    sources, (grads, held, total, sems) = refs[:9], refs[9:]
    step = pl.program_id(0)
    size = held.shape[1] // CHUNKS
    values = steps[0, 1] == VALUE_UNITS[0][1]

    def start(units):
        seen = []
        for unit in units:
            for i in unit[:2]:
                if i not in seen:
                    seen.append(i)
                    pltpu.make_async_copy(sources[i], held.at[i], sems.at[i]).start()

    @pl.when(jnp.logical_and(step == 0, values))
    def _():
        start(VALUE_UNITS)

    @pl.when(jnp.logical_and(step == 0, jnp.logical_not(values)))
    def _():
        start(QUERY_UNITS)

    left = steps[step, 0]
    right = steps[step, 1]

    @pl.when(steps[step, 5] == 1)
    def _():
        pltpu.make_async_copy(sources[0], held.at[left], sems.at[left]).wait()

    pltpu.make_async_copy(sources[0], held.at[right], sems.at[right]).wait()

    @pl.when(steps[step, 2] == 1)
    def _():
        total[...] = dot(held[left], held[right], TN)

    @pl.when(steps[step, 2] != 1)
    def _():
        total[...] += dot(held[left], held[right], TN)

    @pl.when(steps[step, 3] == 1)
    def _():
        unit = steps[step, 4]
        me = meta[4 + unit]
        for a in range(CHUNKS):
            grads[unit, a ^ me] = total[a * size:(a + 1) * size, :].astype(BF)


def weigh(meta, steps, arrays):
    arrays = [a.reshape(-1, a.shape[-1]) for a in arrays]
    rows, width = arrays[0].shape
    shape = (2, CHUNKS, width // CHUNKS, width)
    return pl.pallas_call(
        weigh_kernel,
        out_shape=jax.ShapeDtypeStruct(shape, BF),
        grid_spec=pltpu.PrefetchScalarGridSpec(
            num_scalar_prefetch=2,
            grid=(3,),
            in_specs=[HBM] * 9,
            out_specs=pl.BlockSpec(shape, lambda i, *_: (0, 0, 0, 0)),
            scratch_shapes=[
                pltpu.VMEM((9, rows, width), BF),
                pltpu.VMEM((rows, width), F32),
                pltpu.SemaphoreType.DMA((9,)),
            ],
        ),
        compiler_params=params(19),
        cost_estimate=cost(3 * 2 * rows * width * width, 1e7),
        name="weigh",
    )(meta, steps, *arrays)


def close_kernel(gq, gk, gv, w_qkv, tokens, grad_hidden, gain, *refs):
    partials, (out, total) = refs[:-2], refs[-2:]
    step = pl.program_id(0)
    slots, rows, width = gq.shape
    flat = (slots * rows, width)

    @pl.when(step == 0)
    def _():
        total[...] = dot(gq[...].reshape(flat), w_qkv[...], NT)

    @pl.when(step == 1)
    def _():
        total[...] += dot(gk[...].reshape(flat), w_qkv[...], NT)

    @pl.when(step == 2)
    def _():
        total[...] += dot(gv[...].reshape(flat), w_qkv[...], NT)
        for s, partial in enumerate(partials):
            total[s * rows:(s + 1) * rows, :] += partial[0].astype(F32)

    @pl.when(step > 2)
    def _():
        first = total[pl.ds(pl.multiple_of((step - 3) * rows, rows), rows), :]
        out[0] = (grad_hidden[0].astype(F32) + layer_norm_back(tokens[0].astype(F32), gain[...], first)).astype(BF)


def close(gq, gk, gv, partials, tokens, grad_hidden, gain, w_qkv):
    slots, rows, width = tokens.shape
    row_spec = pl.BlockSpec((1, rows, width), lambda i: (jnp.maximum(i - 3, 0), 0, 0))
    whole = pl.BlockSpec((slots, rows, width), lambda i: (0, 0, 0))
    return pl.pallas_call(
        close_kernel,
        out_shape=jax.ShapeDtypeStruct(tokens.shape, BF),
        grid=(3 + slots,),
        in_specs=[whole] * 3 + [pl.BlockSpec((width, width), lambda i: (0, jnp.minimum(i, 2)))] + [row_spec] * 2 + [
            pl.BlockSpec((1, width), lambda i: (0, 0)),
        ] + [pl.BlockSpec((1, rows, width), lambda i: (0, 0, 0))] * slots,
        out_specs=row_spec,
        scratch_shapes=[pltpu.VMEM((slots * rows, width), F32)],
        compiler_params=params(18),
        cost_estimate=cost(3 * 2 * slots * rows * width * width, 1.2e7),
        name="close",
    )(gq, gk, gv, w_qkv, tokens, grad_hidden, gain, *partials)


SPREAD = 4


def keep_row_sums(held, value):
    step = pl.program_id(0)
    rows = value.shape[0]
    column = jnp.sum(value, axis=-1, keepdims=True)
    held[pl.ds(pl.multiple_of(step * rows, rows), rows), :] = jnp.broadcast_to(column, (rows, 128))


def put_row_sums(norm, held, gain):
    @pl.when(pl.program_id(0) == pl.num_programs(0) - 1)
    def _():
        for r in range(norm.shape[0]):
            norm[r:r + 1, :] = held[r * 128:(r + 1) * 128, :].T[:1] / gain[r:r + 1, :]


def load_pieces(groups, targets, sems):
    copies = []
    for group, target in zip(groups, targets):
        place = 0
        for piece in group:
            size = piece.shape[0]
            copies.append(pltpu.make_async_copy(piece, target.at[pl.ds(place, size)], sems.at[len(copies)]))
            place += size
    for copy in copies:
        copy.start()
    for copy in copies:
        copy.wait()


def spread_mlp_kernel(meta, *refs):
    pieces, (w_fc1, gain, grad_fc1, grad_fc2, norm, one, two, held, sems) = refs[:6], refs[6:]
    step = pl.program_id(0)
    size, width = one.shape[-2:]

    @pl.when(step == 0)
    def _():
        own_one, own_two, own_rest, part_one, part_two, part_rest = pieces
        groups = ((own_one,), (part_one,), (own_two, own_rest), (part_two, part_rest))
        load_pieces(groups, (one.at[0], one.at[1], two.at[0], two.at[1]), sems)

    mine = [meta[6 + i] for i in range(4)]
    for a in range(4):
        here = slice(a * size, (a + 1) * size)
        for half, held_chunks in enumerate((one, two)):
            high, low, third, fourth = step // 2, step % 2, a // 2, a % 2
            digits = (low, third, high, fourth) if half == 0 else (low, high, third, fourth)
            x, y, z, w = [d ^ m for d, m in zip(digits, mine)]
            place = x * 8 + z * 4 + y * 2 + w if half == 0 else y * 8 + z * 4 + x * 2 + w
            for core in range(2):
                value = held_chunks[core ^ meta[1], place].astype(F32)
                column = 2 * core + half
                grad_fc1[here, column * width:(column + 1) * width] = value[0]
                grad_fc2[column, here, :] = value[1]
    keep_row_sums(held, grad_fc1[...] * w_fc1[...].astype(F32))
    put_row_sums(norm, held, gain)


def spread_mlp(meta, pieces, w_fc1, gain):
    width, hidden_width = w_fc1.shape
    per = CHUNKS // SPREAD
    size = width // CHUNKS
    outs = pl.pallas_call(
        spread_mlp_kernel,
        out_shape=[
            jax.ShapeDtypeStruct((width, hidden_width), F32),
            jax.ShapeDtypeStruct((4, width, width), F32),
            jax.ShapeDtypeStruct((width // 128, 128), F32),
        ],
        grid_spec=pltpu.PrefetchScalarGridSpec(
            num_scalar_prefetch=1,
            grid=(SPREAD,),
            in_specs=[HBM] * 6 + [
                pl.BlockSpec((per * size, hidden_width), lambda a, *_: (a, 0)),
                pl.BlockSpec((width // 128, 128), lambda a, *_: (0, 0)),
            ],
            out_specs=[
                pl.BlockSpec((per * size, hidden_width), lambda a, *_: (a, 0)),
                pl.BlockSpec((4, per * size, width), lambda a, *_: (0, a, 0)),
                pl.BlockSpec((width // 128, 128), lambda a, *_: (0, 0)),
            ],
            scratch_shapes=[
                pltpu.VMEM((2, CHUNKS, 2, size, width), BF),
                pltpu.VMEM((2, CHUNKS, 2, size, width), BF),
                pltpu.VMEM((width, 128), F32),
                pltpu.SemaphoreType.DMA((6,)),
            ],
        ),
        compiler_params=params(26),
        cost_estimate=cost(1e6, 4.7e7),
        name="spread_mlp",
    )(meta, *pieces, w_fc1, gain.reshape(width // 128, 128))
    return outs[0], outs[1].reshape(hidden_width, width), outs[2].reshape(width)


def spread_qkv_kernel(meta, *refs):
    pieces, (w_qkv, gain, grad_qkv, grad_proj, norm, chunks, held, sems) = refs[:8], refs[8:]
    step = pl.program_id(0)
    size, width = chunks.shape[-2:]

    @pl.when(step == 0)
    def _():
        load_pieces([pieces[2 * i:2 * i + 2] for i in range(4)], [chunks.at[i] for i in range(4)], sems)

    high, low = step // 2, step % 2
    tops = (((high ^ meta[6]) * 2 + (low ^ meta[7])) * 4, ((high ^ meta[7]) * 2 + (low ^ meta[6])) * 4)
    own = 2 * meta[1]
    part = 2 - own
    for a in range(4):
        here = slice(a * size, (a + 1) * size)
        last = a ^ (meta[8] * 2 + meta[9])
        for i in range(3):
            unit = i % 2
            grad_qkv[here, i * width:(i + 1) * width] = chunks[
                (own if i < 2 else part) + unit, tops[unit] + last
            ].astype(F32)
        grad_proj[here, :] = chunks[part + 1, tops[1] + last].astype(F32)
    keep_row_sums(held, grad_qkv[...] * w_qkv[...].astype(F32))
    put_row_sums(norm, held, gain)


def spread_qkv(meta, pieces, w_qkv, gain):
    width = w_qkv.shape[0]
    size = width // CHUNKS
    per = CHUNKS // SPREAD

    def rows(columns):
        return pl.BlockSpec((per * size, columns), lambda a, *_: (a, 0))

    line = pl.BlockSpec((width // 128, 128), lambda a, *_: (0, 0))
    outs = pl.pallas_call(
        spread_qkv_kernel,
        out_shape=[
            jax.ShapeDtypeStruct((width, 3 * width), F32),
            jax.ShapeDtypeStruct((width, width), F32),
            jax.ShapeDtypeStruct((width // 128, 128), F32),
        ],
        grid_spec=pltpu.PrefetchScalarGridSpec(
            num_scalar_prefetch=1,
            grid=(SPREAD,),
            in_specs=[HBM] * 8 + [rows(3 * width), line],
            out_specs=[rows(3 * width), rows(width), line],
            scratch_shapes=[
                pltpu.VMEM((4, CHUNKS, size, width), BF),
                pltpu.VMEM((width, 128), F32),
                pltpu.SemaphoreType.DMA((8,)),
            ],
        ),
        compiler_params=params(18),
        cost_estimate=cost(1e6, 1.8e7),
        name="spread_qkv",
    )(meta, *pieces, w_qkv, gain.reshape(width // 128, 128))
    return outs[0], outs[1], outs[2].reshape(width)


DIGITS = {"x": (0, 2), "y": (1, 0), "z": (2, 0), "w": (4, 0)}


def swap(value, axis, mask):
    return lax.ppermute(value, axis, [(i, i ^ mask) for i in range(lax.axis_size(axis))])


def swap_digits(value, masks):
    batch, band = masks
    if not band:
        return swap(value, "batch", batch)
    if not batch:
        return swap(value, "band", band)
    return swap(value, ("batch", "band"), batch * lax.axis_size("band") + band)


def add(*values):
    total = values[0].astype(F32)
    for value in values[1:]:
        total = total + value.astype(F32)
    return total.astype(BF)


def pack_kernel(groups, *refs):
    total = sum(count for count, _ in groups)
    sources, refs = refs[:total], refs[total:]
    outs = sum(1 + split for _, split in groups)
    targets, refs = list(refs[:outs]), refs[outs:]
    held, (sems, out_sems) = refs[:len(groups)], refs[len(groups):]
    loads, stores = [], []
    for group, (count, split) in enumerate(groups):
        mine = [targets.pop(0) for _ in range(1 + split)]
        for i in range(count):
            at = len(loads)
            size = sources[at].shape[0]
            here = pl.ds(i * size, size)
            loads.append(pltpu.make_async_copy(sources[at], held[group].at[here], sems.at[at]))
            stores.append([
                pltpu.make_async_copy(
                    held[group].at[here, j] if split else held[group].at[here], target.at[here], out_sems.at[at, j]
                )
                for j, target in enumerate(mine)
            ])
    for load in loads:
        load.start()
    for load, store in zip(loads, stores):
        load.wait()
        for copy in store:
            copy.start()
    for store in stores:
        for copy in store:
            copy.wait()


def pack(*groups):
    shapes = [(len(parts) * parts[0].shape[0],) + parts[0].shape[1:] for parts, _ in groups]
    out = []
    for shape, (_, split) in zip(shapes, groups):
        out += [shape[:1] + shape[2:]] * 2 if split else [shape]
    parts = [p for group, _ in groups for p in group]
    return list(pl.pallas_call(
        functools.partial(pack_kernel, [(len(p), int(split)) for p, split in groups]),
        out_shape=[jax.ShapeDtypeStruct(o, BF) for o in out],
        in_specs=[HBM] * len(parts),
        out_specs=[HBM] * len(out),
        scratch_shapes=[pltpu.VMEM(shape, BF) for shape in shapes]
        + [pltpu.SemaphoreType.DMA((len(parts),)), pltpu.SemaphoreType.DMA((len(parts), 2))],
        compiler_params=params(12),
        cost_estimate=cost(0, 2e6),
        name="pack",
    )(*parts))


class Line:
    def __init__(self):
        self.mark = None

    def tie(self, value):
        if self.mark is None:
            return value
        value, self.mark = lax.optimization_barrier((value, self.mark))
        return value


class Chain:
    def __init__(self, terms=(), halves=(), upper=None, pieces=(), joins=()):
        self.terms = list(terms)
        self.upper = upper
        self.pieces = list(pieces)
        self.steps = [("part", group) for group in halves] + [("join", group) for group in joins]

    def masks(self, group):
        count = 1 << len(group)
        masks = []
        for place in range(1, count):
            digits = [DIGITS[d] for i, d in enumerate(group) if place & (count >> (i + 1))]
            masks.append((sum(d[0] for d in digits), sum(d[1] for d in digits)))
        return masks

    def total_here(self):
        return add(*self.terms)

    def total(self):
        value = add(*self.terms)
        mask = 8
        while mask < lax.axis_size("batch"):
            value = add(value, swap(value, "batch", mask))
            mask *= 2
        return value

    def offers(self):
        kind, what = self.steps[0]
        if kind == "join":
            return self.pieces
        if self.upper is not None:
            sent, self.upper = [self.upper], None
            return sent
        count = 1 << len(what)
        size = self.terms[0].shape[0] // count
        sent = [add(*[t[i * size:(i + 1) * size] for t in self.terms]) for i in range(1, count)]
        self.terms = [t[:size] for t in self.terms]
        return sent

    def start(self, sent):
        kind, what = self.steps[0]
        masks = self.masks(what)
        if kind == "join":
            return [swap_digits(s, mask) for mask in masks for s in sent]
        return [swap_digits(s, mask) for s, mask in zip(sent, masks)]

    def take(self, moved):
        kind, _ = self.steps.pop(0)
        if kind == "join":
            self.pieces = self.pieces + list(moved)
        else:
            self.terms = self.terms + list(moved)


class Flight:
    def __init__(self, line):
        self.line = line
        self.parts = {}

    def land(self, *names):
        names = [n for n in (names or tuple(self.parts)) if n in self.parts]
        if not names:
            return {}
        held = [self.parts.pop(n) for n in names]
        got = self.line.tie(held)
        self.line.mark = got
        for name, moved in zip(names, got):
            if isinstance(name, Chain):
                name.take(moved)
        return {n: g for n, g in zip(names, got) if not isinstance(n, Chain)}

    def launch(self, *items):
        items = [i for i in items if not isinstance(i, Chain) or i.steps]
        arrays = [i.offers() if isinstance(i, Chain) else list(i[1]) for i in items]
        arrays = self.line.tie(arrays)
        self.line.mark = arrays
        for item, sent in zip(items, arrays):
            if isinstance(item, Chain):
                self.parts[item] = item.start(sent)
            else:
                name, _, axis, mask = item
                self.parts[name] = [swap(a, axis, mask) for a in sent]


def place_in(order):
    place = 0
    for digit in "".join(order):
        batch, band = DIGITS[digit]
        bit = lax.axis_index("batch") // batch if batch else lax.axis_index("band") // band
        place = place * 2 + bit % 2
    return place


ORDERS = (("z", "x", "yw"), ("y", "x", "zw"))
LAST_ORDERS = (("x", "y"), ("y", "x"))


def body(
    tokens, w_qkv, w_proj, w_fc1, w_fc2, gain_one, gain_two, cotangent, band_counts, slot_live
):
    slots, rows, width = tokens.shape
    flat = (slots * rows, width)
    band = lax.axis_index("band")
    core = band % 2
    meta = jnp.stack(
        [band, core] + [place_in(o) for o in ORDERS + tuple(order + ("zw",) for order in LAST_ORDERS) + ("x", "y", "z", "w")]
    ).astype(jnp.int32)
    gain_one = gain_one[None]
    gain_two = gain_two[None]
    at = (band_counts, slot_live, meta)
    line = Line()

    tokens, *tokens_other = lax.optimization_barrier(
        (tokens,) + tuple(tokens[s:s + 1] for s in range(slots))
    )
    tokens_other = [swap(t, "band", 2) for t in tokens_other]
    cotangent_p = swap(cotangent, "band", 1)
    first_own, query, kv_own = project(tokens, w_qkv, gain_one)
    tables = weigh_steps(QUERY_UNITS), weigh_steps(VALUE_UNITS)
    steps_theirs = jnp.where(core == 1, *tables)
    steps_ours = jnp.where(core == 0, *tables)
    line.mark = (first_own, meta, gain_two, steps_theirs, steps_ours)
    first_other, pairs = [], []
    seconds, seconds_p = [], []
    kept = ()

    def take(s):
        first, pair = project_other(s, line.tie(tokens_other[s]), kv_own, w_qkv, gain_one, first_other)
        line.mark = pair
        first_other[:] = [first]
        pairs.append((pair, swap(pair, "band", 1)))

    def look(s):
        *out, second = attend(s, *at, line.tie(query), *pairs[s], tokens, w_proj, gain_two, kept)
        line.mark = second
        seconds.append(second)
        seconds_p.append(swap(second, "band", 1))
        return tuple(out)

    take(0)
    for s in range(slots):
        if s == 1:
            for n in range(1, slots):
                take(n)
            cotangent_p = line.tie(cotangent_p)
        kept = look(s)
    attended, lse, hidden = kept

    flight = Flight(line)
    chains = []
    acts, pres = [], []
    all_seconds = seconds + seconds_p
    for half in range(2):
        act, pre, lower, upper = mlp(
            *at, [line.tie(all_seconds[0])] + all_seconds[1:], cotangent, cotangent_p, w_fc1, w_fc2, half
        )
        line.mark = upper
        acts.append(act)
        pres.append(pre)
        chains.append(Chain((lower,), ORDERS[half], upper))
        flight.launch(chains[half])
    one, two = chains
    turn_parts = lend(True, 2, meta, line.tie(pres[0]), pres[1], w_fc1)
    line.mark = turn_parts
    flight.launch(("turn", turn_parts, "band", 1))
    got = flight.land("turn")
    flight.land(one)
    flight.launch(one)
    branch, grad_attended, delta = turn(
        *at, line.tie(pres[0]), pres[1], w_fc1, *got["turn"], hidden, cotangent, attended, gain_two, w_proj
    )
    line.mark = delta

    grad_query, sums, keeps, waiting = (), (), [], []

    def bring(s):
        *kept_sums, partial = gather(s, slots, line.tie(keeps[s]), got[f"send{s}"][0], w_qkv, sums)
        line.mark = partial
        return tuple(kept_sums), [(f"partial{s}", [partial], "band", 2)]

    for s in range(slots):
        query_grad, keep, send = attend_back(
            s, *at, line.tie(query), *pairs[s], grad_attended, lse, delta, grad_query
        )
        line.mark = send
        grad_query = (query_grad,)
        keeps.append(keep)
        got.update(flight.land())
        if s < slots - 1:
            flight.launch((f"send{s}", [send], "band", 1), two, one)
            if s > 0:
                sums, waiting = bring(s - 1)
                flight.launch(*waiting)
    both = Chain(pieces=[jnp.stack([one.total(), two.total()], axis=1)], joins=("w",))
    flight.launch((f"send{slots - 1}", [send], "band", 1), both)
    if slots > 1:
        sums, waiting = bring(slots - 2)
        flight.launch(*waiting)
    got.update(flight.land(f"send{slots - 1}"))
    sums, waiting = bring(slots - 1)
    arrays = (first_own, first_other[0], grad_query[0], *sums, attended, branch)
    theirs = weigh(meta, steps_theirs, (line.tie(first_own),) + arrays[1:])
    line.mark = theirs
    finish_part = lend(False, 1, meta, line.tie(acts[0]), acts[1], w_fc2)
    line.mark = (theirs, finish_part)

    got.update(flight.land())
    left, right = pack((both.pieces, True))
    one = Chain(pieces=[left], joins=("y", "z", "x"))
    two = Chain(pieces=[right], joins=("x", "z", "y"))
    flight.launch(("theirs", [theirs], "band", 1), ("finish", finish_part, "band", 1), one, two)
    ours = weigh(meta, steps_ours, (line.tie(first_own),) + arrays[1:])
    line.mark = ours

    got.update(flight.land())
    (theirs,) = got["theirs"]
    three = Chain((ours[0], theirs[0]), LAST_ORDERS[0])
    four = Chain((ours[1], theirs[1]), LAST_ORDERS[1])
    left, right = pack((one.pieces, False), (two.pieces, False))
    one.pieces, two.pieces = [left], [right]
    flight.launch(three, four, one, two, *waiting)
    output = finish(*at, line.tie(acts[0]), acts[1], w_fc2, got["finish"][0], hidden)
    line.mark = output

    flight.land(three, four)
    flight.launch(three, four)

    got.update(flight.land(one, two, f"partial{slots - 1}"))
    left, right = pack((one.pieces, False), (two.pieces, False))
    one.pieces, two.pieces = [left], [right]
    line.mark = (left, right)
    flight.land(three, four)
    five = Chain((jnp.stack([three.total_here(), four.total_here()], axis=1),), ("zw",))
    flight.launch(five, one, two)
    partials = [got[f"partial{s}"][0] for s in range(slots)]
    grad_input = close(
        line.tie(grad_query[0]), sums[0], sums[1], partials, tokens, branch, gain_one, w_qkv
    )
    line.mark = grad_input

    flight.land(five)
    five = Chain(pieces=[five.total()], joins=("zw",))
    flight.launch(five)

    flight.land(one, two)
    flight.land(five)
    *halves, whole = pack((five.pieces, True), (one.pieces, False))
    three = Chain(pieces=halves[:1], joins=("y", "x"))
    four = Chain(pieces=halves[1:], joins=("x", "y"))
    flight.launch(three, four, ("one", [whole], "band", 1), ("two_held", two.pieces[:1], "band", 1))

    got.update(flight.land())
    held = pack((three.pieces, False), (four.pieces, False))
    three.pieces, four.pieces = held[:1], held[1:]
    flight.launch(three, four, ("two_rest", two.pieces[1:], "band", 1), ("qkv_held", held, "band", 1))
    got.update(flight.land("two_rest"))
    mlp_pieces = [line.tie(whole), *two.pieces, got["one"][0], got["two_held"][0], got["two_rest"][0]]
    grad_fc1, grad_fc2, norm2 = spread_mlp(meta, mlp_pieces, w_fc1, gain_two)
    line.mark = norm2

    got.update(flight.land())
    flight.launch(("qkv_rest", [three.pieces[1], four.pieces[1]], "band", 1))
    got.update(flight.land())
    last_pieces = three.pieces + four.pieces + [p for pair in zip(got["qkv_held"], got["qkv_rest"]) for p in pair]
    grad_qkv, grad_proj, norm1 = spread_qkv(meta, last_pieces, w_qkv, gain_one)
    return (output, grad_input, grad_qkv, grad_proj, grad_fc1, grad_fc2, norm1, norm2)


def solution(mesh):
    placed = (
        P("batch", "band", None),
        P(),
        P(),
        P(),
        P(),
        P(),
        P(),
        P("batch", "band", None),
        P("batch", None),
        P("batch"),
    )
    return jax.shard_map(
        body,
        mesh=mesh,
        in_specs=placed,
        out_specs=(
            P("batch", "band", None),
            P("batch", "band", None),
            P(),
            P(),
            P(),
            P(),
            P(),
            P(),
        ),
        check_vma=False,
    )
```

```python
import functools
import jax
import jax.numpy as jnp
from jax import lax
from jax.experimental import pallas as pl
from jax.experimental.pallas import tpu as pltpu
from jax.sharding import PartitionSpec as P

BF = jnp.bfloat16
F32 = jnp.float32
EPSILON = 1e-06
HEAD_DIM = 64
GROUP = 256
NN = (((1,), (0,)), ((), ()))
NT = (((1,), (1,)), ((), ()))
TN = (((0,), (0,)), ((), ()))


def dot(left, right, dims=NN):
    return lax.dot_general(left, right, dims, preferred_element_type=F32)


def params(mib=60):
    return pltpu.CompilerParams(vmem_limit_bytes=mib * 1024 * 1024)


def cost(flops, moved, exps=0):
    return pl.CostEstimate(flops=1, bytes_accessed=1, transcendentals=0)


HBM = pl.BlockSpec(memory_space=pl.ANY)
STAY = pl.BlockSpec(memory_space=pltpu.HBM)


def normalized(values):
    centered = values - jnp.mean(values, axis=-1, keepdims=True)
    spread = jnp.mean(centered * centered, axis=-1, keepdims=True)
    scale = lax.rsqrt(spread + EPSILON)
    return centered * scale, scale


def project_kernel(tokens, weight, gain, first_in, query, both):
    normed, _ = normalized(tokens[0].astype(F32))
    first = (normed * gain[...]).astype(BF)
    first_in[0] = first
    width = first.shape[1]
    query[0] = (dot(first, weight[:, :width]) * HEAD_DIM ** -0.5).astype(BF)
    both[0, 0] = dot(first, weight[:, width:2 * width]).astype(BF)
    both[0, 1] = dot(first, weight[:, 2 * width:]).astype(BF)


def project(tokens, w_qkv, gain):
    slots, rows, width = tokens.shape
    row_spec = pl.BlockSpec((1, rows, width), lambda s: (s, 0, 0))
    return pl.pallas_call(
        project_kernel,
        out_shape=[
            pltpu.HBM(tokens.shape, BF),
            jax.ShapeDtypeStruct(tokens.shape, BF),
            jax.ShapeDtypeStruct((slots, 2, rows, width), BF),
        ],
        grid=(slots,),
        in_specs=[
            row_spec,
            pl.BlockSpec((width, 3 * width), lambda s: (0, 0)),
            pl.BlockSpec((1, width), lambda s: (0, 0)),
        ],
        out_specs=[row_spec, row_spec, pl.BlockSpec((1, 2, rows, width), lambda s: (s, 0, 0, 0))],
        compiler_params=params(14),
        cost_estimate=cost(2 * slots * rows * width * width * 3, 8e6),
        name="project",
    )(tokens, w_qkv, gain)


def project_other_kernel(tokens, own, weight, gain, *refs):
    first_in, both = refs[-2:]
    normed, _ = normalized(tokens[0].astype(F32))
    first = (normed * gain[...]).astype(BF)
    first_in[0] = first
    width = first.shape[1]
    both[0] = own[0]
    both[1, 0] = dot(first, weight[:, :width]).astype(BF)
    both[1, 1] = dot(first, weight[:, width:]).astype(BF)


def project_other(slot, tokens, kv_own, w_qkv, gain, before):
    slots, _, rows, width = kv_own.shape
    return pl.pallas_call(
        project_other_kernel,
        out_shape=[
            jax.ShapeDtypeStruct((slots, rows, width), BF),
            jax.ShapeDtypeStruct((2, 2, rows, width), BF),
        ],
        grid=(1,),
        in_specs=[
            pl.BlockSpec((1, rows, width), lambda i: (0, 0, 0)),
            pl.BlockSpec((1, 2, rows, width), lambda i: (slot, 0, 0, 0)),
            pl.BlockSpec((pl.Element(width), pl.Element(2 * width)), lambda i: (0, width)),
            pl.BlockSpec((1, width), lambda i: (0, 0)),
        ] + [HBM] * len(before),
        out_specs=[
            pl.BlockSpec((1, rows, width), lambda i: (slot, 0, 0)),
            pl.BlockSpec((2, 2, rows, width), lambda i: (0, 0, 0, 0)),
        ],
        input_output_aliases={4 + i: i for i in range(len(before))},
        compiler_params=params(10),
        cost_estimate=cost(2 * rows * width * width * 2, 5e6),
        name="project_other",
    )(tokens, kv_own, w_qkv, gain, *before)


def key_masks(counts, live, meta, slot, rows, flips, axis):
    shape = (rows, 1) if axis == 0 else (1, rows)
    place = lax.broadcasted_iota(jnp.int32, shape, axis)
    alive = live[slot] > 0
    return [place < jnp.where(alive, counts[slot, meta[0] ^ flip], 0) for flip in flips]


FLIPS = (0, 2, 1, 3)


def attend_kernel(slot, counts, live, meta, query, pair, pair_p, tokens, w_proj, gain, *refs):
    attended, lse, hidden, second, held, own_tokens, weight, sems = refs[-8:]
    group = pl.program_id(0)
    rows = query.shape[1]
    copies = (
        pltpu.make_async_copy(tokens.at[slot], own_tokens, sems.at[0]),
        pltpu.make_async_copy(w_proj, weight, sems.at[1]),
    )

    @pl.when(group == 0)
    def _():
        for copy in copies:
            copy.start()

    masks = key_masks(counts, live, meta, slot, rows, FLIPS, 1)
    q = query[0]
    lane = lax.broadcasted_iota(jnp.int32, (1, GROUP), 1)
    result = jnp.zeros((rows, GROUP), F32)
    sums = jnp.zeros((rows, 128), F32)
    lane128 = lax.broadcasted_iota(jnp.int32, (1, 128), 1)
    blocks = (pair.at[0], pair.at[1], pair_p.at[0], pair_p.at[1])

    def scores_of(h):
        qm = jnp.where((lane // HEAD_DIM) == h, q, jnp.zeros_like(q))
        return [jnp.where(mask, dot(qm, block[0], NT), -10000.0) for mask, block in zip(masks, blocks)]

    ahead = scores_of(0)
    for h in range(GROUP // HEAD_DIM):
        here = (lane // HEAD_DIM) == h
        scores = ahead
        if h + 1 < GROUP // HEAD_DIM:
            ahead = scores_of(h + 1)
        top = scores[0]
        for s in scores[1:]:
            top = jnp.maximum(top, s)
        top = jnp.max(top, axis=-1, keepdims=True)
        out = jnp.zeros((rows, GROUP), F32)
        exps = [jnp.exp(s - top) for s in scores]
        total = exps[0]
        for e in exps[1:]:
            total = total + e
        total = jnp.sum(total, axis=-1, keepdims=True)
        for e, block in zip(exps, blocks):
            out = out + dot(e.astype(BF), block[1])
        result = jnp.where(here, out * (1.0 / total), result)
        sums = jnp.where(lane128 == h, top + jnp.log(total), sums)
    low = result.astype(BF)
    attended[0] = low
    held[group] = low
    lse[0, 0] = sums.T[:8]

    @pl.when(group == pl.num_programs(0) - 1)
    def _():
        for copy in copies:
            copy.wait()
        value = own_tokens[...].astype(F32)
        for g in range(held.shape[0]):
            value = value + dot(held[g], weight[g * GROUP:(g + 1) * GROUP, :])
        hidden[0] = value
        normed, _ = normalized(value)
        second[...] = (normed * gain[...]).astype(BF)


def attend(slot, counts, live, meta, query, pair, pair_p, tokens, w_proj, gain, before):
    slots, rows, width = query.shape
    groups = width // GROUP
    at = slot
    kv_spec = pl.BlockSpec((2, 2, rows, GROUP), lambda g, *_: (0, 0, 0, g))
    piece = pl.BlockSpec((1, rows, GROUP), lambda g, *_: (at, 0, g))
    row_spec = pl.BlockSpec((1, rows, width), lambda g, *_: (at, 0, 0))
    operands = (counts, live, meta, query, pair, pair_p, tokens, w_proj, gain)
    return pl.pallas_call(
        functools.partial(attend_kernel, slot),
        out_shape=[
            jax.ShapeDtypeStruct(query.shape, BF),
            jax.ShapeDtypeStruct((slots, groups, 8, rows), F32),
            jax.ShapeDtypeStruct(query.shape, F32),
            jax.ShapeDtypeStruct((rows, width), BF),
        ],
        grid_spec=pltpu.PrefetchScalarGridSpec(
            num_scalar_prefetch=3,
            grid=(groups,),
            in_specs=[piece, kv_spec, kv_spec, HBM, HBM, pl.BlockSpec((1, width), lambda g, *_: (0, 0))]
            + [HBM] * len(before),
            out_specs=[
                piece,
                pl.BlockSpec((1, 1, 8, rows), lambda g, *_: (at, g, 0, 0)),
                row_spec,
                pl.BlockSpec((rows, width), lambda g, *_: (0, 0)),
            ],
            scratch_shapes=[
                pltpu.VMEM((groups, rows, GROUP), BF),
                pltpu.VMEM((rows, width), BF),
                pltpu.VMEM((width, width), BF),
                pltpu.SemaphoreType.DMA((2,)),
            ],
        ),
        input_output_aliases={len(operands) + i: i for i in range(len(before))},
        compiler_params=params(14),
        cost_estimate=cost(2 * 2 * rows * 4 * rows * 4 * width, 1e7, 12 * rows * 4 * rows),
        name="attend",
    )(*operands, *before)


def attend_back_kernel(
    slot, counts, live, meta, query, pair, pair_p, grad, lse, delta, *refs
):
    grad_query, grad_keep, grad_send, probs, slopes, qms, gms, keys, values, keys_t = refs[-10:]
    rows = query.shape[1]
    heads = GROUP // HEAD_DIM
    masks = key_masks(counts, live, meta, slot, rows, FLIPS, 0)
    q = query[0]
    ga = grad[0]
    lane = lax.broadcasted_iota(jnp.int32, (1, GROUP), 1)
    zero = jnp.zeros_like(q)
    for h in range(heads):
        here = (lane // HEAD_DIM) == h
        qms[h * rows:(h + 1) * rows, :] = jnp.where(here, q, zero)
        gms[h * rows:(h + 1) * rows, :] = jnp.where(here, ga, zero)
    for i, mask in enumerate(masks):
        block = (pair, pair_p)[i // 2]
        keys[i * rows:(i + 1) * rows, :] = jnp.where(mask, block[i % 2, 0], zero)
        values[i * rows:(i + 1) * rows, :] = block[i % 2, 1]
    keys_t[...] = keys[...].T
    gq = []
    for h in range(heads):
        mine = slice(h * rows, (h + 1) * rows)
        for i, mask in enumerate(masks):
            at = slice(i * rows, (i + 1) * rows)
            scores = jnp.where(mask, dot(keys[at, :], qms[mine, :], NT), -10000.0)
            gp = dot(values[at, :], gms[mine, :], NT)
            p = jnp.exp(scores - lse[0, 0, h:h + 1, :])
            probs[at, mine] = p.astype(BF)
            slopes[at, mine] = (p * (gp - delta[0, 0, h:h + 1, :])).astype(BF)
        gq.append(dot(keys_t[h * HEAD_DIM:(h + 1) * HEAD_DIM, :], slopes[:, mine]))
    gk = dot(slopes[...], qms[...])
    gv = dot(probs[...], gms[...])
    outs = ((grad_keep, 0), (grad_keep, 1), (grad_send, 0), (grad_send, 1))
    for i, ((out, place), mask) in enumerate(zip(outs, masks)):
        at = slice(i * rows, (i + 1) * rows)
        out[0, place, 0] = jnp.where(mask, gk[at], 0.0).astype(BF)
        out[0, place, 1] = gv[at].astype(BF)
    grad_query[0] = (jnp.concatenate(gq, axis=0).T * HEAD_DIM ** -0.5).astype(BF)


def attend_back(slot, counts, live, meta, query, pair, pair_p, grad, lse, delta, before):
    slots, rows, width = query.shape
    groups = width // GROUP
    heads = GROUP // HEAD_DIM
    at = slot
    kv_spec = pl.BlockSpec((2, 2, rows, GROUP), lambda g, *_: (0, 0, 0, g))
    row_spec = pl.BlockSpec((1, rows, GROUP), lambda g, *_: (at, 0, g))
    stat_spec = pl.BlockSpec((1, 1, 8, rows), lambda g, *_: (at, g, 0, 0))
    out_spec = pl.BlockSpec((1, 2, 2, rows, GROUP), lambda g, *_: (0, 0, 0, 0, g))
    operands = (counts, live, meta, query, pair, pair_p, grad, lse, delta)
    return pl.pallas_call(
        functools.partial(attend_back_kernel, slot),
        out_shape=[
            jax.ShapeDtypeStruct(query.shape, BF),
            jax.ShapeDtypeStruct((1, 2, 2, rows, width), BF),
            jax.ShapeDtypeStruct((1, 2, 2, rows, width), BF),
        ],
        grid_spec=pltpu.PrefetchScalarGridSpec(
            num_scalar_prefetch=3,
            grid=(groups,),
            in_specs=[row_spec, kv_spec, kv_spec, row_spec, stat_spec, stat_spec]
            + [pl.BlockSpec(memory_space=pl.ANY)] * len(before),
            out_specs=[row_spec, out_spec, out_spec],
            scratch_shapes=[
                pltpu.VMEM((4 * rows, heads * rows), BF),
                pltpu.VMEM((4 * rows, heads * rows), BF),
                pltpu.VMEM((heads * rows, GROUP), BF),
                pltpu.VMEM((heads * rows, GROUP), BF),
                pltpu.VMEM((4 * rows, GROUP), BF),
                pltpu.VMEM((4 * rows, GROUP), BF),
                pltpu.VMEM((GROUP, 4 * rows), BF),
            ],
        ),
        input_output_aliases={len(operands) + i: i for i in range(len(before))},
        compiler_params=params(18),
        cost_estimate=cost(5 * 2 * rows * 4 * rows * 4 * width, 2e7, 12 * rows * 4 * rows),
        name="attend_back",
    )(*operands, *before)


CHUNKS = 16


def row_mask(counts, live, meta, slot, rows):
    return key_masks(counts, live, meta, slot, rows, (0,), 0)[0]


def gelu_parts(v):
    size = jnp.abs(v)
    decay = jnp.exp2(v * v * (-0.5 * 1.4426950408889634))
    scale = 1.0 + (0.3275911 * 0.7071067811865476) * size
    t = pl.reciprocal(scale, approx=True)
    t = t * (2.0 - scale * t)
    poly = t * (0.127414796 + t * (-0.142248368 + t * (0.7107068705 + t * (-0.7265760135 + t * 0.5307027145))))
    tail = poly * decay
    phi = jnp.where(v >= 0, 1.0 - tail, tail)
    return phi, decay * 0.3989422804014327


def mlp_kernel(slots, half, counts, live, meta, *refs):
    seconds, rest = refs[:2 * slots], refs[2 * slots:]
    cot, cot_p, w_in, w_out, act_out, pre_out, *grads_out = rest[:8]
    sec, go, win, wout, act, pre, grads, sems, out_sems = rest[8:]
    rows = seconds[0].shape[0]
    count = slots * rows
    width = sec.shape[1]
    me = meta[2 + half]
    part = pl.multiple_of((2 * meta[1] + half) * width, width)

    def copies_for(side):
        whole = pl.ds(side * count, count)
        out = [
            pltpu.make_async_copy(
                seconds[side * slots + s], sec.at[pl.ds(side * count + s * rows, rows)], sems.at[side * (slots + 1) + s]
            )
            for s in range(slots)
        ]
        source = (cot, cot_p)[side]
        return out, pltpu.make_async_copy(source, go.at[whole], sems.at[side * (slots + 1) + slots])

    last = 2 * (slots + 1)
    load_in = pltpu.make_async_copy(w_in.at[:, pl.ds(part, width)], win, sems.at[last])
    load_out = pltpu.make_async_copy(w_out.at[pl.ds(part, width), :], wout, sems.at[last + 1])
    sides = [copies_for(side) for side in range(2)]
    for c in sides[0][0]:
        c.start()
    load_in.start()
    sides[0][1].start()
    load_out.start()
    for c in sides[1][0]:
        c.start()
    sides[1][1].start()
    stores = []

    def store(source, target):
        copy = pltpu.make_async_copy(source, target, out_sems.at[len(stores)])
        copy.start()
        stores.append(copy)

    def activate(at, before, grad_act):
        phi, density = gelu_parts(before)
        act[at, :] = (before * phi).astype(BF)
        pre[at, :] = (grad_act * (phi + before * density)).astype(BF)

    own = slice(0, count)
    for c in sides[0][0]:
        c.wait()
    load_in.wait()
    before = dot(sec[own, :], win[...])
    sides[0][1].wait()
    load_out.wait()
    for c in sides[1][0]:
        c.wait()
    sides[1][1].wait()
    for side in range(2):
        for s in range(slots):
            mask = key_masks(counts, live, meta, s, rows, (side,), 0)[0]
            here = slice(side * count + s * rows, side * count + (s + 1) * rows)
            go[here, :] = jnp.where(mask, go[here, :], jnp.zeros((rows, width), BF))
    activate(own, before, dot(go[own, :], wout[...], NT))
    for s in range(slots):
        at = slice(count + s * rows, count + (s + 1) * rows)
        activate(at, dot(sec[at, :], win[...]), dot(go[at, :], wout[...], NT))
    for side in range(2):
        window = pl.ds(side * count, count)
        store(act.at[window], act_out.at[window])
        store(pre.at[window], pre_out.at[window])
    size = width // CHUNKS
    for kind, (left, right) in ((1, (act, go)), (0, (sec, pre))):
        value = dot(left[...], right[...], TN)
        for a in range(CHUNKS):
            grads[kind, a ^ me] = value[a * size:(a + 1) * size].astype(BF)
        for i, out in enumerate(grads_out):
            store(grads.at[kind, pl.ds(i * CHUNKS // 2, CHUNKS // 2)], out.at[:, kind])
    for copy in stores:
        copy.wait()


def mlp(counts, live, meta, seconds, cotangent, cotangent_p, w_fc1, w_fc2, half):
    rows, width = seconds[0].shape
    slots = len(seconds) // 2
    both = 2 * slots * rows
    operands = (*seconds, cotangent.reshape(slots * rows, width), cotangent_p.reshape(slots * rows, width), w_fc1, w_fc2)
    return pl.pallas_call(
        functools.partial(mlp_kernel, slots, half),
        out_shape=[
            pltpu.HBM((both, width), BF),
            pltpu.HBM((both, width), BF),
        ]
        + [jax.ShapeDtypeStruct((CHUNKS // 2, 2, width // CHUNKS, width), BF)] * 2,
        grid_spec=pltpu.PrefetchScalarGridSpec(
            num_scalar_prefetch=3,
            grid=(1,),
            in_specs=[HBM] * (len(operands) - 2) + [STAY] * 2,
            out_specs=[STAY] * 2 + [HBM] * 2,
            scratch_shapes=[pltpu.VMEM((both, width), BF)] * 2
            + [pltpu.VMEM((width, width), BF)] * 2
            + [pltpu.VMEM((both, width), BF)] * 2
            + [
                pltpu.VMEM((2, CHUNKS, width // CHUNKS, width), BF),
                pltpu.SemaphoreType.DMA((2 * (slots + 1) + 2,)),
                pltpu.SemaphoreType.DMA((8,)),
            ],
        ),
        compiler_params=params(24),
        cost_estimate=cost(2 * 4 * 2 * slots * rows * width * width, 2e7),
        name="mlp",
    )(counts, live, meta, *operands)


def lend_kernel(nt, meta, first, second, weight, *refs):
    outs, (left, held, sems) = refs[:-3], refs[-3:]
    _, count, width = left.shape
    core = meta[1]
    loads = []
    for i, source in enumerate((first, second)):
        place = pl.ds(pl.multiple_of((2 * core + i) * width, width), width)
        loads.append(pltpu.make_async_copy(source.at[pl.ds(count, count)], left.at[i], sems.at[2 * i]))
        part = weight.at[:, place] if nt else weight.at[place, :]
        loads.append(pltpu.make_async_copy(part, held.at[i], sems.at[2 * i + 1]))
    for load in loads:
        load.start()
    dims = NT if nt else NN
    loads[0].wait()
    loads[1].wait()
    total = dot(left[0], held[0], dims)
    loads[2].wait()
    loads[3].wait()
    total = (total + dot(left[1], held[1], dims)).astype(BF)
    size = count // len(outs)
    for i, out in enumerate(outs):
        out[...] = total[i * size:(i + 1) * size]


def lend(nt, parts, meta, first, second, weight):
    both, width = first.shape
    size = both // 2 // parts
    return pl.pallas_call(
        functools.partial(lend_kernel, nt),
        out_shape=[jax.ShapeDtypeStruct((size, width), BF)] * parts,
        grid_spec=pltpu.PrefetchScalarGridSpec(
            num_scalar_prefetch=1,
            grid=(1,),
            in_specs=[STAY] * 3,
            out_specs=[pl.BlockSpec((size, width), lambda i, *_: (0, 0))] * parts,
            scratch_shapes=[
                pltpu.VMEM((2, both // 2, width), BF),
                pltpu.VMEM((2, width, width), BF),
                pltpu.SemaphoreType.DMA((4,)),
            ],
        ),
        compiler_params=params(10),
        cost_estimate=cost(2 * both * width * width, 6e6),
        name="lend",
    )(meta, first, second, weight)


def layer_norm_back(values, gain, grad):
    normed, scale = normalized(values)
    t = grad * gain
    return scale * (t - jnp.mean(t, axis=-1, keepdims=True) - normed * jnp.mean(t * normed, axis=-1, keepdims=True))


def turn_kernel(
    counts, live, meta, first, second, weight, got, also, hidden, cotangent, attended, gain, w_proj,
    grad_branch, grad_attended, delta, left, held, got_v, hidden_v, cot_v, att_v, proj_v, sems,
):
    slots, rows, width = grad_branch.shape
    count = slots * rows
    core = meta[1]
    loads = []
    for i, source in enumerate((first, second)):
        place = pl.ds(pl.multiple_of((2 * core + i) * width, width), width)
        loads.append(pltpu.make_async_copy(source.at[pl.ds(0, count)], left.at[i], sems.at[2 * i]))
        loads.append(pltpu.make_async_copy(weight.at[:, place], held.at[i], sems.at[2 * i + 1]))
    for i, (source, target) in enumerate(
        (
            (got, got_v.at[pl.ds(0, count // 2)]), (also, got_v.at[pl.ds(count // 2, count // 2)]),
            (hidden, hidden_v), (cotangent, cot_v), (w_proj, proj_v), (attended, att_v),
        )
    ):
        loads.append(pltpu.make_async_copy(source, target, sems.at[4 + i]))
    for load in loads:
        load.start()
    loads[0].wait()
    loads[1].wait()
    total = dot(left[0], held[0], NT)
    loads[2].wait()
    loads[3].wait()
    total = total + dot(left[1], held[1], NT)
    for load in loads[4:]:
        load.wait()
    head = lax.broadcasted_iota(jnp.int32, (32, width), 0)
    column = lax.broadcasted_iota(jnp.int32, (32, width), 1) // HEAD_DIM
    per = GROUP // HEAD_DIM
    pick = (head == (column // per) * 8 + column % per).astype(BF)
    for s in range(slots):
        here = slice(s * rows, (s + 1) * rows)
        mask = row_mask(counts, live, meta, s, rows)
        grad_out = jnp.where(mask, cot_v[s].astype(F32), 0.0)
        given = total[here] + got_v[here, :].astype(F32)
        branch = (grad_out + layer_norm_back(hidden_v[s], gain[...], given)).astype(BF)
        grad_branch[s] = branch
        back = dot(branch, proj_v[...], NT).astype(BF)
        grad_attended[s] = back
        product = back.astype(F32) * att_v[s].astype(F32)
        high = product.astype(BF)
        low = (product - high.astype(F32)).astype(BF)
        sums = dot(pick, high, NT) + dot(pick, low, NT)
        for g in range(width // GROUP):
            delta[s, g] = sums[8 * g:8 * g + 8]


def turn(counts, live, meta, first, second, weight, got, also, hidden, cotangent, attended, gain, w_proj):
    slots, rows, width = hidden.shape
    count = slots * rows
    groups = width // GROUP
    whole = pl.BlockSpec(hidden.shape, lambda i, *_: (0, 0, 0))
    return pl.pallas_call(
        turn_kernel,
        out_shape=[
            jax.ShapeDtypeStruct(hidden.shape, BF),
            jax.ShapeDtypeStruct(hidden.shape, BF),
            jax.ShapeDtypeStruct((slots, groups, 8, rows), F32),
        ],
        grid_spec=pltpu.PrefetchScalarGridSpec(
            num_scalar_prefetch=3,
            grid=(1,),
            in_specs=[STAY] * 3 + [HBM] * 5 + [pl.BlockSpec((1, width), lambda i, *_: (0, 0)), HBM],
            out_specs=[whole, whole, pl.BlockSpec((slots, groups, 8, rows), lambda i, *_: (0, 0, 0, 0))],
            scratch_shapes=[
                pltpu.VMEM((2, count, width), BF),
                pltpu.VMEM((2, width, width), BF),
                pltpu.VMEM((count, width), BF),
                pltpu.VMEM(hidden.shape, F32),
                pltpu.VMEM(hidden.shape, BF),
                pltpu.VMEM(hidden.shape, BF),
                pltpu.VMEM((width, width), BF),
                pltpu.SemaphoreType.DMA((10,)),
            ],
        ),
        compiler_params=params(20),
        cost_estimate=cost(3 * 2 * slots * rows * width * width, 1.5e7),
        name="turn",
    )(counts, live, meta, first, second, weight, got, also, hidden, cotangent, attended, gain, w_proj)


def finish_kernel(counts, live, meta, first, second, weight, got, hidden, output, left, held, got_v, hidden_v, sems):
    slots, rows, width = output.shape
    count = slots * rows
    core = meta[1]
    loads = []
    for i, source in enumerate((first, second)):
        place = pl.ds(pl.multiple_of((2 * core + i) * width, width), width)
        loads.append(pltpu.make_async_copy(source.at[pl.ds(0, count)], left.at[i], sems.at[2 * i]))
        loads.append(pltpu.make_async_copy(weight.at[place, :], held.at[i], sems.at[2 * i + 1]))
    loads.append(pltpu.make_async_copy(got, got_v, sems.at[4]))
    loads.append(pltpu.make_async_copy(hidden, hidden_v, sems.at[5]))
    for load in loads:
        load.start()
    loads[0].wait()
    loads[1].wait()
    total = dot(left[0], held[0])
    loads[2].wait()
    loads[3].wait()
    total = total + dot(left[1], held[1])
    loads[4].wait()
    loads[5].wait()
    for s in range(slots):
        here = slice(s * rows, (s + 1) * rows)
        mask = row_mask(counts, live, meta, s, rows)
        output[s] = jnp.where(mask, total[here] + got_v[here, :].astype(F32) + hidden_v[s], 0.0).astype(BF)


def finish(counts, live, meta, first, second, weight, got, hidden):
    slots, rows, width = hidden.shape
    count = slots * rows
    return pl.pallas_call(
        finish_kernel,
        out_shape=jax.ShapeDtypeStruct(hidden.shape, BF),
        grid_spec=pltpu.PrefetchScalarGridSpec(
            num_scalar_prefetch=3,
            grid=(1,),
            in_specs=[STAY] * 3 + [HBM] * 2,
            out_specs=pl.BlockSpec(hidden.shape, lambda i, *_: (0, 0, 0)),
            scratch_shapes=[
                pltpu.VMEM((2, count, width), BF),
                pltpu.VMEM((2, width, width), BF),
                pltpu.VMEM((count, width), BF),
                pltpu.VMEM(hidden.shape, F32),
                pltpu.SemaphoreType.DMA((6,)),
            ],
        ),
        compiler_params=params(16),
        cost_estimate=cost(2 * 2 * slots * rows * width * width, 9e6),
        name="finish",
    )(counts, live, meta, first, second, weight, got, hidden)


def gather_kernel(mine, got, w_kv, *refs):
    key_own, value_own, key_other, value_other, partial = refs[-5:]
    width = partial.shape[-1]
    parts = []
    for place, out in ((0, (key_own, value_own)), (1, (key_other, value_other))):
        for i in range(2):
            total = (mine[0, place, i].astype(F32) + got[0, place, i].astype(F32)).astype(BF)
            out[i][0] = total
            parts.append(total)
    partial[0] = (dot(parts[2], w_kv[:, :width], NT) + dot(parts[3], w_kv[:, width:], NT)).astype(BF)


def gather(slot, slots, mine, got, w_qkv, before):
    _, _, _, rows, width = mine.shape
    row_spec = pl.BlockSpec((1, rows, width), lambda i: (slot, 0, 0))
    kv_spec = pl.BlockSpec((1, 2, 2, rows, width), lambda i: (0, 0, 0, 0, 0))
    return pl.pallas_call(
        gather_kernel,
        out_shape=[jax.ShapeDtypeStruct((slots, rows, width), BF)] * 4 + [jax.ShapeDtypeStruct((1, rows, width), BF)],
        grid=(1,),
        in_specs=[kv_spec, kv_spec, pl.BlockSpec((pl.Element(width), pl.Element(2 * width)), lambda s: (0, width))]
        + [pl.BlockSpec(memory_space=pl.ANY)] * len(before),
        out_specs=[row_spec] * 4 + [pl.BlockSpec((1, rows, width), lambda i: (0, 0, 0))],
        input_output_aliases={3 + i: i for i in range(len(before))},
        compiler_params=params(10),
        cost_estimate=cost(2 * 2 * rows * width * width, 6e6),
        name="gather",
    )(mine, got, w_qkv, *before)


VALUE_UNITS = ((0, 4, 1, 0, 0), (1, 6, 0, 1, 0), (7, 8, 1, 1, 1))
QUERY_UNITS = ((0, 2, 1, 1, 0), (0, 3, 1, 0, 1), (1, 5, 0, 1, 1))


def weigh_steps(units):
    seen = set()
    steps = []
    for step in units:
        steps.append(step + (int(step[0] not in seen),))
        seen.add(step[0])
    return jnp.array(steps, jnp.int32)


def weigh_kernel(meta, steps, *refs):
    sources, (grads, held, total, sems) = refs[:9], refs[9:]
    step = pl.program_id(0)
    size = held.shape[1] // CHUNKS
    values = steps[0, 1] == VALUE_UNITS[0][1]

    def start(units):
        seen = []
        for unit in units:
            for i in unit[:2]:
                if i not in seen:
                    seen.append(i)
                    pltpu.make_async_copy(sources[i], held.at[i], sems.at[i]).start()

    @pl.when(jnp.logical_and(step == 0, values))
    def _():
        start(VALUE_UNITS)

    @pl.when(jnp.logical_and(step == 0, jnp.logical_not(values)))
    def _():
        start(QUERY_UNITS)

    left = steps[step, 0]
    right = steps[step, 1]

    @pl.when(steps[step, 5] == 1)
    def _():
        pltpu.make_async_copy(sources[0], held.at[left], sems.at[left]).wait()

    pltpu.make_async_copy(sources[0], held.at[right], sems.at[right]).wait()

    @pl.when(steps[step, 2] == 1)
    def _():
        total[...] = dot(held[left], held[right], TN)

    @pl.when(steps[step, 2] != 1)
    def _():
        total[...] += dot(held[left], held[right], TN)

    @pl.when(steps[step, 3] == 1)
    def _():
        unit = steps[step, 4]
        me = meta[4 + unit]
        for a in range(CHUNKS):
            grads[unit, a ^ me] = total[a * size:(a + 1) * size, :].astype(BF)


def weigh(meta, steps, arrays):
    arrays = [a.reshape(-1, a.shape[-1]) for a in arrays]
    rows, width = arrays[0].shape
    shape = (2, CHUNKS, width // CHUNKS, width)
    return pl.pallas_call(
        weigh_kernel,
        out_shape=jax.ShapeDtypeStruct(shape, BF),
        grid_spec=pltpu.PrefetchScalarGridSpec(
            num_scalar_prefetch=2,
            grid=(3,),
            in_specs=[HBM] * 9,
            out_specs=pl.BlockSpec(shape, lambda i, *_: (0, 0, 0, 0)),
            scratch_shapes=[
                pltpu.VMEM((9, rows, width), BF),
                pltpu.VMEM((rows, width), F32),
                pltpu.SemaphoreType.DMA((9,)),
            ],
        ),
        compiler_params=params(19),
        cost_estimate=cost(3 * 2 * rows * width * width, 1e7),
        name="weigh",
    )(meta, steps, *arrays)


def close_kernel(gq, gk, gv, w_qkv, tokens, grad_hidden, gain, *refs):
    partials, (out, total) = refs[:-2], refs[-2:]
    step = pl.program_id(0)
    slots, rows, width = gq.shape
    flat = (slots * rows, width)

    @pl.when(step == 0)
    def _():
        total[...] = dot(gq[...].reshape(flat), w_qkv[...], NT)

    @pl.when(step == 1)
    def _():
        total[...] += dot(gk[...].reshape(flat), w_qkv[...], NT)

    @pl.when(step == 2)
    def _():
        total[...] += dot(gv[...].reshape(flat), w_qkv[...], NT)
        for s, partial in enumerate(partials):
            total[s * rows:(s + 1) * rows, :] += partial[0].astype(F32)

    @pl.when(step > 2)
    def _():
        first = total[pl.ds(pl.multiple_of((step - 3) * rows, rows), rows), :]
        out[0] = (grad_hidden[0].astype(F32) + layer_norm_back(tokens[0].astype(F32), gain[...], first)).astype(BF)


def close(gq, gk, gv, partials, tokens, grad_hidden, gain, w_qkv):
    slots, rows, width = tokens.shape
    row_spec = pl.BlockSpec((1, rows, width), lambda i: (jnp.maximum(i - 3, 0), 0, 0))
    whole = pl.BlockSpec((slots, rows, width), lambda i: (0, 0, 0))
    return pl.pallas_call(
        close_kernel,
        out_shape=jax.ShapeDtypeStruct(tokens.shape, BF),
        grid=(3 + slots,),
        in_specs=[whole] * 3 + [pl.BlockSpec((width, width), lambda i: (0, jnp.minimum(i, 2)))] + [row_spec] * 2 + [
            pl.BlockSpec((1, width), lambda i: (0, 0)),
        ] + [pl.BlockSpec((1, rows, width), lambda i: (0, 0, 0))] * slots,
        out_specs=row_spec,
        scratch_shapes=[pltpu.VMEM((slots * rows, width), F32)],
        compiler_params=params(18),
        cost_estimate=cost(3 * 2 * slots * rows * width * width, 1.2e7),
        name="close",
    )(gq, gk, gv, w_qkv, tokens, grad_hidden, gain, *partials)


SPREAD = 4


def keep_row_sums(held, value):
    step = pl.program_id(0)
    rows = value.shape[0]
    column = jnp.sum(value, axis=-1, keepdims=True)
    held[pl.ds(pl.multiple_of(step * rows, rows), rows), :] = jnp.broadcast_to(column, (rows, 128))


def put_row_sums(norm, held, gain):
    @pl.when(pl.program_id(0) == pl.num_programs(0) - 1)
    def _():
        for r in range(norm.shape[0]):
            norm[r:r + 1, :] = held[r * 128:(r + 1) * 128, :].T[:1] / gain[r:r + 1, :]


def load_pieces(groups, targets, sems):
    copies = []
    for group, target in zip(groups, targets):
        place = 0
        for piece in group:
            size = piece.shape[0]
            copies.append(pltpu.make_async_copy(piece, target.at[pl.ds(place, size)], sems.at[len(copies)]))
            place += size
    for copy in copies:
        copy.start()
    for copy in copies:
        copy.wait()


def spread_mlp_kernel(meta, *refs):
    pieces, (w_fc1, gain, grad_fc1, grad_fc2, norm, one, two, held, sems) = refs[:8], refs[8:]
    step = pl.program_id(0)
    size, width = one.shape[-2:]

    @pl.when(step == 0)
    def _():
        groups = [pieces[2 * i:2 * i + 2] for i in range(4)]
        load_pieces(groups, (one.at[0], two.at[0], one.at[1], two.at[1]), sems)

    mine = [meta[6 + i] for i in range(4)]
    for a in range(4):
        here = slice(a * size, (a + 1) * size)
        for half, held_chunks in enumerate((one, two)):
            high, low, third, fourth = step // 2, step % 2, a // 2, a % 2
            digits = (low, third, high, fourth) if half == 0 else (low, high, third, fourth)
            x, y, z, w = [d ^ m for d, m in zip(digits, mine)]
            place = x * 8 + z * 4 + y * 2 + w if half == 0 else y * 8 + z * 4 + x * 2 + w
            for core in range(2):
                value = held_chunks[core ^ meta[1], place].astype(F32)
                column = 2 * core + half
                grad_fc1[here, column * width:(column + 1) * width] = value[0]
                grad_fc2[column, here, :] = value[1]
    keep_row_sums(held, grad_fc1[...] * w_fc1[...].astype(F32))
    put_row_sums(norm, held, gain)


def spread_mlp(meta, pieces, w_fc1, gain):
    width, hidden_width = w_fc1.shape
    per = CHUNKS // SPREAD
    size = width // CHUNKS
    outs = pl.pallas_call(
        spread_mlp_kernel,
        out_shape=[
            jax.ShapeDtypeStruct((width, hidden_width), F32),
            jax.ShapeDtypeStruct((4, width, width), F32),
            jax.ShapeDtypeStruct((width // 128, 128), F32),
        ],
        grid_spec=pltpu.PrefetchScalarGridSpec(
            num_scalar_prefetch=1,
            grid=(SPREAD,),
            in_specs=[HBM] * 8 + [
                pl.BlockSpec((per * size, hidden_width), lambda a, *_: (a, 0)),
                pl.BlockSpec((width // 128, 128), lambda a, *_: (0, 0)),
            ],
            out_specs=[
                pl.BlockSpec((per * size, hidden_width), lambda a, *_: (a, 0)),
                pl.BlockSpec((4, per * size, width), lambda a, *_: (0, a, 0)),
                pl.BlockSpec((width // 128, 128), lambda a, *_: (0, 0)),
            ],
            scratch_shapes=[
                pltpu.VMEM((2, CHUNKS, 2, size, width), BF),
                pltpu.VMEM((2, CHUNKS, 2, size, width), BF),
                pltpu.VMEM((width, 128), F32),
                pltpu.SemaphoreType.DMA((8,)),
            ],
        ),
        compiler_params=params(26),
        cost_estimate=cost(1e6, 4.7e7),
        name="spread_mlp",
    )(meta, *pieces, w_fc1, gain.reshape(width // 128, 128))
    return outs[0], outs[1].reshape(hidden_width, width), outs[2].reshape(width)


def spread_qkv_kernel(meta, *refs):
    pieces, (w_qkv, gain, grad_qkv, grad_proj, norm, chunks, held, sems) = refs[:8], refs[8:]
    step = pl.program_id(0)
    size, width = chunks.shape[-2:]

    @pl.when(step == 0)
    def _():
        load_pieces([pieces[2 * i:2 * i + 2] for i in range(4)], [chunks.at[i] for i in range(4)], sems)

    high, low = step // 2, step % 2
    tops = (((high ^ meta[6]) * 2 + (low ^ meta[7])) * 4, ((high ^ meta[7]) * 2 + (low ^ meta[6])) * 4)
    own = 2 * meta[1]
    part = 2 - own
    for a in range(4):
        here = slice(a * size, (a + 1) * size)
        last = a ^ (meta[8] * 2 + meta[9])
        for i in range(3):
            unit = i % 2
            grad_qkv[here, i * width:(i + 1) * width] = chunks[
                (own if i < 2 else part) + unit, tops[unit] + last
            ].astype(F32)
        grad_proj[here, :] = chunks[part + 1, tops[1] + last].astype(F32)
    keep_row_sums(held, grad_qkv[...] * w_qkv[...].astype(F32))
    put_row_sums(norm, held, gain)


def spread_qkv(meta, pieces, w_qkv, gain):
    width = w_qkv.shape[0]
    size = width // CHUNKS
    per = CHUNKS // SPREAD

    def rows(columns):
        return pl.BlockSpec((per * size, columns), lambda a, *_: (a, 0))

    line = pl.BlockSpec((width // 128, 128), lambda a, *_: (0, 0))
    outs = pl.pallas_call(
        spread_qkv_kernel,
        out_shape=[
            jax.ShapeDtypeStruct((width, 3 * width), F32),
            jax.ShapeDtypeStruct((width, width), F32),
            jax.ShapeDtypeStruct((width // 128, 128), F32),
        ],
        grid_spec=pltpu.PrefetchScalarGridSpec(
            num_scalar_prefetch=1,
            grid=(SPREAD,),
            in_specs=[HBM] * 8 + [rows(3 * width), line],
            out_specs=[rows(3 * width), rows(width), line],
            scratch_shapes=[
                pltpu.VMEM((4, CHUNKS, size, width), BF),
                pltpu.VMEM((width, 128), F32),
                pltpu.SemaphoreType.DMA((8,)),
            ],
        ),
        compiler_params=params(18),
        cost_estimate=cost(1e6, 1.8e7),
        name="spread_qkv",
    )(meta, *pieces, w_qkv, gain.reshape(width // 128, 128))
    return outs[0], outs[1], outs[2].reshape(width)


DIGITS = {"x": (0, 2), "y": (1, 0), "z": (2, 0), "w": (4, 0)}


def swap(value, axis, mask):
    return lax.ppermute(value, axis, [(i, i ^ mask) for i in range(lax.axis_size(axis))])


def swap_digits(value, masks):
    batch, band = masks
    if not band:
        return swap(value, "batch", batch)
    if not batch:
        return swap(value, "band", band)
    return swap(value, ("batch", "band"), batch * lax.axis_size("band") + band)


def add(*values):
    total = values[0].astype(F32)
    for value in values[1:]:
        total = total + value.astype(F32)
    return total.astype(BF)


def pack_kernel(groups, *refs):
    total = sum(count for count, _ in groups)
    sources, refs = refs[:total], refs[total:]
    outs = sum(1 + split for _, split in groups)
    targets, refs = list(refs[:outs]), refs[outs:]
    held, (sems, out_sems) = refs[:len(groups)], refs[len(groups):]
    loads, stores = [], []
    for group, (count, split) in enumerate(groups):
        mine = [targets.pop(0) for _ in range(1 + split)]
        for i in range(count):
            at = len(loads)
            size = sources[at].shape[0]
            here = pl.ds(i * size, size)
            loads.append(pltpu.make_async_copy(sources[at], held[group].at[here], sems.at[at]))
            stores.append([
                pltpu.make_async_copy(
                    held[group].at[here, j] if split else held[group].at[here], target.at[here], out_sems.at[at, j]
                )
                for j, target in enumerate(mine)
            ])
    for load in loads:
        load.start()
    for load, store in zip(loads, stores):
        load.wait()
        for copy in store:
            copy.start()
    for store in stores:
        for copy in store:
            copy.wait()


def pack(*groups):
    shapes = [(len(parts) * parts[0].shape[0],) + parts[0].shape[1:] for parts, _ in groups]
    out = []
    for shape, (_, split) in zip(shapes, groups):
        out += [shape[:1] + shape[2:]] * 2 if split else [shape]
    parts = [p for group, _ in groups for p in group]
    return list(pl.pallas_call(
        functools.partial(pack_kernel, [(len(p), int(split)) for p, split in groups]),
        out_shape=[jax.ShapeDtypeStruct(o, BF) for o in out],
        in_specs=[HBM] * len(parts),
        out_specs=[HBM] * len(out),
        scratch_shapes=[pltpu.VMEM(shape, BF) for shape in shapes]
        + [pltpu.SemaphoreType.DMA((len(parts),)), pltpu.SemaphoreType.DMA((len(parts), 2))],
        compiler_params=params(12),
        cost_estimate=cost(0, 2e6),
        name="pack",
    )(*parts))


class Line:
    def __init__(self):
        self.mark = None

    def tie(self, value):
        if self.mark is None:
            return value
        value, self.mark = lax.optimization_barrier((value, self.mark))
        return value


class Chain:
    def __init__(self, terms=(), halves=(), upper=None, pieces=(), joins=()):
        self.terms = list(terms)
        self.upper = upper
        self.pieces = list(pieces)
        self.steps = [("part", group) for group in halves] + [("join", group) for group in joins]

    def masks(self, group):
        count = 1 << len(group)
        masks = []
        for place in range(1, count):
            digits = [DIGITS[d] for i, d in enumerate(group) if place & (count >> (i + 1))]
            masks.append((sum(d[0] for d in digits), sum(d[1] for d in digits)))
        return masks

    def total_here(self):
        return add(*self.terms)

    def total(self):
        value = add(*self.terms)
        mask = 8
        while mask < lax.axis_size("batch"):
            value = add(value, swap(value, "batch", mask))
            mask *= 2
        return value

    def offers(self):
        kind, what = self.steps[0]
        if kind == "join":
            return self.pieces
        if self.upper is not None:
            sent, self.upper = [self.upper], None
            return sent
        count = 1 << len(what)
        size = self.terms[0].shape[0] // count
        sent = [add(*[t[i * size:(i + 1) * size] for t in self.terms]) for i in range(1, count)]
        self.terms = [t[:size] for t in self.terms]
        return sent

    def start(self, sent):
        kind, what = self.steps[0]
        masks = self.masks(what)
        if kind == "join":
            return [swap_digits(s, mask) for mask in masks for s in sent]
        return [swap_digits(s, mask) for s, mask in zip(sent, masks)]

    def take(self, moved):
        kind, _ = self.steps.pop(0)
        if kind == "join":
            self.pieces = self.pieces + list(moved)
        else:
            self.terms = self.terms + list(moved)


class Flight:
    def __init__(self, line):
        self.line = line
        self.parts = {}

    def land(self, *names):
        names = [n for n in (names or tuple(self.parts)) if n in self.parts]
        if not names:
            return {}
        held = [self.parts.pop(n) for n in names]
        got = self.line.tie(held)
        self.line.mark = got
        for name, moved in zip(names, got):
            if isinstance(name, Chain):
                name.take(moved)
        return {n: g for n, g in zip(names, got) if not isinstance(n, Chain)}

    def launch(self, *items):
        items = [i for i in items if not isinstance(i, Chain) or i.steps]
        arrays = [i.offers() if isinstance(i, Chain) else list(i[1]) for i in items]
        arrays = self.line.tie(arrays)
        self.line.mark = arrays
        for item, sent in zip(items, arrays):
            if isinstance(item, Chain):
                self.parts[item] = item.start(sent)
            else:
                name, _, axis, mask = item
                self.parts[name] = [swap(a, axis, mask) for a in sent]


def place_in(order):
    place = 0
    for digit in "".join(order):
        batch, band = DIGITS[digit]
        bit = lax.axis_index("batch") // batch if batch else lax.axis_index("band") // band
        place = place * 2 + bit % 2
    return place


ORDERS = (("z", "x", "yw"), ("y", "x", "zw"))
LAST_ORDERS = (("x", "y"), ("y", "x"))


def body(
    tokens, w_qkv, w_proj, w_fc1, w_fc2, gain_one, gain_two, cotangent, band_counts, slot_live
):
    slots, rows, width = tokens.shape
    flat = (slots * rows, width)
    band = lax.axis_index("band")
    core = band % 2
    meta = jnp.stack(
        [band, core] + [place_in(o) for o in ORDERS + tuple(order + ("zw",) for order in LAST_ORDERS) + ("x", "y", "z", "w")]
    ).astype(jnp.int32)
    gain_one = gain_one[None]
    gain_two = gain_two[None]
    at = (band_counts, slot_live, meta)
    line = Line()

    tokens, *tokens_other = lax.optimization_barrier(
        (tokens,) + tuple(tokens[s:s + 1] for s in range(slots))
    )
    tokens_other = [swap(t, "band", 2) for t in tokens_other]
    cotangent_p = swap(cotangent, "band", 1)
    first_own, query, kv_own = project(tokens, w_qkv, gain_one)
    tables = weigh_steps(QUERY_UNITS), weigh_steps(VALUE_UNITS)
    steps_theirs = jnp.where(core == 1, *tables)
    steps_ours = jnp.where(core == 0, *tables)
    line.mark = (first_own, meta, gain_two, steps_theirs, steps_ours)
    first_other, pairs = [], []
    seconds, seconds_p = [], []
    kept = ()

    def take(s):
        first, pair = project_other(s, line.tie(tokens_other[s]), kv_own, w_qkv, gain_one, first_other)
        line.mark = pair
        first_other[:] = [first]
        pairs.append((pair, swap(pair, "band", 1)))

    def look(s):
        *out, second = attend(s, *at, line.tie(query), *pairs[s], tokens, w_proj, gain_two, kept)
        line.mark = second
        seconds.append(second)
        seconds_p.append(swap(second, "band", 1))
        return tuple(out)

    take(0)
    for s in range(slots):
        if s == 1:
            for n in range(1, slots):
                take(n)
            cotangent_p = line.tie(cotangent_p)
        kept = look(s)
    attended, lse, hidden = kept

    flight = Flight(line)
    chains = []
    acts, pres = [], []
    all_seconds = seconds + seconds_p
    for half in range(2):
        act, pre, lower, upper = mlp(
            *at, [line.tie(all_seconds[0])] + all_seconds[1:], cotangent, cotangent_p, w_fc1, w_fc2, half
        )
        line.mark = upper
        acts.append(act)
        pres.append(pre)
        chains.append(Chain((lower,), ORDERS[half], upper))
        flight.launch(chains[half])
    one, two = chains
    turn_parts = lend(True, 2, meta, line.tie(pres[0]), pres[1], w_fc1)
    line.mark = turn_parts
    flight.launch(("turn", turn_parts, "band", 1))
    got = flight.land("turn")
    flight.land(one)
    flight.launch(one)
    branch, grad_attended, delta = turn(
        *at, line.tie(pres[0]), pres[1], w_fc1, *got["turn"], hidden, cotangent, attended, gain_two, w_proj
    )
    line.mark = delta

    grad_query, sums, keeps, waiting = (), (), [], []

    def bring(s):
        *kept_sums, partial = gather(s, slots, line.tie(keeps[s]), got[f"send{s}"][0], w_qkv, sums)
        line.mark = partial
        return tuple(kept_sums), [(f"partial{s}", [partial], "band", 2)]

    for s in range(slots):
        query_grad, keep, send = attend_back(
            s, *at, line.tie(query), *pairs[s], grad_attended, lse, delta, grad_query
        )
        line.mark = send
        grad_query = (query_grad,)
        keeps.append(keep)
        got.update(flight.land())
        if s < slots - 1:
            flight.launch((f"send{s}", [send], "band", 1), two, one)
            if s > 0:
                sums, waiting = bring(s - 1)
                flight.launch(*waiting)
    both = Chain(pieces=[jnp.stack([one.total(), two.total()], axis=1)], joins=("w",))
    flight.launch((f"send{slots - 1}", [send], "band", 1), both)
    if slots > 1:
        sums, waiting = bring(slots - 2)
        flight.launch(*waiting)
    got.update(flight.land(f"send{slots - 1}"))
    sums, waiting = bring(slots - 1)
    arrays = (first_own, first_other[0], grad_query[0], *sums, attended, branch)
    theirs = weigh(meta, steps_theirs, (line.tie(first_own),) + arrays[1:])
    line.mark = theirs
    finish_part = lend(False, 1, meta, line.tie(acts[0]), acts[1], w_fc2)
    line.mark = (theirs, finish_part)

    got.update(flight.land())
    left, right = pack((both.pieces, True))
    one = Chain(pieces=[left], joins=("y", "z", "x"))
    two = Chain(pieces=[right], joins=("x", "z", "y"))
    flight.launch(("theirs", [theirs], "band", 1), ("finish", finish_part, "band", 1), one, two)
    ours = weigh(meta, steps_ours, (line.tie(first_own),) + arrays[1:])
    line.mark = ours

    got.update(flight.land())
    (theirs,) = got["theirs"]
    three = Chain((ours[0], theirs[0]), LAST_ORDERS[0])
    four = Chain((ours[1], theirs[1]), LAST_ORDERS[1])
    left, right = pack((one.pieces, False), (two.pieces, False))
    one.pieces, two.pieces = [left], [right]
    flight.launch(three, four, one, two, *waiting)
    output = finish(*at, line.tie(acts[0]), acts[1], w_fc2, got["finish"][0], hidden)
    line.mark = output

    flight.land(three, four)
    flight.launch(three, four)

    got.update(flight.land(one, two, f"partial{slots - 1}"))
    left, right = pack((one.pieces, False), (two.pieces, False))
    one.pieces, two.pieces = [left], [right]
    line.mark = (left, right)
    flight.land(three, four)
    five = Chain((jnp.stack([three.total_here(), four.total_here()], axis=1),), ("zw",))
    flight.launch(five, one, two)
    partials = [got[f"partial{s}"][0] for s in range(slots)]
    grad_input = close(
        line.tie(grad_query[0]), sums[0], sums[1], partials, tokens, branch, gain_one, w_qkv
    )
    line.mark = grad_input

    flight.land(five)
    five = Chain(pieces=[five.total()], joins=("zw",))
    flight.launch(five)

    flight.land(one, two)
    flight.land(five)
    halves = pack((five.pieces, True))
    three = Chain(pieces=halves[:1], joins=("y", "x"))
    four = Chain(pieces=halves[1:], joins=("x", "y"))
    flight.launch(three, four, ("one", one.pieces, "band", 1), ("two_held", two.pieces[:1], "band", 1))

    got.update(flight.land())
    held = pack((three.pieces, False), (four.pieces, False))
    three.pieces, four.pieces = held[:1], held[1:]
    flight.launch(three, four, ("two_rest", two.pieces[1:], "band", 1), ("qkv_held", held, "band", 1))
    got.update(flight.land("two_rest"))
    mlp_pieces = [line.tie(one.pieces[0]), one.pieces[1], *two.pieces]
    mlp_pieces += [*got["one"], got["two_held"][0], got["two_rest"][0]]
    grad_fc1, grad_fc2, norm2 = spread_mlp(meta, mlp_pieces, w_fc1, gain_two)
    line.mark = norm2

    got.update(flight.land())
    flight.launch(("qkv_rest", [three.pieces[1], four.pieces[1]], "band", 1))
    got.update(flight.land())
    last_pieces = three.pieces + four.pieces + [p for pair in zip(got["qkv_held"], got["qkv_rest"]) for p in pair]
    grad_qkv, grad_proj, norm1 = spread_qkv(meta, last_pieces, w_qkv, gain_one)
    return (output, grad_input, grad_qkv, grad_proj, grad_fc1, grad_fc2, norm1, norm2)


def solution(mesh):
    placed = (
        P("batch", "band", None),
        P(),
        P(),
        P(),
        P(),
        P(),
        P(),
        P("batch", "band", None),
        P("batch", None),
        P("batch"),
    )
    return jax.shard_map(
        body,
        mesh=mesh,
        in_specs=placed,
        out_specs=(
            P("batch", "band", None),
            P("batch", "band", None),
            P(),
            P(),
            P(),
            P(),
            P(),
            P(),
        ),
        check_vma=False,
    )
```

```python
import functools
import jax
import jax.numpy as jnp
from jax import lax
from jax.experimental import pallas as pl
from jax.experimental.pallas import tpu as pltpu
from jax.sharding import PartitionSpec as P

BF = jnp.bfloat16
F32 = jnp.float32
EPSILON = 1e-06
HEAD_DIM = 64
GROUP = 256
NN = (((1,), (0,)), ((), ()))
NT = (((1,), (1,)), ((), ()))
TN = (((0,), (0,)), ((), ()))


def dot(left, right, dims=NN):
    return lax.dot_general(left, right, dims, preferred_element_type=F32)


def params(mib=60):
    return pltpu.CompilerParams(vmem_limit_bytes=mib * 1024 * 1024)


def cost(flops, moved, exps=0):
    return pl.CostEstimate(flops=1, bytes_accessed=1, transcendentals=0)


HBM = pl.BlockSpec(memory_space=pl.ANY)
STAY = pl.BlockSpec(memory_space=pltpu.HBM)


def normalized(values):
    centered = values - jnp.mean(values, axis=-1, keepdims=True)
    spread = jnp.mean(centered * centered, axis=-1, keepdims=True)
    scale = lax.rsqrt(spread + EPSILON)
    return centered * scale, scale


def project_kernel(tokens, weight, gain, first_in, query, both):
    normed, _ = normalized(tokens[0].astype(F32))
    first = (normed * gain[...]).astype(BF)
    first_in[0] = first
    width = first.shape[1]
    query[0] = (dot(first, weight[:, :width]) * HEAD_DIM ** -0.5).astype(BF)
    both[0, 0] = dot(first, weight[:, width:2 * width]).astype(BF)
    both[0, 1] = dot(first, weight[:, 2 * width:]).astype(BF)


def project(tokens, w_qkv, gain):
    slots, rows, width = tokens.shape
    row_spec = pl.BlockSpec((1, rows, width), lambda s: (s, 0, 0))
    return pl.pallas_call(
        project_kernel,
        out_shape=[
            pltpu.HBM(tokens.shape, BF),
            jax.ShapeDtypeStruct(tokens.shape, BF),
            jax.ShapeDtypeStruct((slots, 2, rows, width), BF),
        ],
        grid=(slots,),
        in_specs=[
            row_spec,
            pl.BlockSpec((width, 3 * width), lambda s: (0, 0)),
            pl.BlockSpec((1, width), lambda s: (0, 0)),
        ],
        out_specs=[row_spec, row_spec, pl.BlockSpec((1, 2, rows, width), lambda s: (s, 0, 0, 0))],
        compiler_params=params(14),
        cost_estimate=cost(2 * slots * rows * width * width * 3, 8e6),
        name="project",
    )(tokens, w_qkv, gain)


def project_other_kernel(tokens, own, weight, gain, *refs):
    first_in, both = refs[-2:]
    normed, _ = normalized(tokens[0].astype(F32))
    first = (normed * gain[...]).astype(BF)
    first_in[0] = first
    width = first.shape[1]
    both[0] = own[0]
    both[1, 0] = dot(first, weight[:, :width]).astype(BF)
    both[1, 1] = dot(first, weight[:, width:]).astype(BF)


def project_other(slot, tokens, kv_own, w_qkv, gain, before):
    slots, _, rows, width = kv_own.shape
    return pl.pallas_call(
        project_other_kernel,
        out_shape=[
            jax.ShapeDtypeStruct((slots, rows, width), BF),
            jax.ShapeDtypeStruct((2, 2, rows, width), BF),
        ],
        grid=(1,),
        in_specs=[
            pl.BlockSpec((1, rows, width), lambda i: (0, 0, 0)),
            pl.BlockSpec((1, 2, rows, width), lambda i: (slot, 0, 0, 0)),
            pl.BlockSpec((pl.Element(width), pl.Element(2 * width)), lambda i: (0, width)),
            pl.BlockSpec((1, width), lambda i: (0, 0)),
        ] + [HBM] * len(before),
        out_specs=[
            pl.BlockSpec((1, rows, width), lambda i: (slot, 0, 0)),
            pl.BlockSpec((2, 2, rows, width), lambda i: (0, 0, 0, 0)),
        ],
        input_output_aliases={4 + i: i for i in range(len(before))},
        compiler_params=params(10),
        cost_estimate=cost(2 * rows * width * width * 2, 5e6),
        name="project_other",
    )(tokens, kv_own, w_qkv, gain, *before)


def key_masks(counts, live, meta, slot, rows, flips, axis):
    shape = (rows, 1) if axis == 0 else (1, rows)
    place = lax.broadcasted_iota(jnp.int32, shape, axis)
    alive = live[slot] > 0
    return [place < jnp.where(alive, counts[slot, meta[0] ^ flip], 0) for flip in flips]


FLIPS = (0, 2, 1, 3)


def attend_kernel(slot, counts, live, meta, query, pair, pair_p, tokens, w_proj, gain, *refs):
    attended, lse, hidden, second, held, own_tokens, weight, sems = refs[-8:]
    group = pl.program_id(0)
    rows = query.shape[1]
    copies = (
        pltpu.make_async_copy(tokens.at[slot], own_tokens, sems.at[0]),
        pltpu.make_async_copy(w_proj, weight, sems.at[1]),
    )

    @pl.when(group == 0)
    def _():
        for copy in copies:
            copy.start()

    masks = key_masks(counts, live, meta, slot, rows, FLIPS, 1)
    q = query[0]
    lane = lax.broadcasted_iota(jnp.int32, (1, GROUP), 1)
    result = jnp.zeros((rows, GROUP), F32)
    sums = jnp.zeros((rows, 128), F32)
    lane128 = lax.broadcasted_iota(jnp.int32, (1, 128), 1)
    blocks = (pair.at[0], pair.at[1], pair_p.at[0], pair_p.at[1])

    def scores_of(h):
        qm = jnp.where((lane // HEAD_DIM) == h, q, jnp.zeros_like(q))
        return [jnp.where(mask, dot(qm, block[0], NT), -10000.0) for mask, block in zip(masks, blocks)]

    ahead = scores_of(0)
    for h in range(GROUP // HEAD_DIM):
        here = (lane // HEAD_DIM) == h
        scores = ahead
        if h + 1 < GROUP // HEAD_DIM:
            ahead = scores_of(h + 1)
        top = scores[0]
        for s in scores[1:]:
            top = jnp.maximum(top, s)
        top = jnp.max(top, axis=-1, keepdims=True)
        out = jnp.zeros((rows, GROUP), F32)
        exps = [jnp.exp(s - top) for s in scores]
        total = exps[0]
        for e in exps[1:]:
            total = total + e
        total = jnp.sum(total, axis=-1, keepdims=True)
        for e, block in zip(exps, blocks):
            out = out + dot(e.astype(BF), block[1])
        result = jnp.where(here, out * (1.0 / total), result)
        sums = jnp.where(lane128 == h, top + jnp.log(total), sums)
    low = result.astype(BF)
    attended[0] = low
    held[group] = low
    lse[0, 0] = sums.T[:8]

    @pl.when(group == pl.num_programs(0) - 1)
    def _():
        for copy in copies:
            copy.wait()
        value = own_tokens[...].astype(F32)
        for g in range(held.shape[0]):
            value = value + dot(held[g], weight[g * GROUP:(g + 1) * GROUP, :])
        hidden[0] = value
        normed, _ = normalized(value)
        second[...] = (normed * gain[...]).astype(BF)


def attend(slot, counts, live, meta, query, pair, pair_p, tokens, w_proj, gain, before):
    slots, rows, width = query.shape
    groups = width // GROUP
    at = slot
    kv_spec = pl.BlockSpec((2, 2, rows, GROUP), lambda g, *_: (0, 0, 0, g))
    piece = pl.BlockSpec((1, rows, GROUP), lambda g, *_: (at, 0, g))
    row_spec = pl.BlockSpec((1, rows, width), lambda g, *_: (at, 0, 0))
    operands = (counts, live, meta, query, pair, pair_p, tokens, w_proj, gain)
    return pl.pallas_call(
        functools.partial(attend_kernel, slot),
        out_shape=[
            jax.ShapeDtypeStruct(query.shape, BF),
            jax.ShapeDtypeStruct((slots, groups, 8, rows), F32),
            jax.ShapeDtypeStruct(query.shape, F32),
            jax.ShapeDtypeStruct((rows, width), BF),
        ],
        grid_spec=pltpu.PrefetchScalarGridSpec(
            num_scalar_prefetch=3,
            grid=(groups,),
            in_specs=[piece, kv_spec, kv_spec, HBM, HBM, pl.BlockSpec((1, width), lambda g, *_: (0, 0))]
            + [HBM] * len(before),
            out_specs=[
                piece,
                pl.BlockSpec((1, 1, 8, rows), lambda g, *_: (at, g, 0, 0)),
                row_spec,
                pl.BlockSpec((rows, width), lambda g, *_: (0, 0)),
            ],
            scratch_shapes=[
                pltpu.VMEM((groups, rows, GROUP), BF),
                pltpu.VMEM((rows, width), BF),
                pltpu.VMEM((width, width), BF),
                pltpu.SemaphoreType.DMA((2,)),
            ],
        ),
        input_output_aliases={len(operands) + i: i for i in range(len(before))},
        compiler_params=params(14),
        cost_estimate=cost(2 * 2 * rows * 4 * rows * 4 * width, 1e7, 12 * rows * 4 * rows),
        name="attend",
    )(*operands, *before)


def attend_back_kernel(
    slot, counts, live, meta, query, pair, pair_p, grad, lse, delta, *refs
):
    grad_query, grad_keep, grad_send, probs, slopes, qms, gms, keys, values, keys_t = refs[-10:]
    rows = query.shape[1]
    heads = GROUP // HEAD_DIM
    masks = key_masks(counts, live, meta, slot, rows, FLIPS, 0)
    q = query[0]
    ga = grad[0]
    lane = lax.broadcasted_iota(jnp.int32, (1, GROUP), 1)
    zero = jnp.zeros_like(q)
    for h in range(heads):
        here = (lane // HEAD_DIM) == h
        qms[h * rows:(h + 1) * rows, :] = jnp.where(here, q, zero)
        gms[h * rows:(h + 1) * rows, :] = jnp.where(here, ga, zero)
    for i, mask in enumerate(masks):
        block = (pair, pair_p)[i // 2]
        keys[i * rows:(i + 1) * rows, :] = jnp.where(mask, block[i % 2, 0], zero)
        values[i * rows:(i + 1) * rows, :] = block[i % 2, 1]
    keys_t[...] = keys[...].T
    gq = []
    for h in range(heads):
        mine = slice(h * rows, (h + 1) * rows)
        for i, mask in enumerate(masks):
            at = slice(i * rows, (i + 1) * rows)
            scores = jnp.where(mask, dot(keys[at, :], qms[mine, :], NT), -10000.0)
            gp = dot(values[at, :], gms[mine, :], NT)
            p = jnp.exp(scores - lse[0, 0, h:h + 1, :])
            probs[at, mine] = p.astype(BF)
            slopes[at, mine] = (p * (gp - delta[0, 0, h:h + 1, :])).astype(BF)
        gq.append(dot(keys_t[h * HEAD_DIM:(h + 1) * HEAD_DIM, :], slopes[:, mine]))
    gk = dot(slopes[...], qms[...])
    gv = dot(probs[...], gms[...])
    outs = ((grad_keep, 0), (grad_keep, 1), (grad_send, 0), (grad_send, 1))
    for i, ((out, place), mask) in enumerate(zip(outs, masks)):
        at = slice(i * rows, (i + 1) * rows)
        out[0, place, 0] = jnp.where(mask, gk[at], 0.0).astype(BF)
        out[0, place, 1] = gv[at].astype(BF)
    grad_query[0] = (jnp.concatenate(gq, axis=0).T * HEAD_DIM ** -0.5).astype(BF)


def attend_back(slot, counts, live, meta, query, pair, pair_p, grad, lse, delta, before):
    slots, rows, width = query.shape
    groups = width // GROUP
    heads = GROUP // HEAD_DIM
    at = slot
    kv_spec = pl.BlockSpec((2, 2, rows, GROUP), lambda g, *_: (0, 0, 0, g))
    row_spec = pl.BlockSpec((1, rows, GROUP), lambda g, *_: (at, 0, g))
    stat_spec = pl.BlockSpec((1, 1, 8, rows), lambda g, *_: (at, g, 0, 0))
    out_spec = pl.BlockSpec((1, 2, 2, rows, GROUP), lambda g, *_: (0, 0, 0, 0, g))
    operands = (counts, live, meta, query, pair, pair_p, grad, lse, delta)
    return pl.pallas_call(
        functools.partial(attend_back_kernel, slot),
        out_shape=[
            jax.ShapeDtypeStruct(query.shape, BF),
            jax.ShapeDtypeStruct((1, 2, 2, rows, width), BF),
            jax.ShapeDtypeStruct((1, 2, 2, rows, width), BF),
        ],
        grid_spec=pltpu.PrefetchScalarGridSpec(
            num_scalar_prefetch=3,
            grid=(groups,),
            in_specs=[row_spec, kv_spec, kv_spec, row_spec, stat_spec, stat_spec]
            + [pl.BlockSpec(memory_space=pl.ANY)] * len(before),
            out_specs=[row_spec, out_spec, out_spec],
            scratch_shapes=[
                pltpu.VMEM((4 * rows, heads * rows), BF),
                pltpu.VMEM((4 * rows, heads * rows), BF),
                pltpu.VMEM((heads * rows, GROUP), BF),
                pltpu.VMEM((heads * rows, GROUP), BF),
                pltpu.VMEM((4 * rows, GROUP), BF),
                pltpu.VMEM((4 * rows, GROUP), BF),
                pltpu.VMEM((GROUP, 4 * rows), BF),
            ],
        ),
        input_output_aliases={len(operands) + i: i for i in range(len(before))},
        compiler_params=params(18),
        cost_estimate=cost(5 * 2 * rows * 4 * rows * 4 * width, 2e7, 12 * rows * 4 * rows),
        name="attend_back",
    )(*operands, *before)


CHUNKS = 16


def row_mask(counts, live, meta, slot, rows):
    return key_masks(counts, live, meta, slot, rows, (0,), 0)[0]


def gelu_parts(v):
    size = jnp.abs(v)
    decay = jnp.exp2(v * v * (-0.5 * 1.4426950408889634))
    scale = 1.0 + (0.3275911 * 0.7071067811865476) * size
    t = pl.reciprocal(scale, approx=True)
    t = t * (2.0 - scale * t)
    poly = t * (0.127414796 + t * (-0.142248368 + t * (0.7107068705 + t * (-0.7265760135 + t * 0.5307027145))))
    tail = poly * decay
    phi = jnp.where(v >= 0, 1.0 - tail, tail)
    return phi, decay * 0.3989422804014327


def mlp_kernel(slots, half, counts, live, meta, *refs):
    seconds, rest = refs[:2 * slots], refs[2 * slots:]
    cot, cot_p, w_in, w_out, act_out, pre_out, *grads_out = rest[:8]
    sec, go, win, wout, act, pre, grads, sems, out_sems = rest[8:]
    rows = seconds[0].shape[0]
    count = slots * rows
    width = sec.shape[1]
    me = meta[2 + half]
    part = pl.multiple_of((2 * meta[1] + half) * width, width)

    def copies_for(side):
        whole = pl.ds(side * count, count)
        out = [
            pltpu.make_async_copy(
                seconds[side * slots + s], sec.at[pl.ds(side * count + s * rows, rows)], sems.at[side * (slots + 1) + s]
            )
            for s in range(slots)
        ]
        source = (cot, cot_p)[side]
        return out, pltpu.make_async_copy(source, go.at[whole], sems.at[side * (slots + 1) + slots])

    last = 2 * (slots + 1)
    load_in = pltpu.make_async_copy(w_in.at[:, pl.ds(part, width)], win, sems.at[last])
    load_out = pltpu.make_async_copy(w_out.at[pl.ds(part, width), :], wout, sems.at[last + 1])
    sides = [copies_for(side) for side in range(2)]
    for c in sides[0][0]:
        c.start()
    load_in.start()
    sides[0][1].start()
    load_out.start()
    for c in sides[1][0]:
        c.start()
    sides[1][1].start()
    stores = []

    def store(source, target):
        copy = pltpu.make_async_copy(source, target, out_sems.at[len(stores)])
        copy.start()
        stores.append(copy)

    def activate(at, before, grad_act):
        phi, density = gelu_parts(before)
        act[at, :] = (before * phi).astype(BF)
        pre[at, :] = (grad_act * (phi + before * density)).astype(BF)

    own = slice(0, count)
    for c in sides[0][0]:
        c.wait()
    load_in.wait()
    before = dot(sec[own, :], win[...])
    sides[0][1].wait()
    load_out.wait()
    for c in sides[1][0]:
        c.wait()
    sides[1][1].wait()
    for side in range(2):
        for s in range(slots):
            mask = key_masks(counts, live, meta, s, rows, (side,), 0)[0]
            here = slice(side * count + s * rows, side * count + (s + 1) * rows)
            go[here, :] = jnp.where(mask, go[here, :], jnp.zeros((rows, width), BF))
    activate(own, before, dot(go[own, :], wout[...], NT))
    for s in range(slots):
        at = slice(count + s * rows, count + (s + 1) * rows)
        activate(at, dot(sec[at, :], win[...]), dot(go[at, :], wout[...], NT))
    for side in range(2):
        window = pl.ds(side * count, count)
        store(act.at[window], act_out.at[window])
        store(pre.at[window], pre_out.at[window])
    size = width // CHUNKS
    for kind, (left, right) in ((1, (act, go)), (0, (sec, pre))):
        value = dot(left[...], right[...], TN)
        for a in range(CHUNKS):
            grads[kind, a ^ me] = value[a * size:(a + 1) * size].astype(BF)
        for i, out in enumerate(grads_out):
            store(grads.at[kind, pl.ds(i * CHUNKS // 2, CHUNKS // 2)], out.at[:, kind])
    for copy in stores:
        copy.wait()


def mlp(counts, live, meta, seconds, cotangent, cotangent_p, w_fc1, w_fc2, half):
    rows, width = seconds[0].shape
    slots = len(seconds) // 2
    both = 2 * slots * rows
    operands = (*seconds, cotangent.reshape(slots * rows, width), cotangent_p.reshape(slots * rows, width), w_fc1, w_fc2)
    return pl.pallas_call(
        functools.partial(mlp_kernel, slots, half),
        out_shape=[
            pltpu.HBM((both, width), BF),
            pltpu.HBM((both, width), BF),
        ]
        + [jax.ShapeDtypeStruct((CHUNKS // 2, 2, width // CHUNKS, width), BF)] * 2,
        grid_spec=pltpu.PrefetchScalarGridSpec(
            num_scalar_prefetch=3,
            grid=(1,),
            in_specs=[HBM] * (len(operands) - 2) + [STAY] * 2,
            out_specs=[STAY] * 2 + [HBM] * 2,
            scratch_shapes=[pltpu.VMEM((both, width), BF)] * 2
            + [pltpu.VMEM((width, width), BF)] * 2
            + [pltpu.VMEM((both, width), BF)] * 2
            + [
                pltpu.VMEM((2, CHUNKS, width // CHUNKS, width), BF),
                pltpu.SemaphoreType.DMA((2 * (slots + 1) + 2,)),
                pltpu.SemaphoreType.DMA((8,)),
            ],
        ),
        compiler_params=params(24),
        cost_estimate=cost(2 * 4 * 2 * slots * rows * width * width, 2e7),
        name="mlp",
    )(counts, live, meta, *operands)


def lend_kernel(nt, meta, first, second, weight, *refs):
    outs, (left, held, sems) = refs[:-3], refs[-3:]
    _, count, width = left.shape
    core = meta[1]
    loads = []
    for i, source in enumerate((first, second)):
        place = pl.ds(pl.multiple_of((2 * core + i) * width, width), width)
        loads.append(pltpu.make_async_copy(source.at[pl.ds(count, count)], left.at[i], sems.at[2 * i]))
        part = weight.at[:, place] if nt else weight.at[place, :]
        loads.append(pltpu.make_async_copy(part, held.at[i], sems.at[2 * i + 1]))
    for load in loads:
        load.start()
    dims = NT if nt else NN
    loads[0].wait()
    loads[1].wait()
    total = dot(left[0], held[0], dims)
    loads[2].wait()
    loads[3].wait()
    total = (total + dot(left[1], held[1], dims)).astype(BF)
    size = count // len(outs)
    for i, out in enumerate(outs):
        out[...] = total[i * size:(i + 1) * size]


def lend(nt, parts, meta, first, second, weight):
    both, width = first.shape
    size = both // 2 // parts
    return pl.pallas_call(
        functools.partial(lend_kernel, nt),
        out_shape=[jax.ShapeDtypeStruct((size, width), BF)] * parts,
        grid_spec=pltpu.PrefetchScalarGridSpec(
            num_scalar_prefetch=1,
            grid=(1,),
            in_specs=[STAY] * 3,
            out_specs=[pl.BlockSpec((size, width), lambda i, *_: (0, 0))] * parts,
            scratch_shapes=[
                pltpu.VMEM((2, both // 2, width), BF),
                pltpu.VMEM((2, width, width), BF),
                pltpu.SemaphoreType.DMA((4,)),
            ],
        ),
        compiler_params=params(10),
        cost_estimate=cost(2 * both * width * width, 6e6),
        name="lend",
    )(meta, first, second, weight)


def layer_norm_back(values, gain, grad):
    normed, scale = normalized(values)
    t = grad * gain
    return scale * (t - jnp.mean(t, axis=-1, keepdims=True) - normed * jnp.mean(t * normed, axis=-1, keepdims=True))


def turn_kernel(
    counts, live, meta, first, second, weight, got, also, hidden, cotangent, attended, gain, w_proj,
    grad_branch, grad_attended, delta, left, held, got_v, hidden_v, cot_v, att_v, proj_v, sems,
):
    slots, rows, width = grad_branch.shape
    count = slots * rows
    core = meta[1]
    loads = []
    for i, source in enumerate((first, second)):
        place = pl.ds(pl.multiple_of((2 * core + i) * width, width), width)
        loads.append(pltpu.make_async_copy(source.at[pl.ds(0, count)], left.at[i], sems.at[2 * i]))
        loads.append(pltpu.make_async_copy(weight.at[:, place], held.at[i], sems.at[2 * i + 1]))
    for i, (source, target) in enumerate(
        (
            (got, got_v.at[pl.ds(0, count // 2)]), (also, got_v.at[pl.ds(count // 2, count // 2)]),
            (hidden, hidden_v), (cotangent, cot_v), (w_proj, proj_v), (attended, att_v),
        )
    ):
        loads.append(pltpu.make_async_copy(source, target, sems.at[4 + i]))
    for load in loads:
        load.start()
    loads[0].wait()
    loads[1].wait()
    total = dot(left[0], held[0], NT)
    loads[2].wait()
    loads[3].wait()
    total = total + dot(left[1], held[1], NT)
    for load in loads[4:]:
        load.wait()
    head = lax.broadcasted_iota(jnp.int32, (32, width), 0)
    column = lax.broadcasted_iota(jnp.int32, (32, width), 1) // HEAD_DIM
    per = GROUP // HEAD_DIM
    pick = (head == (column // per) * 8 + column % per).astype(BF)
    for s in range(slots):
        here = slice(s * rows, (s + 1) * rows)
        mask = row_mask(counts, live, meta, s, rows)
        grad_out = jnp.where(mask, cot_v[s].astype(F32), 0.0)
        given = total[here] + got_v[here, :].astype(F32)
        branch = (grad_out + layer_norm_back(hidden_v[s], gain[...], given)).astype(BF)
        grad_branch[s] = branch
        back = dot(branch, proj_v[...], NT).astype(BF)
        grad_attended[s] = back
        product = back.astype(F32) * att_v[s].astype(F32)
        high = product.astype(BF)
        low = (product - high.astype(F32)).astype(BF)
        sums = dot(pick, high, NT) + dot(pick, low, NT)
        for g in range(width // GROUP):
            delta[s, g] = sums[8 * g:8 * g + 8]


def turn(counts, live, meta, first, second, weight, got, also, hidden, cotangent, attended, gain, w_proj):
    slots, rows, width = hidden.shape
    count = slots * rows
    groups = width // GROUP
    whole = pl.BlockSpec(hidden.shape, lambda i, *_: (0, 0, 0))
    return pl.pallas_call(
        turn_kernel,
        out_shape=[
            jax.ShapeDtypeStruct(hidden.shape, BF),
            jax.ShapeDtypeStruct(hidden.shape, BF),
            jax.ShapeDtypeStruct((slots, groups, 8, rows), F32),
        ],
        grid_spec=pltpu.PrefetchScalarGridSpec(
            num_scalar_prefetch=3,
            grid=(1,),
            in_specs=[STAY] * 3 + [HBM] * 5 + [pl.BlockSpec((1, width), lambda i, *_: (0, 0)), HBM],
            out_specs=[whole, whole, pl.BlockSpec((slots, groups, 8, rows), lambda i, *_: (0, 0, 0, 0))],
            scratch_shapes=[
                pltpu.VMEM((2, count, width), BF),
                pltpu.VMEM((2, width, width), BF),
                pltpu.VMEM((count, width), BF),
                pltpu.VMEM(hidden.shape, F32),
                pltpu.VMEM(hidden.shape, BF),
                pltpu.VMEM(hidden.shape, BF),
                pltpu.VMEM((width, width), BF),
                pltpu.SemaphoreType.DMA((10,)),
            ],
        ),
        compiler_params=params(20),
        cost_estimate=cost(3 * 2 * slots * rows * width * width, 1.5e7),
        name="turn",
    )(counts, live, meta, first, second, weight, got, also, hidden, cotangent, attended, gain, w_proj)


def finish_kernel(counts, live, meta, first, second, weight, got, hidden, output, left, held, got_v, hidden_v, sems):
    slots, rows, width = output.shape
    count = slots * rows
    core = meta[1]
    loads = []
    for i, source in enumerate((first, second)):
        place = pl.ds(pl.multiple_of((2 * core + i) * width, width), width)
        loads.append(pltpu.make_async_copy(source.at[pl.ds(0, count)], left.at[i], sems.at[2 * i]))
        loads.append(pltpu.make_async_copy(weight.at[place, :], held.at[i], sems.at[2 * i + 1]))
    loads.append(pltpu.make_async_copy(got, got_v, sems.at[4]))
    loads.append(pltpu.make_async_copy(hidden, hidden_v, sems.at[5]))
    for load in loads:
        load.start()
    loads[0].wait()
    loads[1].wait()
    total = dot(left[0], held[0])
    loads[2].wait()
    loads[3].wait()
    total = total + dot(left[1], held[1])
    loads[4].wait()
    loads[5].wait()
    for s in range(slots):
        here = slice(s * rows, (s + 1) * rows)
        mask = row_mask(counts, live, meta, s, rows)
        output[s] = jnp.where(mask, total[here] + got_v[here, :].astype(F32) + hidden_v[s], 0.0).astype(BF)


def finish(counts, live, meta, first, second, weight, got, hidden):
    slots, rows, width = hidden.shape
    count = slots * rows
    return pl.pallas_call(
        finish_kernel,
        out_shape=jax.ShapeDtypeStruct(hidden.shape, BF),
        grid_spec=pltpu.PrefetchScalarGridSpec(
            num_scalar_prefetch=3,
            grid=(1,),
            in_specs=[STAY] * 3 + [HBM] * 2,
            out_specs=pl.BlockSpec(hidden.shape, lambda i, *_: (0, 0, 0)),
            scratch_shapes=[
                pltpu.VMEM((2, count, width), BF),
                pltpu.VMEM((2, width, width), BF),
                pltpu.VMEM((count, width), BF),
                pltpu.VMEM(hidden.shape, F32),
                pltpu.SemaphoreType.DMA((6,)),
            ],
        ),
        compiler_params=params(16),
        cost_estimate=cost(2 * 2 * slots * rows * width * width, 9e6),
        name="finish",
    )(counts, live, meta, first, second, weight, got, hidden)


def gather_kernel(mine, got, w_kv, *refs):
    key_own, value_own, key_other, value_other, partial = refs[-5:]
    width = partial.shape[-1]
    parts = []
    for place, out in ((0, (key_own, value_own)), (1, (key_other, value_other))):
        for i in range(2):
            total = (mine[0, place, i].astype(F32) + got[0, place, i].astype(F32)).astype(BF)
            out[i][0] = total
            parts.append(total)
    partial[0] = (dot(parts[2], w_kv[:, :width], NT) + dot(parts[3], w_kv[:, width:], NT)).astype(BF)


def gather(slot, slots, mine, got, w_qkv, before):
    _, _, _, rows, width = mine.shape
    row_spec = pl.BlockSpec((1, rows, width), lambda i: (slot, 0, 0))
    kv_spec = pl.BlockSpec((1, 2, 2, rows, width), lambda i: (0, 0, 0, 0, 0))
    return pl.pallas_call(
        gather_kernel,
        out_shape=[jax.ShapeDtypeStruct((slots, rows, width), BF)] * 4 + [jax.ShapeDtypeStruct((1, rows, width), BF)],
        grid=(1,),
        in_specs=[kv_spec, kv_spec, pl.BlockSpec((pl.Element(width), pl.Element(2 * width)), lambda s: (0, width))]
        + [pl.BlockSpec(memory_space=pl.ANY)] * len(before),
        out_specs=[row_spec] * 4 + [pl.BlockSpec((1, rows, width), lambda i: (0, 0, 0))],
        input_output_aliases={3 + i: i for i in range(len(before))},
        compiler_params=params(10),
        cost_estimate=cost(2 * 2 * rows * width * width, 6e6),
        name="gather",
    )(mine, got, w_qkv, *before)


VALUE_UNITS = ((0, 4, 1, 0, 0), (1, 6, 0, 1, 0), (7, 8, 1, 1, 1))
QUERY_UNITS = ((0, 2, 1, 1, 0), (0, 3, 1, 0, 1), (1, 5, 0, 1, 1))


def weigh_steps(units):
    seen = set()
    steps = []
    for step in units:
        steps.append(step + (int(step[0] not in seen),))
        seen.add(step[0])
    return jnp.array(steps, jnp.int32)


def weigh_kernel(meta, steps, *refs):
    sources, (grads, held, total, sems) = refs[:9], refs[9:]
    step = pl.program_id(0)
    size = held.shape[1] // CHUNKS
    values = steps[0, 1] == VALUE_UNITS[0][1]

    def start(units):
        seen = []
        for unit in units:
            for i in unit[:2]:
                if i not in seen:
                    seen.append(i)
                    pltpu.make_async_copy(sources[i], held.at[i], sems.at[i]).start()

    @pl.when(jnp.logical_and(step == 0, values))
    def _():
        start(VALUE_UNITS)

    @pl.when(jnp.logical_and(step == 0, jnp.logical_not(values)))
    def _():
        start(QUERY_UNITS)

    left = steps[step, 0]
    right = steps[step, 1]

    @pl.when(steps[step, 5] == 1)
    def _():
        pltpu.make_async_copy(sources[0], held.at[left], sems.at[left]).wait()

    pltpu.make_async_copy(sources[0], held.at[right], sems.at[right]).wait()

    @pl.when(steps[step, 2] == 1)
    def _():
        total[...] = dot(held[left], held[right], TN)

    @pl.when(steps[step, 2] != 1)
    def _():
        total[...] += dot(held[left], held[right], TN)

    @pl.when(steps[step, 3] == 1)
    def _():
        unit = steps[step, 4]
        me = meta[4 + unit]
        for a in range(CHUNKS):
            grads[unit, a ^ me] = total[a * size:(a + 1) * size, :].astype(BF)


def weigh(meta, steps, arrays):
    arrays = [a.reshape(-1, a.shape[-1]) for a in arrays]
    rows, width = arrays[0].shape
    shape = (2, CHUNKS, width // CHUNKS, width)
    return pl.pallas_call(
        weigh_kernel,
        out_shape=jax.ShapeDtypeStruct(shape, BF),
        grid_spec=pltpu.PrefetchScalarGridSpec(
            num_scalar_prefetch=2,
            grid=(3,),
            in_specs=[HBM] * 9,
            out_specs=pl.BlockSpec(shape, lambda i, *_: (0, 0, 0, 0)),
            scratch_shapes=[
                pltpu.VMEM((9, rows, width), BF),
                pltpu.VMEM((rows, width), F32),
                pltpu.SemaphoreType.DMA((9,)),
            ],
        ),
        compiler_params=params(19),
        cost_estimate=cost(3 * 2 * rows * width * width, 1e7),
        name="weigh",
    )(meta, steps, *arrays)


def close_kernel(gq, gk, gv, w_qkv, tokens, grad_hidden, gain, *refs):
    partials, (out, total) = refs[:-2], refs[-2:]
    step = pl.program_id(0)
    slots, rows, width = gq.shape
    flat = (slots * rows, width)

    @pl.when(step == 0)
    def _():
        total[...] = dot(gq[...].reshape(flat), w_qkv[...], NT)

    @pl.when(step == 1)
    def _():
        total[...] += dot(gk[...].reshape(flat), w_qkv[...], NT)

    @pl.when(step == 2)
    def _():
        total[...] += dot(gv[...].reshape(flat), w_qkv[...], NT)
        for s, partial in enumerate(partials):
            total[s * rows:(s + 1) * rows, :] += partial[0].astype(F32)

    @pl.when(step > 2)
    def _():
        first = total[pl.ds(pl.multiple_of((step - 3) * rows, rows), rows), :]
        out[0] = (grad_hidden[0].astype(F32) + layer_norm_back(tokens[0].astype(F32), gain[...], first)).astype(BF)


def close(gq, gk, gv, partials, tokens, grad_hidden, gain, w_qkv):
    slots, rows, width = tokens.shape
    row_spec = pl.BlockSpec((1, rows, width), lambda i: (jnp.maximum(i - 3, 0), 0, 0))
    whole = pl.BlockSpec((slots, rows, width), lambda i: (0, 0, 0))
    return pl.pallas_call(
        close_kernel,
        out_shape=jax.ShapeDtypeStruct(tokens.shape, BF),
        grid=(3 + slots,),
        in_specs=[whole] * 3 + [pl.BlockSpec((width, width), lambda i: (0, jnp.minimum(i, 2)))] + [row_spec] * 2 + [
            pl.BlockSpec((1, width), lambda i: (0, 0)),
        ] + [pl.BlockSpec((1, rows, width), lambda i: (0, 0, 0))] * slots,
        out_specs=row_spec,
        scratch_shapes=[pltpu.VMEM((slots * rows, width), F32)],
        compiler_params=params(18),
        cost_estimate=cost(3 * 2 * slots * rows * width * width, 1.2e7),
        name="close",
    )(gq, gk, gv, w_qkv, tokens, grad_hidden, gain, *partials)


SPREAD = 4


def keep_row_sums(held, value):
    step = pl.program_id(0)
    rows = value.shape[0]
    column = jnp.sum(value, axis=-1, keepdims=True)
    held[pl.ds(pl.multiple_of(step * rows, rows), rows), :] = jnp.broadcast_to(column, (rows, 128))


def put_row_sums(norm, held, gain):
    @pl.when(pl.program_id(0) == pl.num_programs(0) - 1)
    def _():
        for r in range(norm.shape[0]):
            norm[r:r + 1, :] = held[r * 128:(r + 1) * 128, :].T[:1] / gain[r:r + 1, :]


def load_pieces(groups, targets, sems):
    copies = []
    for group, target in zip(groups, targets):
        place = 0
        for piece in group:
            size = piece.shape[0]
            copies.append(pltpu.make_async_copy(piece, target.at[pl.ds(place, size)], sems.at[len(copies)]))
            place += size
    for copy in copies:
        copy.start()
    for copy in copies:
        copy.wait()


def spread_mlp_kernel(meta, *refs):
    pieces, (w_fc1, gain, grad_fc1, grad_fc2, norm, one, two, held, sems) = refs[:8], refs[8:]
    step = pl.program_id(0)
    size, width = one.shape[-2:]

    @pl.when(step == 0)
    def _():
        groups = [pieces[2 * i:2 * i + 2] for i in range(4)]
        load_pieces(groups, (one.at[0], two.at[0], one.at[1], two.at[1]), sems)

    mine = [meta[6 + i] for i in range(4)]
    for a in range(4):
        here = slice(a * size, (a + 1) * size)
        for half, held_chunks in enumerate((one, two)):
            high, low, third, fourth = step // 2, step % 2, a // 2, a % 2
            digits = (low, third, high, fourth) if half == 0 else (low, high, third, fourth)
            x, y, z, w = [d ^ m for d, m in zip(digits, mine)]
            place = x * 8 + z * 4 + y * 2 + w if half == 0 else y * 8 + z * 4 + x * 2 + w
            for core in range(2):
                value = held_chunks[core ^ meta[1], place].astype(F32)
                column = 2 * core + half
                grad_fc1[here, column * width:(column + 1) * width] = value[0]
                grad_fc2[column, here, :] = value[1]
    keep_row_sums(held, grad_fc1[...] * w_fc1[...].astype(F32))
    put_row_sums(norm, held, gain)


def spread_mlp(meta, pieces, w_fc1, gain):
    width, hidden_width = w_fc1.shape
    per = CHUNKS // SPREAD
    size = width // CHUNKS
    outs = pl.pallas_call(
        spread_mlp_kernel,
        out_shape=[
            jax.ShapeDtypeStruct((width, hidden_width), F32),
            jax.ShapeDtypeStruct((4, width, width), F32),
            jax.ShapeDtypeStruct((width // 128, 128), F32),
        ],
        grid_spec=pltpu.PrefetchScalarGridSpec(
            num_scalar_prefetch=1,
            grid=(SPREAD,),
            in_specs=[HBM] * 8 + [
                pl.BlockSpec((per * size, hidden_width), lambda a, *_: (a, 0)),
                pl.BlockSpec((width // 128, 128), lambda a, *_: (0, 0)),
            ],
            out_specs=[
                pl.BlockSpec((per * size, hidden_width), lambda a, *_: (a, 0)),
                pl.BlockSpec((4, per * size, width), lambda a, *_: (0, a, 0)),
                pl.BlockSpec((width // 128, 128), lambda a, *_: (0, 0)),
            ],
            scratch_shapes=[
                pltpu.VMEM((2, CHUNKS, 2, size, width), BF),
                pltpu.VMEM((2, CHUNKS, 2, size, width), BF),
                pltpu.VMEM((width, 128), F32),
                pltpu.SemaphoreType.DMA((8,)),
            ],
        ),
        compiler_params=params(26),
        cost_estimate=cost(1e6, 4.7e7),
        name="spread_mlp",
    )(meta, *pieces, w_fc1, gain.reshape(width // 128, 128))
    return outs[0], outs[1].reshape(hidden_width, width), outs[2].reshape(width)


def spread_qkv_kernel(meta, *refs):
    pieces, (w_qkv, gain, grad_qkv, grad_proj, norm, chunks, held, sems) = refs[:8], refs[8:]
    step = pl.program_id(0)
    size, width = chunks.shape[-2:]

    @pl.when(step == 0)
    def _():
        load_pieces([pieces[2 * i:2 * i + 2] for i in range(4)], [chunks.at[i] for i in range(4)], sems)

    high, low = step // 2, step % 2
    tops = (((high ^ meta[6]) * 2 + (low ^ meta[7])) * 4, ((high ^ meta[7]) * 2 + (low ^ meta[6])) * 4)
    own = 2 * meta[1]
    part = 2 - own
    for a in range(4):
        here = slice(a * size, (a + 1) * size)
        last = a ^ (meta[8] * 2 + meta[9])
        for i in range(3):
            unit = i % 2
            grad_qkv[here, i * width:(i + 1) * width] = chunks[
                (own if i < 2 else part) + unit, tops[unit] + last
            ].astype(F32)
        grad_proj[here, :] = chunks[part + 1, tops[1] + last].astype(F32)
    keep_row_sums(held, grad_qkv[...] * w_qkv[...].astype(F32))
    put_row_sums(norm, held, gain)


def spread_qkv(meta, pieces, w_qkv, gain):
    width = w_qkv.shape[0]
    size = width // CHUNKS
    per = CHUNKS // SPREAD

    def rows(columns):
        return pl.BlockSpec((per * size, columns), lambda a, *_: (a, 0))

    line = pl.BlockSpec((width // 128, 128), lambda a, *_: (0, 0))
    outs = pl.pallas_call(
        spread_qkv_kernel,
        out_shape=[
            jax.ShapeDtypeStruct((width, 3 * width), F32),
            jax.ShapeDtypeStruct((width, width), F32),
            jax.ShapeDtypeStruct((width // 128, 128), F32),
        ],
        grid_spec=pltpu.PrefetchScalarGridSpec(
            num_scalar_prefetch=1,
            grid=(SPREAD,),
            in_specs=[HBM] * 8 + [rows(3 * width), line],
            out_specs=[rows(3 * width), rows(width), line],
            scratch_shapes=[
                pltpu.VMEM((4, CHUNKS, size, width), BF),
                pltpu.VMEM((width, 128), F32),
                pltpu.SemaphoreType.DMA((8,)),
            ],
        ),
        compiler_params=params(18),
        cost_estimate=cost(1e6, 1.8e7),
        name="spread_qkv",
    )(meta, *pieces, w_qkv, gain.reshape(width // 128, 128))
    return outs[0], outs[1], outs[2].reshape(width)


DIGITS = {"x": (0, 2), "y": (1, 0), "z": (2, 0), "w": (4, 0)}


def swap(value, axis, mask):
    return lax.ppermute(value, axis, [(i, i ^ mask) for i in range(lax.axis_size(axis))])


def swap_digits(value, masks):
    batch, band = masks
    if not band:
        return swap(value, "batch", batch)
    if not batch:
        return swap(value, "band", band)
    return swap(value, ("batch", "band"), batch * lax.axis_size("band") + band)


def add(*values):
    total = values[0].astype(F32)
    for value in values[1:]:
        total = total + value.astype(F32)
    return total.astype(BF)


def pack_kernel(groups, *refs):
    total = sum(count for count, _ in groups)
    sources, refs = refs[:total], refs[total:]
    outs = sum(1 + split for _, split in groups)
    targets, refs = list(refs[:outs]), refs[outs:]
    held, (sems, out_sems) = refs[:len(groups)], refs[len(groups):]
    loads, stores = [], []
    for group, (count, split) in enumerate(groups):
        mine = [targets.pop(0) for _ in range(1 + split)]
        for i in range(count):
            at = len(loads)
            size = sources[at].shape[0]
            here = pl.ds(i * size, size)
            loads.append(pltpu.make_async_copy(sources[at], held[group].at[here], sems.at[at]))
            stores.append([
                pltpu.make_async_copy(
                    held[group].at[here, j] if split else held[group].at[here], target.at[here], out_sems.at[at, j]
                )
                for j, target in enumerate(mine)
            ])
    for load in loads:
        load.start()
    for load, store in zip(loads, stores):
        load.wait()
        for copy in store:
            copy.start()
    for store in stores:
        for copy in store:
            copy.wait()


def pack(*groups):
    shapes = [(len(parts) * parts[0].shape[0],) + parts[0].shape[1:] for parts, _ in groups]
    out = []
    for shape, (_, split) in zip(shapes, groups):
        out += [shape[:1] + shape[2:]] * 2 if split else [shape]
    parts = [p for group, _ in groups for p in group]
    return list(pl.pallas_call(
        functools.partial(pack_kernel, [(len(p), int(split)) for p, split in groups]),
        out_shape=[jax.ShapeDtypeStruct(o, BF) for o in out],
        in_specs=[HBM] * len(parts),
        out_specs=[HBM] * len(out),
        scratch_shapes=[pltpu.VMEM(shape, BF) for shape in shapes]
        + [pltpu.SemaphoreType.DMA((len(parts),)), pltpu.SemaphoreType.DMA((len(parts), 2))],
        compiler_params=params(12),
        cost_estimate=cost(0, 2e6),
        name="pack",
    )(*parts))


class Line:
    def __init__(self):
        self.mark = None

    def tie(self, value):
        if self.mark is None:
            return value
        value, self.mark = lax.optimization_barrier((value, self.mark))
        return value


class Chain:
    def __init__(self, terms=(), halves=(), upper=None, pieces=(), joins=()):
        self.terms = list(terms)
        self.upper = upper
        self.pieces = list(pieces)
        self.steps = [("part", group) for group in halves] + [("join", group) for group in joins]

    def masks(self, group):
        count = 1 << len(group)
        masks = []
        for place in range(1, count):
            digits = [DIGITS[d] for i, d in enumerate(group) if place & (count >> (i + 1))]
            masks.append((sum(d[0] for d in digits), sum(d[1] for d in digits)))
        return masks

    def total_here(self):
        return add(*self.terms)

    def total(self):
        value = add(*self.terms)
        mask = 8
        while mask < lax.axis_size("batch"):
            value = add(value, swap(value, "batch", mask))
            mask *= 2
        return value

    def offers(self):
        kind, what = self.steps[0]
        if kind == "join":
            return self.pieces
        if self.upper is not None:
            sent, self.upper = [self.upper], None
            return sent
        count = 1 << len(what)
        size = self.terms[0].shape[0] // count
        sent = [add(*[t[i * size:(i + 1) * size] for t in self.terms]) for i in range(1, count)]
        self.terms = [t[:size] for t in self.terms]
        return sent

    def start(self, sent):
        kind, what = self.steps[0]
        masks = self.masks(what)
        if kind == "join":
            return [swap_digits(s, mask) for mask in masks for s in sent]
        return [swap_digits(s, mask) for s, mask in zip(sent, masks)]

    def take(self, moved):
        kind, _ = self.steps.pop(0)
        if kind == "join":
            self.pieces = self.pieces + list(moved)
        else:
            self.terms = self.terms + list(moved)


class Flight:
    def __init__(self, line):
        self.line = line
        self.parts = {}

    def land(self, *names):
        names = [n for n in (names or tuple(self.parts)) if n in self.parts]
        if not names:
            return {}
        held = [self.parts.pop(n) for n in names]
        got = self.line.tie(held)
        self.line.mark = got
        for name, moved in zip(names, got):
            if isinstance(name, Chain):
                name.take(moved)
        return {n: g for n, g in zip(names, got) if not isinstance(n, Chain)}

    def launch(self, *items):
        items = [i for i in items if not isinstance(i, Chain) or i.steps]
        arrays = [i.offers() if isinstance(i, Chain) else list(i[1]) for i in items]
        arrays = self.line.tie(arrays)
        self.line.mark = arrays
        for item, sent in zip(items, arrays):
            if isinstance(item, Chain):
                self.parts[item] = item.start(sent)
            else:
                name, _, axis, mask = item
                self.parts[name] = [swap(a, axis, mask) for a in sent]


def place_in(order):
    place = 0
    for digit in "".join(order):
        batch, band = DIGITS[digit]
        bit = lax.axis_index("batch") // batch if batch else lax.axis_index("band") // band
        place = place * 2 + bit % 2
    return place


ORDERS = (("z", "x", "yw"), ("y", "x", "zw"))
LAST_ORDERS = (("x", "y"), ("y", "x"))


def body(
    tokens, w_qkv, w_proj, w_fc1, w_fc2, gain_one, gain_two, cotangent, band_counts, slot_live
):
    slots, rows, width = tokens.shape
    flat = (slots * rows, width)
    band = lax.axis_index("band")
    core = band % 2
    meta = jnp.stack(
        [band, core] + [place_in(o) for o in ORDERS + tuple(order + ("zw",) for order in LAST_ORDERS) + ("x", "y", "z", "w")]
    ).astype(jnp.int32)
    gain_one = gain_one[None]
    gain_two = gain_two[None]
    at = (band_counts, slot_live, meta)
    line = Line()

    tokens, *tokens_other = lax.optimization_barrier(
        (tokens,) + tuple(tokens[s:s + 1] for s in range(slots))
    )
    tokens_other = [swap(t, "band", 2) for t in tokens_other]
    cotangent_p = swap(cotangent, "band", 1)
    first_own, query, kv_own = project(tokens, w_qkv, gain_one)
    tables = weigh_steps(QUERY_UNITS), weigh_steps(VALUE_UNITS)
    steps_theirs = jnp.where(core == 1, *tables)
    steps_ours = jnp.where(core == 0, *tables)
    line.mark = (first_own, meta, gain_two)
    first_other, pairs = [], []
    seconds, seconds_p = [], []
    kept = ()

    def take(s):
        first, pair = project_other(s, line.tie(tokens_other[s]), kv_own, w_qkv, gain_one, first_other)
        line.mark = pair
        first_other[:] = [first]
        pairs.append((pair, swap(pair, "band", 1)))

    def look(s):
        *out, second = attend(s, *at, line.tie(query), *pairs[s], tokens, w_proj, gain_two, kept)
        line.mark = second
        seconds.append(second)
        seconds_p.append(swap(second, "band", 1))
        return tuple(out)

    take(0)
    for s in range(slots):
        if s == 1:
            for n in range(1, slots):
                take(n)
                line.mark = (line.mark, steps_theirs, steps_ours)
            cotangent_p = line.tie(cotangent_p)
        kept = look(s)
    attended, lse, hidden = kept

    flight = Flight(line)
    chains = []
    acts, pres = [], []
    all_seconds = seconds + seconds_p
    for half in range(2):
        act, pre, lower, upper = mlp(
            *at, [line.tie(all_seconds[0])] + all_seconds[1:], cotangent, cotangent_p, w_fc1, w_fc2, half
        )
        line.mark = upper
        acts.append(act)
        pres.append(pre)
        chains.append(Chain((lower,), ORDERS[half], upper))
        flight.launch(chains[half])
    one, two = chains
    turn_parts = lend(True, 2, meta, line.tie(pres[0]), pres[1], w_fc1)
    line.mark = turn_parts
    flight.launch(("turn", turn_parts, "band", 1))
    got = flight.land("turn")
    flight.land(one)
    flight.launch(one)
    branch, grad_attended, delta = turn(
        *at, line.tie(pres[0]), pres[1], w_fc1, *got["turn"], hidden, cotangent, attended, gain_two, w_proj
    )
    line.mark = delta

    grad_query, sums, keeps, waiting = (), (), [], []

    def bring(s):
        *kept_sums, partial = gather(s, slots, line.tie(keeps[s]), got[f"send{s}"][0], w_qkv, sums)
        line.mark = partial
        return tuple(kept_sums), [(f"partial{s}", [partial], "band", 2)]

    for s in range(slots):
        query_grad, keep, send = attend_back(
            s, *at, line.tie(query), *pairs[s], grad_attended, lse, delta, grad_query
        )
        line.mark = send
        grad_query = (query_grad,)
        keeps.append(keep)
        got.update(flight.land())
        if s < slots - 1:
            flight.launch((f"send{s}", [send], "band", 1), two, one)
            if s > 0:
                sums, waiting = bring(s - 1)
                flight.launch(*waiting)
    both = Chain(pieces=[jnp.stack([one.total(), two.total()], axis=1)], joins=("w",))
    flight.launch((f"send{slots - 1}", [send], "band", 1), both)
    if slots > 1:
        sums, waiting = bring(slots - 2)
        flight.launch(*waiting)
    got.update(flight.land(f"send{slots - 1}"))
    sums, waiting = bring(slots - 1)
    arrays = (first_own, first_other[0], grad_query[0], *sums, attended, branch)
    theirs = weigh(meta, steps_theirs, (line.tie(first_own),) + arrays[1:])
    line.mark = theirs
    finish_part = lend(False, 1, meta, line.tie(acts[0]), acts[1], w_fc2)
    line.mark = (theirs, finish_part)

    got.update(flight.land())
    left, right = pack((both.pieces, True))
    one = Chain(pieces=[left], joins=("y", "z", "x"))
    two = Chain(pieces=[right], joins=("x", "z", "y"))
    flight.launch(("theirs", [theirs], "band", 1), ("finish", finish_part, "band", 1), one, two)
    ours = weigh(meta, steps_ours, (line.tie(first_own),) + arrays[1:])
    line.mark = ours

    got.update(flight.land())
    (theirs,) = got["theirs"]
    three = Chain((ours[0], theirs[0]), LAST_ORDERS[0])
    four = Chain((ours[1], theirs[1]), LAST_ORDERS[1])
    left, right = pack((one.pieces, False), (two.pieces, False))
    one.pieces, two.pieces = [left], [right]
    flight.launch(three, four, one, two, *waiting)
    output = finish(*at, line.tie(acts[0]), acts[1], w_fc2, got["finish"][0], hidden)
    line.mark = output

    flight.land(three, four)
    flight.launch(three, four)

    got.update(flight.land(one, two, f"partial{slots - 1}"))
    left, right = pack((one.pieces, False), (two.pieces, False))
    one.pieces, two.pieces = [left], [right]
    line.mark = (left, right)
    flight.land(three, four)
    five = Chain((jnp.stack([three.total_here(), four.total_here()], axis=1),), ("zw",))
    flight.launch(five, one, two)
    partials = [got[f"partial{s}"][0] for s in range(slots)]
    grad_input = close(
        line.tie(grad_query[0]), sums[0], sums[1], partials, tokens, branch, gain_one, w_qkv
    )
    line.mark = grad_input

    flight.land(five)
    five = Chain(pieces=[five.total()], joins=("zw",))
    flight.launch(five)

    flight.land(one, two)
    flight.land(five)
    halves = pack((five.pieces, True))
    three = Chain(pieces=halves[:1], joins=("y", "x"))
    four = Chain(pieces=halves[1:], joins=("x", "y"))
    flight.launch(three, four, ("one", one.pieces, "band", 1), ("two_held", two.pieces[:1], "band", 1))

    got.update(flight.land())
    held = pack((three.pieces, False), (four.pieces, False))
    three.pieces, four.pieces = held[:1], held[1:]
    flight.launch(three, four, ("two_rest", two.pieces[1:], "band", 1), ("qkv_held", held, "band", 1))
    got.update(flight.land("two_rest"))
    mlp_pieces = [line.tie(one.pieces[0]), one.pieces[1], *two.pieces]
    mlp_pieces += [*got["one"], got["two_held"][0], got["two_rest"][0]]
    grad_fc1, grad_fc2, norm2 = spread_mlp(meta, mlp_pieces, w_fc1, gain_two)
    line.mark = norm2

    got.update(flight.land())
    flight.launch(("qkv_rest", [three.pieces[1], four.pieces[1]], "band", 1))
    got.update(flight.land())
    last_pieces = three.pieces + four.pieces + [p for pair in zip(got["qkv_held"], got["qkv_rest"]) for p in pair]
    grad_qkv, grad_proj, norm1 = spread_qkv(meta, last_pieces, w_qkv, gain_one)
    return (output, grad_input, grad_qkv, grad_proj, grad_fc1, grad_fc2, norm1, norm2)


def solution(mesh):
    placed = (
        P("batch", "band", None),
        P(),
        P(),
        P(),
        P(),
        P(),
        P(),
        P("batch", "band", None),
        P("batch", None),
        P("batch"),
    )
    return jax.shard_map(
        body,
        mesh=mesh,
        in_specs=placed,
        out_specs=(
            P("batch", "band", None),
            P("batch", "band", None),
            P(),
            P(),
            P(),
            P(),
            P(),
            P(),
        ),
        check_vma=False,
    )
```
